32 devices in a mesh: dp: 8 (over y, x, core), vocab: 4 (over z).
Axes of the slice: x: 2, y: 2, z: 4, core: 2. Of those that a mesh axis runs over, the one named last changes fastest.
Arguments:
- hidden: bfloat16 [64, 3584], P('dp', 'vocab'), may hold values from -8 to 8
- head_weight: bfloat16 [4, 38016, 3584], P('vocab', 'dp'), may hold values from -1 to 1
- teacher_logits: bfloat16 [4, 32, 76032], P('vocab', 'dp'), may hold values from -20 to 310
Outputs:
- hidden_grad: bfloat16 [64, 3584], P('dp', 'vocab')
- head_grad: bfloat16 [4, 38016, 3584], P('vocab', 'dp')
The draws below stay inside these ranges and needn't reach their ends.
All inputs are finite; a program needn't handle non-finite values.
Results may differ from the reference program's by a relative error of at most 0.011.
Values may be sent and summed in bfloat16 or wider, within the bound.
No kernel may reach another device: no remote copies, remote signals or barrier semaphores. Data moves between devices by JAX's collectives and lax.ppermute only.
A program may use at most 128 MiB of HBM per device.

```python
import math
import jax
import jax.numpy as jnp

D = 3584
VOCAB = 152064
TOK_GRP = 8
TOKENS = 64
N_DP = 8
N_VOCAB = 4


def head_row(key, row_index):
    noise = jax.random.normal(jax.random.fold_in(jax.random.fold_in(key, 7), row_index), (D,), jnp.float32)
    trend = 1.0 + 0.12 * row_index.astype(jnp.float32) / VOCAB
    return noise * (3.0 / math.sqrt(D)) * trend


def draw_head_weight(key, part):
    rows_all = jnp.arange(VOCAB, dtype=jnp.int32)
    full_head = jax.vmap(lambda row_index: head_row(key, row_index))(rows_all)
    full_head = jnp.clip(full_head, -1.0, 1.0)
    return full_head.reshape(N_VOCAB, VOCAB // N_VOCAB, D).astype(jnp.bfloat16)


def draw_hidden(key, part):
    states = jnp.clip(jax.random.normal(jax.random.fold_in(key, 3), (TOKENS, D), jnp.float32), -6.0, 6.0)
    return jnp.clip(states, -8.0, 8.0).astype(jnp.bfloat16)


def draw_teacher_logits(key, part):
    shard_width = 2 * VOCAB // N_VOCAB
    noise = jnp.clip(jax.random.normal(jax.random.fold_in(key, 5), (N_VOCAB, TOKENS // 2, shard_width), jnp.float32), -5.0, 5.0)
    column = jnp.arange(shard_width, dtype=jnp.float32)[None, None, :]
    block = (jnp.arange(N_VOCAB, dtype=jnp.int32) // 2).astype(jnp.float32)[:, None, None]
    values = 3.0 * noise + 1.1 * (block * shard_width + column) / VOCAB
    return values.astype(jnp.bfloat16)


def setup_inputs(seed: int = 0) -> dict:
    streams_of = jax.random.split(jax.random.key(seed), 4)
    hidden = draw_hidden(jax.random.fold_in(streams_of[3], 71), 0)
    head_weight = draw_head_weight(jax.random.fold_in(streams_of[3], 71), 0)
    teacher_logits = draw_teacher_logits(jax.random.fold_in(streams_of[3], 71), 0)
    return {"hidden": hidden, "head_weight": head_weight, "teacher_logits": teacher_logits}


GRAD_SCALE = 32.0


def reference(hidden, head_weight, teacher_logits):
    head = head_weight.reshape(VOCAB, D)
    shard_width = 2 * VOCAB // N_VOCAB
    teacher = teacher_logits.reshape(N_VOCAB // 2, 2, N_DP, TOK_GRP // 2, shard_width)
    teacher = jnp.transpose(teacher, (2, 1, 3, 0, 4)).reshape(TOKENS, VOCAB).astype(jnp.float32)
    logits = jnp.dot(hidden, head.T, preferred_element_type=jnp.float32)
    student_max = jnp.max(logits, axis=1, keepdims=True)
    student_sum = jnp.sum(jnp.exp(logits - student_max), axis=1, keepdims=True)
    teacher_max = jnp.max(teacher, axis=1, keepdims=True)
    teacher_sum = jnp.sum(jnp.exp(teacher - teacher_max), axis=1, keepdims=True)
    student_prob = jnp.exp(logits - student_max) / student_sum
    teacher_prob = jnp.exp(teacher - teacher_max) / teacher_sum
    grad_logits = (GRAD_SCALE * (student_prob - teacher_prob)).astype(jnp.bfloat16)
    hidden_grad = jnp.dot(grad_logits, head, preferred_element_type=jnp.float32).astype(jnp.bfloat16)
    head_grad = jnp.dot(grad_logits.T, hidden, preferred_element_type=jnp.float32).astype(jnp.bfloat16)
    return hidden_grad, head_grad.reshape(N_VOCAB, VOCAB // N_VOCAB, D)
```

```python
import functools

import jax
import jax.numpy as jnp
from jax import lax
from jax.experimental import pallas as pl
from jax.experimental.pallas import tpu as pltpu
from jax.sharding import Mesh
from jax.sharding import PartitionSpec as P

GRAD_SCALE = 32.0
F32 = jnp.float32
BF16 = jnp.bfloat16
VMEM_LIMIT = 56 * 2**20


def row_tile(rows, limit):
    best = rows
    for tile in range(16, limit + 1, 16):
        if rows % tile == 0:
            best = tile
    return best


def tile_rows(step, tile, rows):
    if tile == rows:
        return slice(None)
    return pl.ds(pl.multiple_of(step * tile, tile), tile)


def params(limit=VMEM_LIMIT):
    return pltpu.CompilerParams(vmem_limit_bytes=limit)


def whole(shape):
    return pl.BlockSpec(shape, lambda *_: (0,) * len(shape))


def assemble(parts_ref, full_ref):
    width = parts_ref.shape[2]
    for v in range(parts_ref.shape[0]):
        full_ref[:, v * width : (v + 1) * width] = parts_ref[v]


def logits_kernel(tile, h_ref, w_ref, lt_ref, stats_ref, hidden):
    step = pl.program_id(0)

    @pl.when(step == 0)
    def _():
        assemble(h_ref, hidden)

    lt_ref[tile_rows(step, tile, lt_ref.shape[0]), :] = lax.dot_general(
        w_ref[...], hidden[...], (((1,), (1,)), ((), ())), preferred_element_type=F32
    )

    @pl.when(step == pl.num_programs(0) - 1)
    def _():
        values = lt_ref[...]
        top = jnp.max(values, axis=0, keepdims=True)
        total = jnp.sum(jnp.exp(values - top), axis=0, keepdims=True)
        stats_ref[...] = jnp.concatenate([top, total], axis=0)


def student_logits(h_parts, weight):
    rows, width = weight.shape
    n_v, tokens, _ = h_parts.shape
    tile = row_tile(rows, 528)
    return pl.pallas_call(
        functools.partial(logits_kernel, tile),
        grid=(rows // tile,),
        in_specs=[
            whole(h_parts.shape),
            pl.BlockSpec((tile, width), lambda i: (i, 0)),
        ],
        out_specs=[whole((rows, tokens)), whole((2, tokens))],
        out_shape=[
            jax.ShapeDtypeStruct((rows, tokens), F32),
            jax.ShapeDtypeStruct((2, tokens), F32),
        ],
        scratch_shapes=[pltpu.VMEM((tokens, width), BF16)],
        compiler_params=params(),
        cost_estimate=pl.CostEstimate(
            flops=2 * rows * width * tokens, bytes_accessed=2 * rows * width, transcendentals=0
        ),
    )(h_parts, weight)


def teacher_kernel(t_ref, tt_ref, stats_ref):
    values = t_ref[...].astype(F32)
    top = jnp.max(values, axis=1, keepdims=True)
    weights = jnp.exp(values - top)
    total = jnp.sum(weights, axis=1, keepdims=True)
    tt_ref[...] = (weights / total).T
    tokens = values.shape[0]
    row = lax.broadcasted_iota(jnp.int32, (tokens, tokens), 0)
    col = lax.broadcasted_iota(jnp.int32, (tokens, tokens), 1)
    flip = lambda c: jnp.sum(jnp.where(row == col, c, 0.0), axis=0, keepdims=True)
    stats_ref[...] = jnp.concatenate([flip(top), flip(total)], axis=0)


def teacher_prep(teacher):
    tokens, rows = teacher.shape
    return pl.pallas_call(
        teacher_kernel,
        out_shape=[
            jax.ShapeDtypeStruct((rows, tokens), F32),
            jax.ShapeDtypeStruct((2, tokens), F32),
        ],
        compiler_params=params(),
        cost_estimate=pl.CostEstimate(
            flops=4 * rows * tokens, bytes_accessed=6 * rows * tokens, transcendentals=rows * tokens
        ),
    )(teacher)


def products_kernel(tile, w_ref, lt_ref, tt_ref, stats_ref, u_ref):
    step = pl.program_id(0)
    here = tile_rows(step, tile, lt_ref.shape[0])
    share = jnp.exp(lt_ref[here, :] - stats_ref[0:1, :]) / stats_ref[1:2, :]
    teach = tt_ref[here, :]
    both = jnp.concatenate([share - teach, teach], axis=1).astype(BF16)
    value = lax.dot_general(
        both, w_ref[...], (((0,), (0,)), ((), ())), preferred_element_type=F32
    )

    @pl.when(step == 0)
    def _():
        u_ref[...] = value

    @pl.when(step > 0)
    def _():
        u_ref[...] += value


def local_products(weight, lt, tt, stats):
    rows, width = weight.shape
    tokens = lt.shape[1]
    tile = row_tile(rows, 1584)
    return pl.pallas_call(
        functools.partial(products_kernel, tile),
        grid=(rows // tile,),
        in_specs=[
            pl.BlockSpec((tile, width), lambda i: (i, 0)),
            whole(lt.shape),
            whole(tt.shape),
            whole(stats.shape),
        ],
        out_specs=whole((2 * tokens, width)),
        out_shape=jax.ShapeDtypeStruct((2 * tokens, width), F32),
        compiler_params=params(),
        cost_estimate=pl.CostEstimate(
            flops=4 * rows * width * tokens, bytes_accessed=2 * rows * width, transcendentals=0
        ),
    )(weight, lt, tt, stats)


def combine_kernel(all_ref, mine_ref, u_ref, hp_ref, mass_ref):
    tokens = mine_ref.shape[1]

    def mass(k):
        top_all = all_ref[:, k, :tokens]
        top = jnp.max(top_all, axis=0, keepdims=True)
        total = jnp.sum(jnp.exp(top_all - top) * all_ref[:, k + 1, :tokens], axis=0, keepdims=True)
        return jnp.exp(mine_ref[k : k + 1, :] - top) * mine_ref[k + 1 : k + 2, :] / total

    student, teacher = mass(0), mass(2)
    mass_ref[...] = jnp.concatenate([student, teacher], axis=0)
    row = lax.broadcasted_iota(jnp.int32, (tokens, tokens), 0)
    col = lax.broadcasted_iota(jnp.int32, (tokens, tokens), 1)
    flip = lambda r: jnp.sum(jnp.where(row == col, r, 0.0), axis=1, keepdims=True)
    scale_x = GRAD_SCALE * flip(student)
    scale_t = GRAD_SCALE * flip(student - teacher)
    width = hp_ref.shape[2]
    for v in range(hp_ref.shape[0]):
        cols = slice(v * width, (v + 1) * width)
        hp_ref[v] = (u_ref[:tokens, cols] * scale_x + u_ref[tokens:, cols] * scale_t).astype(BF16)


def combine(stats_all, stats, products, n_v):
    tokens = stats.shape[1]
    width = products.shape[1] // n_v
    return pl.pallas_call(
        combine_kernel,
        out_shape=[
            jax.ShapeDtypeStruct((n_v, tokens, width), BF16),
            jax.ShapeDtypeStruct((2, tokens), F32),
        ],
        compiler_params=params(),
    )(stats_all, stats, products)


def head_kernel(tile, lt_ref, tt_ref, stats_ref, mass_ref, h_ref, out_ref, hidden):
    step = pl.program_id(0)

    @pl.when(step == 0)
    def _():
        assemble(h_ref, hidden)

    here = tile_rows(step, tile, lt_ref.shape[0])
    share = jnp.exp(lt_ref[here, :] - stats_ref[0:1, :]) / stats_ref[1:2, :]
    teach = tt_ref[here, :]
    grad = GRAD_SCALE * (share * mass_ref[0:1, :] - teach * mass_ref[1:2, :])
    out_ref[...] = jnp.dot(
        grad.astype(BF16), hidden[...], preferred_element_type=F32
    ).astype(BF16)


def head_gradient(lt, tt, stats, mass, h_parts):
    rows, tokens = lt.shape
    width = h_parts.shape[0] * h_parts.shape[2]
    tile = row_tile(rows, 528)
    return pl.pallas_call(
        functools.partial(head_kernel, tile),
        grid=(rows // tile,),
        in_specs=[whole(x.shape) for x in (lt, tt, stats, mass, h_parts)],
        out_specs=pl.BlockSpec((tile, width), lambda i: (i, 0)),
        out_shape=jax.ShapeDtypeStruct((rows, width), BF16),
        scratch_shapes=[pltpu.VMEM((tokens, width), BF16)],
        compiler_params=params(),
        cost_estimate=pl.CostEstimate(
            flops=2 * rows * width * tokens, bytes_accessed=2 * rows * width, transcendentals=0
        ),
    )(lt, tt, stats, mass, h_parts)


def exchange(parts, axes):
    return lax.all_to_all(parts, axes, split_axis=0, concat_axis=0, tiled=True)


def shards(n_dp, n_v, hidden, head_weight, teacher_logits):
    everyone = ("vk", "vs", "dp")
    count = n_dp * n_v
    group, width = hidden.shape
    tokens = n_dp * group
    h_parts = exchange(jnp.broadcast_to(hidden[None], (count, group, width)), everyone)
    h_parts = h_parts.reshape(n_v, tokens, width)

    weight = head_weight[0]
    piece = teacher_logits[0]
    half, cols = piece.shape[0], piece.shape[1] // (2 * n_dp)
    sends = piece.reshape(half, 2, n_dp, cols).transpose(2, 1, 0, 3).reshape(2 * n_dp, half, cols)
    teacher = exchange(sends, ("dp", "vs")).reshape(tokens, cols)

    lt, s_stats = student_logits(h_parts, weight)
    tt, t_stats = teacher_prep(teacher)
    stats = jnp.concatenate([s_stats, t_stats], axis=0)
    message = jnp.pad(stats, ((0, 4), (0, -tokens % 128)))
    stats_all = exchange(jnp.broadcast_to(message[None], (count, *message.shape)), everyone)
    products = local_products(weight, lt, tt, s_stats)
    partial_value, mass = combine(stats_all, stats, products, n_v)
    pieces = exchange(partial_value.reshape(count, group, width), everyone)
    head_grad = head_gradient(lt, tt, s_stats, mass, h_parts)
    hidden_grad = jnp.sum(pieces.astype(F32), axis=0).astype(BF16)
    return hidden_grad, head_grad[None]


def solution(mesh):
    n_dp, n_v = mesh.shape["dp"], mesh.shape["vocab"]
    split = Mesh(mesh.devices.reshape(n_dp, n_v // 2, 2), ("dp", "vk", "vs"))
    vocab = ("vk", "vs")
    body = jax.shard_map(
        functools.partial(shards, n_dp, n_v),
        mesh=split,
        in_specs=(P("dp", vocab), P(vocab, "dp", None), P(vocab, "dp", None)),
        out_specs=(P("dp", vocab), P(vocab, "dp", None)),
        check_vma=False,
    )
    return body
```

```python
import functools

import jax
import jax.numpy as jnp
from jax import lax
from jax.experimental import pallas as pl
from jax.experimental.pallas import tpu as pltpu
from jax.sharding import Mesh
from jax.sharding import PartitionSpec as P

GRAD_SCALE = 32.0
F32 = jnp.float32
BF16 = jnp.bfloat16
VMEM_LIMIT = 16 * 2**20


def row_tile(rows, limit):
    best = rows
    for tile in range(16, limit + 1, 16):
        if rows % tile == 0:
            best = tile
    return best


def tile_rows(step, tile, rows):
    if tile == rows:
        return slice(None)
    return pl.ds(pl.multiple_of(step * tile, tile), tile)


def params(limit=VMEM_LIMIT):
    return pltpu.CompilerParams(vmem_limit_bytes=limit)


def whole(shape):
    return pl.BlockSpec(shape, lambda *_: (0,) * len(shape))


def assemble(parts_ref, full_ref):
    width = parts_ref.shape[2]
    for v in range(parts_ref.shape[0]):
        full_ref[:, v * width : (v + 1) * width] = parts_ref[v]


def load_kernel(tile, w_ref, out_ref, sems):
    rows = w_ref.shape[0]
    copies = [
        pltpu.make_async_copy(
            w_ref.at[pl.ds(k * tile, tile), :], out_ref.at[pl.ds(k * tile, tile), :], sems.at[k]
        )
        for k in range(rows // tile)
    ]
    for copy in copies:
        copy.start()
    for copy in copies:
        copy.wait()


def resident(weight):
    rows, width = weight.shape
    tile = row_tile(rows, 528)
    return pl.pallas_call(
        functools.partial(load_kernel, tile),
        in_specs=[pl.BlockSpec(memory_space=pl.ANY)],
        out_specs=pl.BlockSpec(memory_space=pltpu.VMEM),
        out_shape=pltpu.VMEM((rows, width), BF16),
        scratch_shapes=[pltpu.SemaphoreType.DMA((rows // tile,))],
        compiler_params=params(2**20),
        cost_estimate=pl.CostEstimate(
            flops=0, bytes_accessed=4 * rows * width, transcendentals=0
        ),
    )(weight)


def logits_kernel(tile, h_ref, w_ref, lt_ref, stats_ref, hidden):
    width = h_ref.shape[2]
    for v in range(h_ref.shape[0]):
        hidden[v * width : (v + 1) * width, :] = h_ref[v].T
    rows = w_ref.shape[0]

    def chunk(step, carry):
        here = tile_rows(step, tile, rows)
        lt_ref[here, :] = jnp.dot(w_ref[here, :], hidden[...], preferred_element_type=F32)
        return carry

    lax.fori_loop(0, rows // tile, chunk, 0)
    values = lt_ref[...]
    top = jnp.max(values, axis=0, keepdims=True)
    total = jnp.sum(jnp.exp(values - top), axis=0, keepdims=True)
    stats_ref[...] = jnp.concatenate([top, total], axis=0)


def student_logits(h_parts, weight):
    rows, width = weight.shape
    tokens = h_parts.shape[1]
    return pl.pallas_call(
        functools.partial(logits_kernel, row_tile(rows, 1584)),
        in_specs=[pl.BlockSpec(memory_space=pltpu.VMEM)] * 2,
        out_specs=[pl.BlockSpec(memory_space=pltpu.VMEM)] * 2,
        out_shape=[
            jax.ShapeDtypeStruct((rows, tokens), F32),
            jax.ShapeDtypeStruct((2, tokens), F32),
        ],
        scratch_shapes=[pltpu.VMEM((width, tokens), BF16)],
        compiler_params=params(12 * 2**20),
        cost_estimate=pl.CostEstimate(
            flops=8 * rows * width * tokens, bytes_accessed=0, transcendentals=0
        ),
    )(h_parts, weight)


def teacher_kernel(t_ref, tt_ref, stats_ref):
    values = jnp.concatenate([t_ref[j].astype(F32) for j in range(t_ref.shape[0])], axis=0)
    top = jnp.max(values, axis=1, keepdims=True)
    weights = jnp.exp(values - top)
    total = jnp.sum(weights, axis=1, keepdims=True)
    tt_ref[...] = (weights / total).T
    tokens = values.shape[0]
    row = lax.broadcasted_iota(jnp.int32, (tokens, tokens), 0)
    col = lax.broadcasted_iota(jnp.int32, (tokens, tokens), 1)
    flip = lambda c: jnp.sum(jnp.where(row == col, c, 0.0), axis=0, keepdims=True)
    stats_ref[...] = jnp.concatenate([flip(top), flip(total)], axis=0)


def teacher_prep(teacher):
    senders, half, rows = teacher.shape
    tokens = senders * half
    return pl.pallas_call(
        teacher_kernel,
        out_shape=[
            jax.ShapeDtypeStruct((rows, tokens), F32),
            jax.ShapeDtypeStruct((2, tokens), F32),
        ],
        compiler_params=params(),
        cost_estimate=pl.CostEstimate(
            flops=4 * rows * tokens, bytes_accessed=6 * rows * tokens, transcendentals=rows * tokens
        ),
    )(teacher)


def products_kernel(block, w_ref, lt_ref, tt_ref, stats_ref, u_ref, both):
    share = jnp.exp(lt_ref[...] - stats_ref[0:1, :]) / stats_ref[1:2, :]
    teach = tt_ref[...]
    both[...] = jnp.concatenate([share - teach, teach], axis=1).T.astype(BF16)

    def columns(step, carry):
        here = pl.ds(pl.multiple_of(step * block, block), block)
        u_ref[:, here] = jnp.dot(both[...], w_ref[:, here], preferred_element_type=F32)
        return carry

    lax.fori_loop(0, w_ref.shape[1] // block, columns, 0)


def local_products(weight, lt, tt, stats):
    rows, width = weight.shape
    tokens = lt.shape[1]
    return pl.pallas_call(
        functools.partial(products_kernel, 256),
        in_specs=[pl.BlockSpec(memory_space=pltpu.VMEM)] * 4,
        out_specs=pl.BlockSpec(memory_space=pltpu.VMEM),
        out_shape=jax.ShapeDtypeStruct((2 * tokens, width), F32),
        scratch_shapes=[pltpu.VMEM((2 * tokens, rows), BF16)],
        compiler_params=params(16 * 2**20),
        cost_estimate=pl.CostEstimate(
            flops=8 * rows * width * tokens, bytes_accessed=0, transcendentals=0
        ),
    )(weight, lt, tt, stats)


def combine_kernel(all_ref, mine_ref, u_ref, hp_ref, mass_ref):
    tokens = mine_ref.shape[1]

    def mass(k):
        top_all = all_ref[:, k, :tokens]
        top = jnp.max(top_all, axis=0, keepdims=True)
        total = jnp.sum(jnp.exp(top_all - top) * all_ref[:, k + 1, :tokens], axis=0, keepdims=True)
        return jnp.exp(mine_ref[k : k + 1, :] - top) * mine_ref[k + 1 : k + 2, :] / total

    student, teacher = mass(0), mass(2)
    mass_ref[...] = jnp.concatenate([student, teacher], axis=0)
    row = lax.broadcasted_iota(jnp.int32, (tokens, tokens), 0)
    col = lax.broadcasted_iota(jnp.int32, (tokens, tokens), 1)
    flip = lambda r: jnp.sum(jnp.where(row == col, r, 0.0), axis=1, keepdims=True)
    scale_x = GRAD_SCALE * flip(student)
    scale_t = GRAD_SCALE * flip(student - teacher)
    width = hp_ref.shape[2]
    for v in range(hp_ref.shape[0]):
        cols = slice(v * width, (v + 1) * width)
        hp_ref[v] = (u_ref[:tokens, cols] * scale_x + u_ref[tokens:, cols] * scale_t).astype(BF16)


def combine(stats_all, stats, products, n_v):
    tokens = stats.shape[1]
    width = products.shape[1] // n_v
    return pl.pallas_call(
        combine_kernel,
        out_shape=[
            jax.ShapeDtypeStruct((n_v, tokens, width), BF16),
            jax.ShapeDtypeStruct((2, tokens), F32),
        ],
        compiler_params=params(),
    )(stats_all, stats, products)


def head_kernel(tile, lt_ref, tt_ref, stats_ref, mass_ref, h_ref, out_ref, hidden):
    step = pl.program_id(0)

    @pl.when(step == 0)
    def _():
        assemble(h_ref, hidden)

    here = tile_rows(step, tile, lt_ref.shape[0])
    share = jnp.exp(lt_ref[here, :] - stats_ref[0:1, :]) / stats_ref[1:2, :]
    teach = tt_ref[here, :]
    grad = GRAD_SCALE * (share * mass_ref[0:1, :] - teach * mass_ref[1:2, :])
    grad = grad.astype(BF16)
    for k in range(0, out_ref.shape[1], 256):
        out_ref[:, k : k + 256] = jnp.dot(
            grad, hidden[:, k : k + 256], preferred_element_type=F32
        ).astype(BF16)


def head_gradient(lt, tt, stats, mass, h_parts):
    rows, tokens = lt.shape
    width = h_parts.shape[0] * h_parts.shape[2]
    tile = row_tile(rows, 528)
    return pl.pallas_call(
        functools.partial(head_kernel, tile),
        grid=(rows // tile,),
        in_specs=[whole(x.shape) for x in (lt, tt, stats, mass, h_parts)],
        out_specs=pl.BlockSpec((tile, width), lambda i: (i, 0)),
        out_shape=jax.ShapeDtypeStruct((rows, width), BF16),
        scratch_shapes=[pltpu.VMEM((tokens, width), BF16)],
        compiler_params=params(),
        cost_estimate=pl.CostEstimate(
            flops=2 * rows * width * tokens, bytes_accessed=2 * rows * width, transcendentals=0
        ),
    )(lt, tt, stats, mass, h_parts)


def exchange(parts, axes):
    return lax.all_to_all(parts, axes, split_axis=0, concat_axis=0, tiled=True)


def shards(n_dp, n_v, hidden, head_weight, teacher_logits):
    everyone = ("vk", "vs", "dp")
    count = n_dp * n_v
    group, width = hidden.shape
    tokens = n_dp * group
    h_parts = exchange(jnp.broadcast_to(hidden[None], (count, group, width)), everyone)
    h_parts = h_parts.reshape(n_v, tokens, width)

    weight = pltpu.with_memory_space_constraint(resident(head_weight[0]), pltpu.VMEM)
    piece = teacher_logits[0]
    half, cols = piece.shape[0], piece.shape[1] // (2 * n_dp)
    sends = piece.reshape(half, 2, n_dp, cols).transpose(2, 1, 0, 3).reshape(2 * n_dp, half, cols)
    teacher = exchange(sends, ("dp", "vs"))

    lt, s_stats = student_logits(h_parts, weight)
    tt, t_stats = teacher_prep(teacher)
    stats = jnp.concatenate([s_stats, t_stats], axis=0)
    message = jnp.pad(stats, ((0, 4), (0, -tokens % 128)))
    stats_all = exchange(jnp.broadcast_to(message[None], (count, *message.shape)), everyone)
    products = local_products(weight, lt, tt, s_stats)
    partial_value, mass = combine(stats_all, stats, products, n_v)
    pieces = exchange(partial_value.reshape(count, group, width), everyone)
    head_grad = head_gradient(lt, tt, s_stats, mass, h_parts)
    hidden_grad = jnp.sum(pieces.astype(F32), axis=0).astype(BF16)
    return hidden_grad, head_grad[None]


def solution(mesh):
    n_dp, n_v = mesh.shape["dp"], mesh.shape["vocab"]
    split = Mesh(mesh.devices.reshape(n_dp, n_v // 2, 2), ("dp", "vk", "vs"))
    vocab = ("vk", "vs")
    body = jax.shard_map(
        functools.partial(shards, n_dp, n_v),
        mesh=split,
        in_specs=(P("dp", vocab), P(vocab, "dp", None), P(vocab, "dp", None)),
        out_specs=(P("dp", vocab), P(vocab, "dp", None)),
        check_vma=False,
    )
    return body
```

```python
import functools

import jax
import jax.numpy as jnp
from jax import lax
from jax.experimental import pallas as pl
from jax.experimental.pallas import tpu as pltpu
from jax.sharding import Mesh
from jax.sharding import PartitionSpec as P

GRAD_SCALE = 32.0
F32 = jnp.float32
BF16 = jnp.bfloat16
MIB = 2**20
LANES = 128


def row_tile(rows, limit):
    best = rows
    for tile in range(16, limit + 1, 16):
        if rows % tile == 0:
            best = tile
    return best


def column_tile(width, limit):
    return max(c for c in range(LANES, limit + 1, LANES) if width % c == 0)


def tile_rows(step, tile, rows):
    if tile == rows:
        return slice(None)
    return pl.ds(pl.multiple_of(step * tile, tile), tile)


def params(limit):
    return pltpu.CompilerParams(vmem_limit_bytes=limit)


def whole(shape):
    return pl.BlockSpec(shape, lambda *_: (0,) * len(shape))


def in_vmem(count):
    return [pl.BlockSpec(memory_space=pltpu.VMEM)] * count


def vocab_index():
    return lax.axis_index("vk") * 2 + lax.axis_index("vs")


def logits_kernel(n_dp, tile, *refs):
    parts, w_ref = refs[:n_dp], refs[n_dp]
    lt_ref, stats_ref, hidden_ref, buffer, turned, staged, sems = refs[n_dp + 1 :]
    rows, width = w_ref.shape
    steps = rows // tile

    def fetch(step):
        here = tile_rows(step, tile, rows)
        return pltpu.make_async_copy(w_ref.at[here, :], buffer.at[here, :], sems.at[step])

    for step in range(min(2, steps)):
        fetch(step).start()

    n_v, _, chunk = parts[0].shape
    for s in range(n_dp):
        staged[s] = parts[s][...].astype(F32)
    dp, v = lax.axis_index("dp"), vocab_index()
    for j in range(n_v):
        cols = slice(j * chunk, (j + 1) * chunk)
        block = jnp.concatenate([staged[dp ^ g, v ^ j] for g in range(n_dp)], axis=0)
        hidden_ref[:, cols] = block.astype(BF16)
        turned[cols, :] = block.T.astype(BF16)

    def body(step, carry):
        @pl.when(step + 2 < steps)
        def _():
            fetch(step + 2).start()

        fetch(step).wait()
        here = tile_rows(step, tile, rows)
        lt_ref[here, :] = jnp.dot(buffer[here, :], turned[...], preferred_element_type=F32)
        return carry

    lax.fori_loop(0, steps, body, 0)
    values = lt_ref[...]
    top = jnp.max(values, axis=0, keepdims=True)
    total = jnp.sum(jnp.exp(values - top), axis=0, keepdims=True)
    stats_ref[...] = jnp.concatenate([top, total], axis=0)


def student_logits(parts, weight):
    rows, width = weight.shape
    n_v, group, chunk = parts[0].shape
    n_dp = len(parts)
    tokens = n_dp * group
    tile = row_tile(rows, 528)
    return pl.pallas_call(
        functools.partial(logits_kernel, n_dp, tile),
        in_specs=[*in_vmem(n_dp), pl.BlockSpec(memory_space=pl.ANY)],
        out_specs=in_vmem(3),
        out_shape=[
            jax.ShapeDtypeStruct((rows, tokens), F32),
            jax.ShapeDtypeStruct((2, tokens), F32),
            jax.ShapeDtypeStruct((tokens, width), BF16),
        ],
        scratch_shapes=[
            pltpu.VMEM((rows, width), BF16),
            pltpu.VMEM((width, tokens), BF16),
            pltpu.VMEM((n_dp, n_v, group, chunk), F32),
            pltpu.SemaphoreType.DMA((rows // tile,)),
        ],
        compiler_params=params(46 * MIB),
        cost_estimate=pl.CostEstimate(
            flops=8 * rows * width * tokens, bytes_accessed=2 * rows * width, transcendentals=0
        ),
    )(*parts, weight)


def teacher_values(t_ref):
    return jnp.concatenate([t_ref[j].astype(F32) for j in range(t_ref.shape[0])], axis=0)


def message_kernel(t_ref, s_ref, stats_ref, message_ref):
    values = teacher_values(t_ref)
    tokens = values.shape[0]
    top = jnp.max(values, axis=1, keepdims=True)
    total = jnp.sum(jnp.exp(values - top), axis=1, keepdims=True)
    row = lax.broadcasted_iota(jnp.int32, (tokens, tokens), 0)
    col = lax.broadcasted_iota(jnp.int32, (tokens, tokens), 1)
    flip = lambda c: jnp.sum(jnp.where(row == col, c, 0.0), axis=0, keepdims=True)
    rest = jnp.zeros((4, tokens), F32)
    stats = jnp.concatenate([s_ref[...], flip(top), flip(total), rest], axis=0)
    stats_ref[...] = stats
    lanes = message_ref.shape[2]
    if lanes > tokens:
        stats = jnp.concatenate([stats, jnp.zeros((8, lanes - tokens), F32)], axis=1)
    for k in range(message_ref.shape[0]):
        message_ref[k] = stats


def stats_message(teacher, s_stats, count):
    tokens = s_stats.shape[1]
    lanes = -(-tokens // LANES) * LANES
    return pl.pallas_call(
        message_kernel,
        in_specs=in_vmem(2),
        out_specs=in_vmem(2),
        out_shape=[
            jax.ShapeDtypeStruct((8, tokens), F32),
            jax.ShapeDtypeStruct((count, 8, lanes), F32),
        ],
        compiler_params=params(12 * MIB),
    )(teacher, s_stats)


def products_kernel(t_ref, lt_ref, stats_ref, w_ref, u_ref, both_ref, packed):
    @pl.when(pl.program_id(0) == 0)
    def _():
        values = teacher_values(t_ref)
        top = jnp.max(values, axis=1, keepdims=True)
        teach = jnp.exp(values - top)
        teach = teach * (1.0 / jnp.sum(teach, axis=1, keepdims=True))
        share = jnp.exp(lt_ref[...] - stats_ref[0:1, :]) * (1.0 / stats_ref[1:2, :])
        both_ref[...] = jnp.concatenate([share, teach.T], axis=1)
        tokens = values.shape[0]
        packed[:tokens, :] = (share.T - teach).astype(BF16)
        packed[tokens:, :] = teach.astype(BF16)

    u_ref[...] = jnp.dot(packed[...], w_ref[...], preferred_element_type=F32)


def local_products(weight, teacher, lt, stats):
    rows, width = weight.shape
    tokens = lt.shape[1]
    tile = column_tile(width, 256)
    return pl.pallas_call(
        products_kernel,
        grid=(width // tile,),
        in_specs=[*in_vmem(3), pl.BlockSpec((rows, tile), lambda i: (0, i))],
        out_specs=[
            pl.BlockSpec((2 * tokens, tile), lambda i: (0, i)),
            pl.BlockSpec(memory_space=pltpu.VMEM),
        ],
        out_shape=[
            jax.ShapeDtypeStruct((2 * tokens, width), F32),
            jax.ShapeDtypeStruct((rows, 2 * tokens), F32),
        ],
        scratch_shapes=[pltpu.VMEM((2 * tokens, rows), BF16)],
        compiler_params=params(24 * MIB),
        cost_estimate=pl.CostEstimate(
            flops=8 * rows * width * tokens, bytes_accessed=2 * rows * width, transcendentals=0
        ),
    )(teacher, lt, stats, weight)


def combine_kernel(all_ref, mine_ref, u_ref, hp_ref, mass_ref):
    tokens = mine_ref.shape[1]

    def mass(k):
        top_all = all_ref[:, k, :tokens]
        top = jnp.max(top_all, axis=0, keepdims=True)
        total = jnp.sum(jnp.exp(top_all - top) * all_ref[:, k + 1, :tokens], axis=0, keepdims=True)
        return jnp.exp(mine_ref[k : k + 1, :] - top) * mine_ref[k + 1 : k + 2, :] / total

    student, teacher = mass(0), mass(2)
    mass_ref[...] = GRAD_SCALE * jnp.concatenate([student, teacher], axis=1)
    row = lax.broadcasted_iota(jnp.int32, (tokens, tokens), 0)
    col = lax.broadcasted_iota(jnp.int32, (tokens, tokens), 1)
    flip = lambda r: jnp.sum(jnp.where(row == col, r, 0.0), axis=1, keepdims=True)
    scale_x = GRAD_SCALE * flip(student)
    scale_t = GRAD_SCALE * flip(student - teacher)
    width = hp_ref.shape[2]
    for v in range(hp_ref.shape[0]):
        cols = slice(v * width, (v + 1) * width)
        hp_ref[v] = (u_ref[:tokens, cols] * scale_x + u_ref[tokens:, cols] * scale_t).astype(BF16)


def combine(stats_all, stats, products, n_v):
    tokens = stats.shape[1]
    width = products.shape[1] // n_v
    return pl.pallas_call(
        combine_kernel,
        in_specs=in_vmem(3),
        out_specs=in_vmem(2),
        out_shape=[
            jax.ShapeDtypeStruct((n_v, tokens, width), BF16),
            jax.ShapeDtypeStruct((1, 2 * tokens), F32),
        ],
        compiler_params=params(12 * MIB),
    )(stats_all, stats, products)


def head_kernel(both_ref, mass_ref, hidden_ref, out_ref):
    tokens, width = hidden_ref.shape
    scaled = both_ref[...] * mass_ref[...]
    grad = (scaled[:, :tokens] - scaled[:, tokens:]).astype(BF16)
    tile = column_tile(width, 256)
    for k in range(0, width, tile):
        out_ref[:, k : k + tile] = jnp.dot(
            grad, hidden_ref[:, k : k + tile], preferred_element_type=F32
        ).astype(BF16)


def head_gradient(both, mass, hidden):
    rows = both.shape[0]
    tokens, width = hidden.shape
    tile = row_tile(rows, 528)
    return pl.pallas_call(
        head_kernel,
        grid=(rows // tile,),
        in_specs=[pl.BlockSpec((tile, 2 * tokens), lambda i: (i, 0)), *in_vmem(2)],
        out_specs=pl.BlockSpec((tile, width), lambda i: (i, 0)),
        out_shape=jax.ShapeDtypeStruct((rows, width), BF16),
        compiler_params=params(24 * MIB),
        cost_estimate=pl.CostEstimate(
            flops=8 * rows * width * tokens, bytes_accessed=2 * rows * width, transcendentals=0
        ),
    )(both, mass, hidden)


def exchange(parts, axes):
    return lax.all_to_all(parts, axes, split_axis=0, concat_axis=0, tiled=True)


def partners(value, axes, size):
    got = [value]
    for s in range(1, size):
        got.append(lax.ppermute(value, axes, [(i, i ^ s) for i in range(size)]))
    return got


def shards(n_dp, n_v, hidden, head_weight, teacher_logits):
    everyone = ("vk", "vs", "dp")
    count = n_dp * n_v
    group, width = hidden.shape
    weight = head_weight[0]

    columns = jnp.stack(partners(hidden, ("vk", "vs"), n_v))
    parts = partners(columns, "dp", n_dp)

    piece = teacher_logits[0]
    half, cols = piece.shape[0], piece.shape[1] // (2 * n_dp)
    sends = piece.reshape(half, 2, n_dp, cols).transpose(2, 1, 0, 3).reshape(2 * n_dp, half, cols)
    teacher = exchange(sends, ("dp", "vs"))

    lt, s_stats, every_row = student_logits(parts, weight)
    stats, message = stats_message(teacher, s_stats, count)
    stats_all = exchange(message, everyone)
    products, both = local_products(weight, teacher, lt, stats)
    partial_value, mass = combine(stats_all, stats, products, n_v)
    pieces = exchange(partial_value.reshape(count, group, width), everyone)
    head_grad = head_gradient(both, mass, every_row)
    hidden_grad = jnp.sum(pieces.astype(F32), axis=0).astype(BF16)
    return hidden_grad, head_grad[None]


def solution(mesh):
    n_dp, n_v = mesh.shape["dp"], mesh.shape["vocab"]
    split = Mesh(mesh.devices.reshape(n_dp, n_v // 2, 2), ("dp", "vk", "vs"))
    vocab = ("vk", "vs")
    return jax.shard_map(
        functools.partial(shards, n_dp, n_v),
        mesh=split,
        in_specs=(P("dp", vocab), P(vocab, "dp", None), P(vocab, "dp", None)),
        out_specs=(P("dp", vocab), P(vocab, "dp", None)),
        check_vma=False,
    )
```

```python
import functools

import jax
import jax.numpy as jnp
from jax import lax
from jax.experimental import pallas as pl
from jax.experimental.pallas import tpu as pltpu
from jax.sharding import Mesh
from jax.sharding import PartitionSpec as P

GRAD_SCALE = 32.0
F32 = jnp.float32
BF16 = jnp.bfloat16
MIB = 2**20
LANES = 128


def row_tile(rows, limit):
    best = rows
    for tile in range(16, limit + 1, 16):
        if rows % tile == 0:
            best = tile
    return best


def column_tile(width, limit):
    return max(c for c in range(LANES, limit + 1, LANES) if width % c == 0)


def tile_rows(step, tile, rows):
    if tile == rows:
        return slice(None)
    return pl.ds(pl.multiple_of(step * tile, tile), tile)


def params(limit):
    return pltpu.CompilerParams(vmem_limit_bytes=limit)


def whole(shape):
    return pl.BlockSpec(shape, lambda *_: (0,) * len(shape))


def in_vmem(count):
    return [pl.BlockSpec(memory_space=pltpu.VMEM)] * count


def logits_kernel(tile, own_ref, other_ref, w_ref, *refs):
    lt_ref, stats_ref, hidden_ref, buffer, turned, staged, sems = refs
    rows = w_ref.shape[0]
    steps = rows // tile
    ahead = min(3, steps)

    def fetch(step):
        here = tile_rows(step, tile, rows)
        return pltpu.make_async_copy(w_ref.at[here, :], buffer.at[here, :], sems.at[step])

    for step in range(ahead):
        fetch(step).start()

    n_v, n_pl, _, chunk = own_ref.shape
    core = lax.axis_index("co")
    staged[core] = own_ref[...].astype(F32)
    staged[1 - core] = other_ref[...].astype(F32)
    for v in range(n_v):
        cols = slice(v * chunk, (v + 1) * chunk)
        groups = [staged[c, v, p] for p in range(n_pl) for c in range(2)]
        block = jnp.concatenate(groups, axis=0)
        hidden_ref[:, cols] = block.astype(BF16)
        turned[cols, :] = block.T.astype(BF16)

    def body(step, carry):
        top, total = carry

        @pl.when(step + ahead < steps)
        def _():
            fetch(step + ahead).start()

        fetch(step).wait()
        here = tile_rows(step, tile, rows)
        values = jnp.dot(buffer[here, :], turned[...], preferred_element_type=F32)
        lt_ref[here, :] = values
        higher = jnp.maximum(top, jnp.max(values, axis=0, keepdims=True))
        added = jnp.sum(jnp.exp(values - higher), axis=0, keepdims=True)
        return higher, total * jnp.exp(top - higher) + added

    low = jnp.full((1, lt_ref.shape[1]), -1e30, F32)
    top, total = lax.fori_loop(0, steps, body, (low, jnp.zeros_like(low)))
    stats_ref[...] = jnp.concatenate([top, total], axis=0)


def student_logits(own, other, weight):
    rows, width = weight.shape
    n_v, n_pl, group, _ = own.shape
    tokens = 2 * n_pl * group
    tile = row_tile(rows, 528)
    return pl.pallas_call(
        functools.partial(logits_kernel, tile),
        in_specs=[*in_vmem(2), pl.BlockSpec(memory_space=pl.ANY)],
        out_specs=in_vmem(3),
        out_shape=[
            jax.ShapeDtypeStruct((rows, tokens), F32),
            jax.ShapeDtypeStruct((2, tokens), F32),
            pltpu.HBM((tokens, width), BF16),
        ],
        scratch_shapes=[
            pltpu.VMEM((rows, width), BF16),
            pltpu.VMEM((width, tokens), BF16),
            pltpu.VMEM((2, *own.shape), F32),
            pltpu.SemaphoreType.DMA((rows // tile,)),
        ],
        compiler_params=params(46 * MIB),
        cost_estimate=pl.CostEstimate(
            flops=8 * rows * width * tokens, bytes_accessed=2 * rows * width, transcendentals=0
        ),
    )(own, other, weight)


def teacher_values(t_ref):
    return jnp.concatenate([t_ref[j].astype(F32) for j in range(t_ref.shape[0])], axis=0)


def message_kernel(t_ref, s_ref, stats_ref, message_ref):
    values = teacher_values(t_ref)
    tokens = values.shape[0]
    top = jnp.max(values, axis=1, keepdims=True)
    total = jnp.sum(jnp.exp(values - top), axis=1, keepdims=True)
    row = lax.broadcasted_iota(jnp.int32, (tokens, tokens), 0)
    col = lax.broadcasted_iota(jnp.int32, (tokens, tokens), 1)
    flip = lambda c: jnp.sum(jnp.where(row == col, c, 0.0), axis=0, keepdims=True)
    rest = jnp.zeros((4, tokens), F32)
    stats = jnp.concatenate([s_ref[...], flip(top), flip(total), rest], axis=0)
    stats_ref[...] = stats
    lanes = message_ref.shape[2]
    if lanes > tokens:
        stats = jnp.concatenate([stats, jnp.zeros((8, lanes - tokens), F32)], axis=1)
    for k in range(message_ref.shape[0]):
        message_ref[k] = stats


def stats_message(teacher, s_stats, count):
    tokens = s_stats.shape[1]
    lanes = -(-tokens // LANES) * LANES
    return pl.pallas_call(
        message_kernel,
        in_specs=in_vmem(2),
        out_specs=in_vmem(2),
        out_shape=[
            jax.ShapeDtypeStruct((8, tokens), F32),
            pltpu.HBM((count, 8, lanes), F32),
        ],
        compiler_params=params(12 * MIB),
    )(teacher, s_stats)


def products_kernel(tile, t_ref, lt_ref, stats_ref, w_ref, u_ref, both_ref, *refs):
    buffer, packed, both, sems, both_sem = refs
    rows = w_ref.shape[0]
    steps = rows // tile
    rest = rows - steps * tile
    ahead = min(2, steps)

    def fetch(step):
        here = pl.ds(pl.multiple_of(step * tile, tile), tile)
        return pltpu.make_async_copy(w_ref.at[here, :], buffer.at[here, :], sems.at[step])

    last = slice(steps * tile, rows)
    final = pltpu.make_async_copy(w_ref.at[last, :], buffer.at[last, :], sems.at[steps])
    for step in range(ahead):
        fetch(step).start()

    values = teacher_values(t_ref)
    tokens = values.shape[0]
    top = jnp.max(values, axis=1, keepdims=True)
    teach = jnp.exp(values - top)
    teach = teach * (1.0 / jnp.sum(teach, axis=1, keepdims=True))
    share = jnp.exp(lt_ref[...] - stats_ref[0:1, :]) * (1.0 / stats_ref[1:2, :])
    both[...] = jnp.concatenate([share, teach.T], axis=1)
    keep = pltpu.make_async_copy(both, both_ref, both_sem)
    keep.start()
    packed[:tokens, :] = (share.T - teach).astype(BF16)
    packed[tokens:, :] = teach.astype(BF16)
    u_ref[...] = jnp.zeros_like(u_ref)
    if rest:
        final.start()

    def body(step, carry):
        @pl.when(step + ahead < steps)
        def _():
            fetch(step + ahead).start()

        fetch(step).wait()
        here = pl.ds(pl.multiple_of(step * tile, tile), tile)
        u_ref[...] += jnp.dot(packed[:, here], buffer[here, :], preferred_element_type=F32)
        return carry

    if steps:
        lax.fori_loop(0, steps, body, 0)
    if rest:
        final.wait()
        u_ref[...] += jnp.dot(packed[:, last], buffer[last, :], preferred_element_type=F32)
    keep.wait()


def local_products(weight, teacher, lt, stats):
    rows, width = weight.shape
    tokens = lt.shape[1]
    tile = 768
    anywhere = pl.BlockSpec(memory_space=pl.ANY)
    return pl.pallas_call(
        functools.partial(products_kernel, tile),
        in_specs=[*in_vmem(3), anywhere],
        out_specs=[*in_vmem(1), anywhere],
        out_shape=[
            jax.ShapeDtypeStruct((2 * tokens, width), F32),
            pltpu.HBM((rows, 2 * tokens), F32),
        ],
        scratch_shapes=[
            pltpu.VMEM((rows, width), BF16),
            pltpu.VMEM((2 * tokens, rows), BF16),
            pltpu.VMEM((rows, 2 * tokens), F32),
            pltpu.SemaphoreType.DMA((rows // tile + 1,)),
            pltpu.SemaphoreType.DMA,
        ],
        compiler_params=params(46 * MIB),
        cost_estimate=pl.CostEstimate(
            flops=8 * rows * width * tokens, bytes_accessed=2 * rows * width, transcendentals=0
        ),
    )(teacher, lt, stats, weight)


def combine_kernel(all_ref, mine_ref, u_ref, hp_ref, mass_ref):
    tokens = mine_ref.shape[1]

    def mass(k):
        top_all = all_ref[:, k, :tokens]
        top = jnp.max(top_all, axis=0, keepdims=True)
        total = jnp.sum(jnp.exp(top_all - top) * all_ref[:, k + 1, :tokens], axis=0, keepdims=True)
        return jnp.exp(mine_ref[k : k + 1, :] - top) * mine_ref[k + 1 : k + 2, :] / total

    student, teacher = mass(0), mass(2)
    mass_ref[...] = GRAD_SCALE * jnp.concatenate([student, teacher], axis=1)
    row = lax.broadcasted_iota(jnp.int32, (tokens, tokens), 0)
    col = lax.broadcasted_iota(jnp.int32, (tokens, tokens), 1)
    flip = lambda r: jnp.sum(jnp.where(row == col, r, 0.0), axis=1, keepdims=True)
    scale_x = GRAD_SCALE * flip(student)
    scale_t = GRAD_SCALE * flip(student - teacher)
    width = hp_ref.shape[2]
    for v in range(hp_ref.shape[0]):
        cols = slice(v * width, (v + 1) * width)
        hp_ref[v] = (u_ref[:tokens, cols] * scale_x + u_ref[tokens:, cols] * scale_t).astype(BF16)


def combine(stats_all, stats, products, n_v):
    tokens = stats.shape[1]
    width = products.shape[1] // n_v
    return pl.pallas_call(
        combine_kernel,
        in_specs=in_vmem(3),
        out_specs=in_vmem(2),
        out_shape=[
            pltpu.HBM((n_v, tokens, width), BF16),
            jax.ShapeDtypeStruct((1, 2 * tokens), F32),
        ],
        compiler_params=params(12 * MIB),
    )(stats_all, stats, products)


def head_kernel(both_ref, mass_ref, hidden_ref, out_ref):
    tokens, width = hidden_ref.shape
    scaled = both_ref[...] * mass_ref[...]
    grad = (scaled[:, :tokens] - scaled[:, tokens:]).astype(BF16)
    tile = column_tile(width, 256)
    for k in range(0, width, tile):
        out_ref[:, k : k + tile] = jnp.dot(
            grad, hidden_ref[:, k : k + tile], preferred_element_type=F32
        ).astype(BF16)


def head_gradient(both, mass, hidden):
    rows = both.shape[0]
    tokens, width = hidden.shape
    tile = row_tile(rows, 528)
    return pl.pallas_call(
        head_kernel,
        grid=(rows // tile,),
        in_specs=[pl.BlockSpec((tile, 2 * tokens), lambda i: (i, 0)), *in_vmem(2)],
        out_specs=pl.BlockSpec((tile, width), lambda i: (i, 0)),
        out_shape=jax.ShapeDtypeStruct((rows, width), BF16),
        compiler_params=params(24 * MIB),
        cost_estimate=pl.CostEstimate(
            flops=8 * rows * width * tokens, bytes_accessed=2 * rows * width, transcendentals=0
        ),
    )(both, mass, hidden)


def exchange(parts, axes):
    return lax.all_to_all(parts, axes, split_axis=0, concat_axis=0, tiled=True)


def shards(n_dp, n_v, hidden, head_weight, teacher_logits):
    everyone = ("vk", "vs", "pl", "co")
    n_pl = n_dp // 2
    count = n_dp * n_v
    group, width = hidden.shape
    weight = head_weight[0]

    copies = jnp.broadcast_to(hidden[None], (n_v * n_pl, group, width))
    own = exchange(copies, ("vk", "vs", "pl"))
    other = lax.ppermute(own, "co", [(0, 1), (1, 0)])
    square = (n_v, n_pl, group, width)

    piece = teacher_logits[0]
    half, cols = piece.shape[0], piece.shape[1] // (2 * n_dp)
    sends = piece.reshape(half, 2, n_dp, cols).transpose(2, 1, 0, 3).reshape(2 * n_dp, half, cols)
    sends, own = lax.optimization_barrier((sends, own))
    teacher = exchange(sends, ("pl", "co", "vs"))

    lt, s_stats, every_row = student_logits(own.reshape(square), other.reshape(square), weight)
    stats, message = stats_message(teacher, s_stats, count)
    stats_all = exchange(message, everyone)
    products, both = local_products(weight, teacher, lt, stats)
    partial_value, mass = combine(stats_all, stats, products, n_v)
    pieces = exchange(partial_value.reshape(count, group, width), everyone)
    head_grad = head_gradient(both, mass, every_row)
    hidden_grad = jnp.sum(pieces.astype(F32), axis=0).astype(BF16)
    return hidden_grad, head_grad[None]


def solution(mesh):
    n_dp, n_v = mesh.shape["dp"], mesh.shape["vocab"]
    split = Mesh(mesh.devices.reshape(n_dp // 2, 2, n_v // 2, 2), ("pl", "co", "vk", "vs"))
    dp, vocab = ("pl", "co"), ("vk", "vs")
    return jax.shard_map(
        functools.partial(shards, n_dp, n_v),
        mesh=split,
        in_specs=(P(dp, vocab), P(vocab, dp, None), P(vocab, dp, None)),
        out_specs=(P(dp, vocab), P(vocab, dp, None)),
        check_vma=False,
    )
```

```python
import functools

import jax
import jax.numpy as jnp
from jax import lax
from jax.experimental import pallas as pl
from jax.experimental.pallas import tpu as pltpu
from jax.sharding import Mesh
from jax.sharding import PartitionSpec as P

GRAD_SCALE = 32.0
F32 = jnp.float32
BF16 = jnp.bfloat16
MIB = 2**20
LANES = 128


def row_tile(rows, limit):
    best = rows
    for tile in range(16, limit + 1, 16):
        if rows % tile == 0:
            best = tile
    return best


def column_tile(width, limit):
    return max(c for c in range(LANES, limit + 1, LANES) if width % c == 0)


def tile_rows(step, tile, rows):
    if tile == rows:
        return slice(None)
    return pl.ds(pl.multiple_of(step * tile, tile), tile)


def params(limit):
    return pltpu.CompilerParams(vmem_limit_bytes=limit)


def whole(shape):
    return pl.BlockSpec(shape, lambda *_: (0,) * len(shape))


def in_vmem(count):
    return [pl.BlockSpec(memory_space=pltpu.VMEM)] * count


def logits_kernel(tile, n_pl, *refs):
    parts, w_ref = refs[: 2 * n_pl], refs[2 * n_pl]
    lt_ref, stats_ref, hidden_ref, buffer, turned, staged, sems = refs[2 * n_pl + 1 :]
    rows = w_ref.shape[0]
    steps = rows // tile
    ahead = min(3, steps)

    def fetch(step):
        here = tile_rows(step, tile, rows)
        return pltpu.make_async_copy(w_ref.at[here, :], buffer.at[here, :], sems.at[step])

    for step in range(ahead):
        fetch(step).start()

    n_v, _, chunk = parts[0].shape
    core, plane = lax.axis_index("co"), lax.axis_index("pl")
    shard = lax.axis_index("vk") * 2 + lax.axis_index("vs")
    for s in range(n_pl):
        staged[core, s] = parts[s][...].astype(F32)
        staged[1 - core, s] = parts[n_pl + s][...].astype(F32)
    for v in range(n_v):
        cols = slice(v * chunk, (v + 1) * chunk)
        groups = [staged[c, p ^ plane, v ^ shard] for p in range(n_pl) for c in range(2)]
        block = jnp.concatenate(groups, axis=0)
        hidden_ref[:, cols] = block.astype(BF16)
        turned[cols, :] = block.T.astype(BF16)

    def collect(step, top, total):
        values = lt_ref[tile_rows(step, tile, rows), :]
        higher = jnp.maximum(top, jnp.max(values, axis=0, keepdims=True))
        added = jnp.sum(jnp.exp(values - higher), axis=0, keepdims=True)
        return higher, total * jnp.exp(top - higher) + added

    def multiply(step):
        @pl.when(step + ahead < steps)
        def _():
            fetch(step + ahead).start()

        fetch(step).wait()
        here = tile_rows(step, tile, rows)
        return jnp.dot(buffer[here, :], turned[...], preferred_element_type=F32)

    lt_ref[tile_rows(0, tile, rows), :] = multiply(0)

    def body(step, carry):
        values = multiply(step)
        carry = collect(step - 1, *carry)
        lt_ref[tile_rows(step, tile, rows), :] = values
        return carry

    low = jnp.full((1, lt_ref.shape[1]), -1e30, F32)
    carry = (low, jnp.zeros_like(low))
    if steps > 1:
        carry = lax.fori_loop(1, steps, body, carry)
    stats_ref[...] = jnp.concatenate(collect(steps - 1, *carry), axis=0)


def student_logits(parts, weight):
    rows, width = weight.shape
    n_v, group, _ = parts[0].shape
    tokens = len(parts) * group
    tile = row_tile(rows, 528)
    return pl.pallas_call(
        functools.partial(logits_kernel, tile, len(parts) // 2),
        in_specs=[*in_vmem(len(parts)), pl.BlockSpec(memory_space=pl.ANY)],
        out_specs=in_vmem(3),
        out_shape=[
            jax.ShapeDtypeStruct((rows, tokens), F32),
            jax.ShapeDtypeStruct((2, tokens), F32),
            pltpu.HBM((tokens, width), BF16),
        ],
        scratch_shapes=[
            pltpu.VMEM((rows, width), BF16),
            pltpu.VMEM((width, tokens), BF16),
            pltpu.VMEM((2, len(parts) // 2, *parts[0].shape), F32),
            pltpu.SemaphoreType.DMA((rows // tile,)),
        ],
        compiler_params=params(46 * MIB),
        cost_estimate=pl.CostEstimate(
            flops=8 * rows * width * tokens, bytes_accessed=2 * rows * width, transcendentals=0
        ),
    )(*parts, weight)


def split_kernel(t_ref, out_ref):
    total, (count, _, cols) = t_ref.shape[1], out_ref.shape
    n_dp = count // 2
    for s in range(2):
        for d in range(n_dp):
            start = (s * n_dp + d) * cols
            low = start // LANES * LANES
            high = min(-(-(start + cols) // LANES) * LANES, total)
            values = t_ref[:, low:high].astype(F32)
            out_ref[d * 2 + s] = values[:, start - low : start - low + cols].astype(BF16)


def split_teacher(piece, n_dp):
    half, total = piece.shape
    return pl.pallas_call(
        split_kernel,
        in_specs=in_vmem(1),
        out_specs=pl.BlockSpec(memory_space=pltpu.VMEM),
        out_shape=pltpu.HBM((2 * n_dp, half, total // (2 * n_dp)), BF16),
        compiler_params=params(12 * MIB),
    )(piece)


def teacher_values(t_ref):
    return jnp.concatenate([t_ref[j].astype(F32) for j in range(t_ref.shape[0])], axis=0)


def message_kernel(t_ref, s_ref, stats_ref, message_ref):
    values = teacher_values(t_ref)
    tokens = values.shape[0]
    top = jnp.max(values, axis=1, keepdims=True)
    total = jnp.sum(jnp.exp(values - top), axis=1, keepdims=True)
    row = lax.broadcasted_iota(jnp.int32, (tokens, tokens), 0)
    col = lax.broadcasted_iota(jnp.int32, (tokens, tokens), 1)
    flip = lambda c: jnp.sum(jnp.where(row == col, c, 0.0), axis=0, keepdims=True)
    rest = jnp.zeros((4, tokens), F32)
    stats = jnp.concatenate([s_ref[...], flip(top), flip(total), rest], axis=0)
    stats_ref[...] = stats
    lanes = message_ref.shape[2]
    if lanes > tokens:
        stats = jnp.concatenate([stats, jnp.zeros((8, lanes - tokens), F32)], axis=1)
    for k in range(message_ref.shape[0]):
        message_ref[k] = stats


def stats_message(teacher, s_stats, count):
    tokens = s_stats.shape[1]
    lanes = -(-tokens // LANES) * LANES
    return pl.pallas_call(
        message_kernel,
        in_specs=in_vmem(2),
        out_specs=in_vmem(2),
        out_shape=[
            jax.ShapeDtypeStruct((8, tokens), F32),
            pltpu.HBM((count, 8, lanes), F32),
        ],
        compiler_params=params(12 * MIB),
    )(teacher, s_stats)


def products_kernel(tile, t_ref, lt_ref, stats_ref, w_ref, u_ref, both_ref, *refs):
    buffer, packed, both, sems, both_sem = refs
    rows = w_ref.shape[0]
    steps = rows // tile
    rest = rows - steps * tile
    ahead = min(3, steps)

    def fetch(step):
        here = pl.ds(pl.multiple_of(step * tile, tile), tile)
        return pltpu.make_async_copy(w_ref.at[here, :], buffer.at[here, :], sems.at[step])

    last = slice(steps * tile, rows)
    final = pltpu.make_async_copy(w_ref.at[last, :], buffer.at[last, :], sems.at[steps])
    for step in range(ahead):
        fetch(step).start()

    values = teacher_values(t_ref)
    tokens = values.shape[0]
    top = jnp.max(values, axis=1, keepdims=True)
    teach = jnp.exp(values - top)
    teach = teach * (1.0 / jnp.sum(teach, axis=1, keepdims=True))
    share = jnp.exp(lt_ref[...] - stats_ref[0:1, :]) * (1.0 / stats_ref[1:2, :])
    both[...] = jnp.concatenate([share, teach.T], axis=1)
    keep = pltpu.make_async_copy(both, both_ref, both_sem)
    keep.start()
    packed[:tokens, :] = (share.T - teach).astype(BF16)
    packed[tokens:, :] = teach.astype(BF16)
    u_ref[...] = jnp.zeros_like(u_ref)
    if rest:
        final.start()

    def add_products(here):
        width = u_ref.shape[1]
        block = column_tile(width, 256)
        for k in range(0, width, block):
            cols = slice(k, k + block)
            u_ref[:, cols] += jnp.dot(
                packed[:, here], buffer[here, cols], preferred_element_type=F32
            )

    def body(step, carry):
        @pl.when(step + ahead < steps)
        def _():
            fetch(step + ahead).start()

        fetch(step).wait()
        add_products(pl.ds(pl.multiple_of(step * tile, tile), tile))
        return carry

    if steps:
        lax.fori_loop(0, steps, body, 0)
    if rest:
        final.wait()
        add_products(last)
    keep.wait()


def local_products(weight, teacher, lt, stats):
    rows, width = weight.shape
    tokens = lt.shape[1]
    tile = 768
    anywhere = pl.BlockSpec(memory_space=pl.ANY)
    return pl.pallas_call(
        functools.partial(products_kernel, tile),
        in_specs=[*in_vmem(3), anywhere],
        out_specs=[*in_vmem(1), anywhere],
        out_shape=[
            jax.ShapeDtypeStruct((2 * tokens, width), F32),
            pltpu.HBM((rows, 2 * tokens), F32),
        ],
        scratch_shapes=[
            pltpu.VMEM((rows, width), BF16),
            pltpu.VMEM((2 * tokens, rows), BF16),
            pltpu.VMEM((rows, 2 * tokens), F32),
            pltpu.SemaphoreType.DMA((rows // tile + 1,)),
            pltpu.SemaphoreType.DMA,
        ],
        compiler_params=params(46 * MIB),
        cost_estimate=pl.CostEstimate(
            flops=8 * rows * width * tokens, bytes_accessed=2 * rows * width, transcendentals=0
        ),
    )(teacher, lt, stats, weight)


def combine_kernel(all_ref, mine_ref, u_ref, hp_ref, mass_ref):
    tokens = mine_ref.shape[1]

    def mass(k):
        top_all = all_ref[:, k, :tokens]
        top = jnp.max(top_all, axis=0, keepdims=True)
        total = jnp.sum(jnp.exp(top_all - top) * all_ref[:, k + 1, :tokens], axis=0, keepdims=True)
        return jnp.exp(mine_ref[k : k + 1, :] - top) * mine_ref[k + 1 : k + 2, :] / total

    student, teacher = mass(0), mass(2)
    mass_ref[...] = GRAD_SCALE * jnp.concatenate([student, teacher], axis=1)
    row = lax.broadcasted_iota(jnp.int32, (tokens, tokens), 0)
    col = lax.broadcasted_iota(jnp.int32, (tokens, tokens), 1)
    flip = lambda r: jnp.sum(jnp.where(row == col, r, 0.0), axis=1, keepdims=True)
    scale_x = GRAD_SCALE * flip(student)
    scale_t = GRAD_SCALE * flip(student - teacher)
    width = hp_ref.shape[2]
    for v in range(hp_ref.shape[0]):
        cols = slice(v * width, (v + 1) * width)
        hp_ref[v] = (u_ref[:tokens, cols] * scale_x + u_ref[tokens:, cols] * scale_t).astype(BF16)


def combine(stats_all, stats, products, n_v):
    tokens = stats.shape[1]
    width = products.shape[1] // n_v
    return pl.pallas_call(
        combine_kernel,
        in_specs=in_vmem(3),
        out_specs=in_vmem(2),
        out_shape=[
            pltpu.HBM((n_v, tokens, width), BF16),
            jax.ShapeDtypeStruct((1, 2 * tokens), F32),
        ],
        compiler_params=params(12 * MIB),
    )(stats_all, stats, products)


def head_kernel(tile, both_ref, mass_ref, hidden_ref, out_ref, both, hidden, grads, slots, sems, out_sems):
    rows = both_ref.shape[0]
    tokens, width = hidden_ref.shape
    steps = rows // tile
    load_both = pltpu.make_async_copy(both_ref, both, sems.at[0])
    load_hidden = pltpu.make_async_copy(hidden_ref, hidden, sems.at[1])
    load_both.start()
    load_hidden.start()
    load_both.wait()
    block = column_tile(width, 256)

    def gradient(step):
        scaled = both[tile_rows(step, tile, rows), :] * mass_ref[...]
        return (scaled[:, :tokens] - scaled[:, tokens:]).astype(BF16)

    def store(step):
        slot = lax.rem(step, 2)
        here = tile_rows(step, tile, rows)
        return pltpu.make_async_copy(slots.at[slot], out_ref.at[here, :], out_sems.at[slot])

    grads[0] = gradient(0)
    load_hidden.wait()

    def body(step, carry):
        slot = lax.rem(step, 2)

        @pl.when(step >= 2)
        def _():
            store(step - 2).wait()

        following = gradient(jnp.minimum(step + 1, steps - 1))
        grad = grads[slot]
        for k in range(0, width, block):
            cols = slice(k, k + block)
            slots[slot, :, cols] = jnp.dot(
                grad, hidden[:, cols], preferred_element_type=F32
            ).astype(BF16)
        grads[1 - slot] = following
        store(step).start()
        return carry

    lax.fori_loop(0, steps, body, 0)
    for step in range(max(0, steps - 2), steps):
        store(step).wait()


def head_gradient(both, mass, hidden):
    rows = both.shape[0]
    tokens, width = hidden.shape
    tile = row_tile(rows, 432)
    anywhere = pl.BlockSpec(memory_space=pl.ANY)
    in_hbm = lambda x: pltpu.with_memory_space_constraint(x, pltpu.HBM)
    return pl.pallas_call(
        functools.partial(head_kernel, tile),
        in_specs=[anywhere, *in_vmem(1), anywhere],
        out_specs=anywhere,
        out_shape=jax.ShapeDtypeStruct((rows, width), BF16),
        scratch_shapes=[
            pltpu.VMEM((rows, 2 * tokens), F32),
            pltpu.VMEM((tokens, width), BF16),
            pltpu.VMEM((2, tile, tokens), BF16),
            pltpu.VMEM((2, tile, width), BF16),
            pltpu.SemaphoreType.DMA((2,)),
            pltpu.SemaphoreType.DMA((2,)),
        ],
        compiler_params=params(24 * MIB),
        cost_estimate=pl.CostEstimate(
            flops=8 * rows * width * tokens, bytes_accessed=2 * rows * width, transcendentals=0
        ),
    )(in_hbm(both), mass, in_hbm(hidden))


def exchange(parts, axes):
    return lax.all_to_all(parts, axes, split_axis=0, concat_axis=0, tiled=True)


def partners(value, axes, size):
    got = [value]
    for s in range(1, size):
        got.append(lax.ppermute(value, axes, [(i, i ^ s) for i in range(size)]))
    return got


def shards(n_dp, n_v, hidden, head_weight, teacher_logits):
    everyone = ("vk", "vs", "pl", "co")
    n_pl = n_dp // 2
    count = n_dp * n_v
    group, width = hidden.shape
    weight = head_weight[0]

    columns = jnp.stack(partners(hidden, ("vk", "vs"), n_v))
    mine = partners(columns, "pl", n_pl)
    others = [lax.ppermute(part, "co", [(0, 1), (1, 0)]) for part in mine]

    sends = split_teacher(teacher_logits[0], n_dp)
    near = min(1, n_pl - 1)
    sends, mine[near] = lax.optimization_barrier((sends, mine[near]))
    teacher = exchange(sends, ("pl", "co", "vs"))

    lt, s_stats, every_row = student_logits(mine + others, weight)
    stats, message = stats_message(teacher, s_stats, count)
    stats_all = exchange(message, everyone)
    products, both = local_products(weight, teacher, lt, stats)
    partial_value, mass = combine(stats_all, stats, products, n_v)
    pieces = exchange(partial_value.reshape(count, group, width), everyone)
    head_grad = head_gradient(both, mass, every_row)
    hidden_grad = jnp.sum(pieces.astype(F32), axis=0).astype(BF16)
    return hidden_grad, head_grad[None]


def solution(mesh):
    n_dp, n_v = mesh.shape["dp"], mesh.shape["vocab"]
    split = Mesh(mesh.devices.reshape(n_dp // 2, 2, n_v // 2, 2), ("pl", "co", "vk", "vs"))
    dp, vocab = ("pl", "co"), ("vk", "vs")
    return jax.shard_map(
        functools.partial(shards, n_dp, n_v),
        mesh=split,
        in_specs=(P(dp, vocab), P(vocab, dp, None), P(vocab, dp, None)),
        out_specs=(P(dp, vocab), P(vocab, dp, None)),
        check_vma=False,
    )
```

```python
import functools

import jax
import jax.numpy as jnp
from jax import lax
from jax.experimental import pallas as pl
from jax.experimental.pallas import tpu as pltpu
from jax.sharding import Mesh
from jax.sharding import PartitionSpec as P

GRAD_SCALE = 32.0
F32 = jnp.float32
BF16 = jnp.bfloat16
MIB = 2**20
LANES = 128


def row_tile(rows, limit):
    best = rows
    for tile in range(16, limit + 1, 16):
        if rows % tile == 0:
            best = tile
    return best


def column_tile(width, limit):
    return max(c for c in range(LANES, limit + 1, LANES) if width % c == 0)


def tile_rows(step, tile, rows):
    if tile == rows:
        return slice(None)
    return pl.ds(pl.multiple_of(step * tile, tile), tile)


def params(limit):
    return pltpu.CompilerParams(vmem_limit_bytes=limit)


def whole(shape):
    return pl.BlockSpec(shape, lambda *_: (0,) * len(shape))


def in_vmem(count):
    return [pl.BlockSpec(memory_space=pltpu.VMEM)] * count


def row_parts(rows):
    if rows < 1024:
        return [(0, rows)]
    first, second = round(rows * 0.42 / 256) * 256, round(rows * 0.38 / 256) * 256
    return [(0, first), (first, second), (first + second, rows - first - second)]


def logits_kernel(n_pl, *refs):
    parts, w_ref = refs[: 2 * n_pl], refs[2 * n_pl]
    lt_ref, stats_ref, hidden_ref = refs[2 * n_pl + 1 : 2 * n_pl + 4]
    held, (turned, staged, sems) = refs[2 * n_pl + 4 : -3], refs[-3:]
    places = row_parts(w_ref.shape[0])

    def fetch(part):
        start, size = places[part]
        for k, at in enumerate(range(0, size, 512)):
            count = min(512, size - at)
            yield pltpu.make_async_copy(
                w_ref.at[start + at : start + at + count, :],
                held[part].at[at : at + count, :],
                sems.at[part, k],
            )

    for copy in fetch(0):
        copy.start()

    n_v, _, chunk = parts[0].shape
    core, plane = lax.axis_index("co"), lax.axis_index("pl")
    shard = lax.axis_index("vk") * 2 + lax.axis_index("vs")
    for s in range(n_pl):
        staged[core, s] = parts[s][...].astype(F32)
        staged[1 - core, s] = parts[n_pl + s][...].astype(F32)
    for v in range(n_v):
        cols = slice(v * chunk, (v + 1) * chunk)
        groups = [staged[c, p ^ plane, v ^ shard] for p in range(n_pl) for c in range(2)]
        block = jnp.concatenate(groups, axis=0)
        hidden_ref[:, cols] = block.astype(BF16)
        turned[cols, :] = block.T.astype(BF16)

    for part, (start, size) in enumerate(places):
        if part + 1 < len(places):
            for copy in fetch(part + 1):
                copy.start()
        for copy in fetch(part):
            copy.wait()
        lt_ref[start : start + size, :] = jnp.dot(
            held[part][...], turned[...], preferred_element_type=F32
        )
    values = lt_ref[...]
    top = jnp.max(values, axis=0, keepdims=True)
    total = jnp.sum(jnp.exp(values - top), axis=0, keepdims=True)
    stats_ref[...] = jnp.concatenate([top, total], axis=0)


def student_logits(parts, weight):
    rows, width = weight.shape
    n_v, group, _ = parts[0].shape
    tokens = len(parts) * group
    places = row_parts(rows)
    return pl.pallas_call(
        functools.partial(logits_kernel, len(parts) // 2),
        in_specs=[*in_vmem(len(parts)), pl.BlockSpec(memory_space=pl.ANY)],
        out_specs=in_vmem(3 + len(places)),
        out_shape=[
            jax.ShapeDtypeStruct((rows, tokens), F32),
            jax.ShapeDtypeStruct((2, tokens), F32),
            pltpu.HBM((tokens, width), BF16),
            *[pltpu.VMEM((size, width), BF16) for _, size in places],
        ],
        scratch_shapes=[
            pltpu.VMEM((width, tokens), BF16),
            pltpu.VMEM((2, len(parts) // 2, *parts[0].shape), F32),
            pltpu.SemaphoreType.DMA((len(places), max(size for _, size in places) // 512 + 1)),
        ],
        compiler_params=params(8 * MIB),
        cost_estimate=pl.CostEstimate(
            flops=8 * rows * width * tokens, bytes_accessed=2 * rows * width, transcendentals=0
        ),
    )(*parts, weight)


def split_kernel(t_ref, give_ref, keep_ref, buffer, sem):
    load = pltpu.make_async_copy(t_ref, buffer, sem)
    load.start()
    load.wait()
    half = buffer.shape[1] // 2
    n_dp, _, cols = keep_ref.shape
    parity = lax.axis_index("vs")
    for out_ref, side in ((give_ref, 1 - parity), (keep_ref, parity)):
        for d in range(n_dp):
            start = d * cols
            low = start // LANES * LANES
            high = min(-(-(start + cols) // LANES) * LANES, half)
            if half % LANES:
                first, second = buffer[:, low:high], buffer[:, half + low : half + high]
                values = jnp.where(side == 0, first.astype(F32), second.astype(F32))
            else:
                origin = pl.multiple_of(side * half, LANES)
                values = buffer[:, pl.ds(origin + low, high - low)].astype(F32)
            out_ref[d] = values[:, start - low : start - low + cols].astype(BF16)


def split_teacher(piece, n_dp):
    group, total = piece.shape
    shape = (n_dp, group, total // (2 * n_dp))
    return pl.pallas_call(
        split_kernel,
        in_specs=[pl.BlockSpec(memory_space=pl.ANY)],
        out_specs=in_vmem(2),
        out_shape=[jax.ShapeDtypeStruct(shape, BF16)] * 2,
        scratch_shapes=[pltpu.VMEM(piece.shape, BF16), pltpu.SemaphoreType.DMA],
        compiler_params=params(8 * MIB),
    )(piece)


def gather_kernel(keep_ref, got_ref, *out_refs):
    n_dp = keep_ref.shape[0]
    parity = lax.axis_index("vs")
    me = lax.axis_index("pl") * 2 + lax.axis_index("co")
    for s in range(n_dp):
        kept, got = keep_ref[me ^ s].astype(F32), got_ref[me ^ s].astype(F32)
        first, second = jnp.where(parity == 0, kept, got), jnp.where(parity == 0, got, kept)
        out_refs[s][...] = jnp.concatenate([first, second], axis=0).astype(BF16)


def join_halves(keep, got):
    n_dp, half, cols = keep.shape
    return pl.pallas_call(
        gather_kernel,
        in_specs=in_vmem(2),
        out_specs=in_vmem(n_dp),
        out_shape=[jax.ShapeDtypeStruct((2 * half, cols), BF16)] * n_dp,
        compiler_params=params(8 * MIB),
    )(keep, got)


def message_kernel(n_dp, *refs):
    parts, s_ref = refs[:n_dp], refs[n_dp]
    stats_ref, t_ref, staged = refs[n_dp + 1 :]
    me = lax.axis_index("pl") * 2 + lax.axis_index("co")
    for s in range(n_dp):
        staged[me ^ s] = parts[s][...].astype(F32)
    values = jnp.concatenate([staged[g] for g in range(n_dp)], axis=0)
    tokens = values.shape[0]
    top = jnp.max(values, axis=1, keepdims=True)
    weights = jnp.exp(values - top)
    total = jnp.sum(weights, axis=1, keepdims=True)
    t_ref[...] = weights * (1.0 / total)
    row = lax.broadcasted_iota(jnp.int32, (tokens, tokens), 0)
    col = lax.broadcasted_iota(jnp.int32, (tokens, tokens), 1)
    flip = lambda c: jnp.sum(jnp.where(row == col, c, 0.0), axis=0, keepdims=True)
    rest = jnp.zeros((4, tokens), F32)
    stats = jnp.concatenate([s_ref[...], flip(top), flip(total), rest], axis=0)
    lanes = stats_ref.shape[1]
    if lanes > tokens:
        stats = jnp.concatenate([stats, jnp.zeros((8, lanes - tokens), F32)], axis=1)
    stats_ref[...] = stats


def stats_message(teacher, s_stats):
    tokens = s_stats.shape[1]
    lanes = -(-tokens // LANES) * LANES
    group, cols = teacher[0].shape
    return pl.pallas_call(
        functools.partial(message_kernel, len(teacher)),
        in_specs=in_vmem(len(teacher) + 1),
        out_specs=in_vmem(2),
        out_shape=[
            jax.ShapeDtypeStruct((8, lanes), F32),
            jax.ShapeDtypeStruct((tokens, cols), F32),
        ],
        scratch_shapes=[pltpu.VMEM((len(teacher), group, cols), F32)],
        compiler_params=params(8 * MIB),
        cost_estimate=pl.CostEstimate(flops=1, bytes_accessed=1, transcendentals=0),
    )(*teacher, s_stats)


def merged(refs, k):
    tops = [ref[k : k + 1, :] for ref in refs]
    top = functools.reduce(jnp.maximum, tops)
    total = sum(jnp.exp(t - top) * ref[k + 1 : k + 2, :] for t, ref in zip(tops, refs))
    return top, total


def merge_kernel(*refs):
    sources, out_ref = refs[:-1], refs[-1]
    rest = jnp.zeros((4, out_ref.shape[1]), F32)
    out_ref[...] = jnp.concatenate([*merged(sources, 0), *merged(sources, 2), rest], axis=0)


def merge(messages):
    return pl.pallas_call(
        merge_kernel,
        in_specs=in_vmem(len(messages)),
        out_specs=pl.BlockSpec(memory_space=pltpu.VMEM),
        out_shape=jax.ShapeDtypeStruct(messages[0].shape, F32),
        compiler_params=params(2 * MIB),
        cost_estimate=pl.CostEstimate(flops=1, bytes_accessed=1, transcendentals=0),
    )(*messages)


def products_kernel(t_ref, lt_ref, stats_ref, *refs):
    held, (u_ref, both_ref, packed, both, sem) = refs[:-5], refs[-5:]
    tokens = t_ref.shape[0]
    teach = t_ref[...]
    share = jnp.exp(lt_ref[...] - stats_ref[0:1, :tokens]) * (1.0 / stats_ref[1:2, :tokens])
    both[...] = jnp.concatenate([share, teach.T], axis=1)
    keep = pltpu.make_async_copy(both, both_ref, sem)
    keep.start()
    packed[:tokens, :] = (share.T - teach).astype(BF16)
    packed[tokens:, :] = teach.astype(BF16)
    width = held[0].shape[1]
    places = row_parts(t_ref.shape[1])
    block = column_tile(width, 256)

    def body(step, carry):
        here = pl.ds(pl.multiple_of(step * block, block), block)
        u_ref[:, here] = sum(
            jnp.dot(packed[:, at : at + size], w_ref[:, here], preferred_element_type=F32)
            for (at, size), w_ref in zip(places, held)
        )
        return carry

    lax.fori_loop(0, width // block, body, 0)
    keep.wait()


def local_products(weights, teacher, lt, stats):
    width = weights[0].shape[1]
    rows, tokens = lt.shape
    return pl.pallas_call(
        products_kernel,
        in_specs=in_vmem(3 + len(weights)),
        out_specs=[*in_vmem(1), pl.BlockSpec(memory_space=pl.ANY)],
        out_shape=[
            jax.ShapeDtypeStruct((2 * tokens, width), F32),
            pltpu.HBM((rows, 2 * tokens), F32),
        ],
        scratch_shapes=[
            pltpu.VMEM((2 * tokens, rows), BF16),
            pltpu.VMEM((rows, 2 * tokens), F32),
            pltpu.SemaphoreType.DMA,
        ],
        compiler_params=params(8 * MIB),
        cost_estimate=pl.CostEstimate(
            flops=8 * rows * width * tokens, bytes_accessed=0, transcendentals=0
        ),
    )(teacher, lt, stats, *weights)


def combine_kernel(n_dp, *refs):
    messages, (mine_ref, u_ref, hp_ref, mass_ref) = refs[:n_dp], refs[n_dp:]
    tokens = u_ref.shape[0] // 2

    def mass(k):
        top, total = merged(messages, k)
        share = jnp.exp(mine_ref[k : k + 1, :] - top) * mine_ref[k + 1 : k + 2, :] / total
        return share[:, :tokens]

    student, teacher = mass(0), mass(2)
    mass_ref[...] = GRAD_SCALE * jnp.concatenate([student, teacher], axis=1)
    row = lax.broadcasted_iota(jnp.int32, (tokens, tokens), 0)
    col = lax.broadcasted_iota(jnp.int32, (tokens, tokens), 1)
    flip = lambda r: jnp.sum(jnp.where(row == col, r, 0.0), axis=1, keepdims=True)
    scale_x = GRAD_SCALE * flip(student)
    scale_t = GRAD_SCALE * flip(student - teacher)
    width = hp_ref.shape[2]
    for v in range(hp_ref.shape[0]):
        cols = slice(v * width, (v + 1) * width)
        hp_ref[v] = (u_ref[:tokens, cols] * scale_x + u_ref[tokens:, cols] * scale_t).astype(BF16)


def combine(messages, mine, products, n_v):
    tokens = products.shape[0] // 2
    width = products.shape[1] // n_v
    return pl.pallas_call(
        functools.partial(combine_kernel, len(messages)),
        in_specs=in_vmem(len(messages) + 2),
        out_specs=in_vmem(2),
        out_shape=[
            pltpu.HBM((n_v, tokens, width), BF16),
            jax.ShapeDtypeStruct((1, 2 * tokens), F32),
        ],
        compiler_params=params(12 * MIB),
    )(*messages, mine, products)


def head_blocks(width):
    first = column_tile(width, 512)
    rest = column_tile(width - first, 1024)
    return [(0, first)] + [(k, rest) for k in range(first, width, rest)]


def head_kernel(tile, both_ref, mass_ref, hidden_ref, out_ref, both, hidden, result, sems, out_sems):
    rows = both_ref.shape[0]
    tokens, width = hidden_ref.shape
    steps = rows // tile
    load_hidden = pltpu.make_async_copy(hidden_ref, hidden, sems.at[steps])

    def load(step):
        here = tile_rows(step, tile, rows)
        return pltpu.make_async_copy(both_ref.at[here, :], both.at[here, :], sems.at[step])

    def store(step, block, start, size):
        here, cols = tile_rows(step, tile, rows), slice(start, start + size)
        return pltpu.make_async_copy(
            result.at[here, cols], out_ref.at[here, cols], out_sems.at[step, block]
        )

    load(0).start()
    load_hidden.start()
    for step in range(1, steps):
        load(step).start()
    load_hidden.wait()

    def body(step, carry):
        load(step).wait()
        here = tile_rows(step, tile, rows)
        scaled = both[here, :] * mass_ref[...]
        grad = (scaled[:, :tokens] - scaled[:, tokens:]).astype(BF16)
        for block, (start, size) in enumerate(head_blocks(width)):
            inner = column_tile(size, 256)
            for k in range(start, start + size, inner):
                result[here, k : k + inner] = jnp.dot(
                    grad, hidden[:, k : k + inner], preferred_element_type=F32
                ).astype(BF16)
            store(step, block, start, size).start()
        return carry

    lax.fori_loop(0, steps, body, 0)
    for step in range(steps):
        for block, (start, size) in enumerate(head_blocks(width)):
            store(step, block, start, size).wait()


def head_gradient(both, mass, hidden):
    rows = both.shape[0]
    tokens, width = hidden.shape
    tile = row_tile(rows, 1584)
    steps = rows // tile
    anywhere = pl.BlockSpec(memory_space=pl.ANY)
    in_hbm = lambda x: pltpu.with_memory_space_constraint(x, pltpu.HBM)
    return pl.pallas_call(
        functools.partial(head_kernel, tile),
        in_specs=[anywhere, *in_vmem(1), anywhere],
        out_specs=anywhere,
        out_shape=jax.ShapeDtypeStruct((rows, width), BF16),
        scratch_shapes=[
            pltpu.VMEM((rows, 2 * tokens), F32),
            pltpu.VMEM((tokens, width), BF16),
            pltpu.VMEM((rows, width), BF16),
            pltpu.SemaphoreType.DMA((steps + 1,)),
            pltpu.SemaphoreType.DMA((steps, len(head_blocks(width)))),
        ],
        compiler_params=params(46 * MIB),
        cost_estimate=pl.CostEstimate(
            flops=8 * rows * width * tokens, bytes_accessed=2 * rows * width, transcendentals=0
        ),
    )(in_hbm(both), mass, in_hbm(hidden))


def exchange(parts, axes):
    return lax.all_to_all(parts, axes, split_axis=0, concat_axis=0, tiled=True)


def partners(value, axes, size):
    got = [value]
    for s in range(1, size):
        got.append(lax.ppermute(value, axes, [(i, i ^ s) for i in range(size)]))
    return got


def shards(n_dp, n_v, hidden, head_weight, teacher_logits):
    vocab, dp = ("vk", "vs"), ("pl", "co")
    n_pl = n_dp // 2
    group, width = hidden.shape
    swap = [(0, 1), (1, 0)]

    piece = pltpu.with_memory_space_constraint(teacher_logits[0], pltpu.HBM)
    give, keep = split_teacher(piece, n_dp)
    columns = jnp.stack(partners(hidden, vocab, n_v))
    columns, give = lax.optimization_barrier((columns, give))
    got = lax.ppermute(give, "vs", swap)
    mine = partners(columns, "pl", n_pl)
    others = [lax.ppermute(part, "co", swap) for part in mine]
    got, *others = lax.optimization_barrier((got, *others))
    pieces = join_halves(keep, got)
    teacher = list(pieces[:1])
    for s in range(1, n_dp):
        teacher.append(lax.ppermute(pieces[s], dp, [(i, i ^ s) for i in range(n_dp)]))

    lt, s_stats, every_row, *resident = student_logits(mine + others, head_weight[0])
    stats, shares = stats_message(teacher, s_stats)
    messages = partners(merge(partners(stats, vocab, n_v)), dp, n_dp)
    resident = [pltpu.with_memory_space_constraint(x, pltpu.VMEM) for x in resident]
    products, both = local_products(resident, shares, lt, stats)
    partial_value, mass = combine(messages, stats, products, n_v)
    outgoing = partial_value.reshape(n_dp * n_v, group, width)
    incoming = exchange(outgoing, (*vocab, *dp))
    head_grad = head_gradient(both, mass, every_row)
    hidden_grad = jnp.sum(incoming.astype(F32), axis=0).astype(BF16)
    return hidden_grad, head_grad[None]


def solution(mesh):
    n_dp, n_v = mesh.shape["dp"], mesh.shape["vocab"]
    split = Mesh(mesh.devices.reshape(n_dp // 2, 2, n_v // 2, 2), ("pl", "co", "vk", "vs"))
    dp, vocab = ("pl", "co"), ("vk", "vs")
    return jax.shard_map(
        functools.partial(shards, n_dp, n_v),
        mesh=split,
        in_specs=(P(dp, vocab), P(vocab, dp, None), P(vocab, dp, None)),
        out_specs=(P(dp, vocab), P(vocab, dp, None)),
        check_vma=False,
    )
```

```python
import functools

import jax
import jax.numpy as jnp
from jax import lax
from jax.experimental import pallas as pl
from jax.experimental.pallas import tpu as pltpu
from jax.sharding import Mesh
from jax.sharding import PartitionSpec as P

GRAD_SCALE = 32.0
F32 = jnp.float32
BF16 = jnp.bfloat16
MIB = 2**20
LANES = 128
LOGIT_TILE = 512
PRODUCT_TILE = 1024


def row_tile(rows, limit):
    best = rows
    for tile in range(16, limit + 1, 16):
        if rows % tile == 0:
            best = tile
    return best


def column_tile(width, limit):
    return max(c for c in range(LANES, limit + 1, LANES) if width % c == 0)


def tile_rows(step, tile, rows):
    if tile == rows:
        return slice(None)
    return pl.ds(pl.multiple_of(step * tile, tile), tile)


def params(limit):
    return pltpu.CompilerParams(vmem_limit_bytes=limit)


def whole(shape):
    return pl.BlockSpec(shape, lambda *_: (0,) * len(shape))


def in_vmem(count):
    return [pl.BlockSpec(memory_space=pltpu.VMEM)] * count


def copies_kernel(h_ref, out_ref):
    for k in range(out_ref.shape[0]):
        out_ref[k] = h_ref[...]


def copies(hidden, count):
    return pl.pallas_call(
        copies_kernel,
        in_specs=in_vmem(1),
        out_specs=pl.BlockSpec(memory_space=pltpu.VMEM),
        out_shape=pltpu.HBM((count, *hidden.shape), BF16),
        compiler_params=params(8 * MIB),
    )(hidden)


def stream(w_ref, buffer, sems, tile, ahead, compute, between=None):
    rows = w_ref.shape[0]
    steps = rows // tile
    last = slice(steps * tile, rows)
    rest = rows - steps * tile
    ahead = min(ahead, steps)

    def fetch(step):
        here = pl.ds(pl.multiple_of(step * tile, tile), tile)
        return pltpu.make_async_copy(w_ref.at[here, :], buffer.at[here, :], sems.at[step])

    final = pltpu.make_async_copy(w_ref.at[last, :], buffer.at[last, :], sems.at[steps])
    for step in range(ahead):
        fetch(step).start()
    if between is not None:
        between()
    if rest and ahead == steps:
        final.start()

    def body(step, carry):
        @pl.when(step + ahead < steps)
        def _():
            fetch(step + ahead).start()

        if rest and ahead < steps:

            @pl.when(step + ahead == steps)
            def _():
                final.start()

        fetch(step).wait()
        compute(pl.ds(pl.multiple_of(step * tile, tile), tile))
        return carry

    if steps:
        lax.fori_loop(0, steps, body, 0)
    if rest:
        final.wait()
        compute(last)


def logits_kernel(own_ref, other_ref, w_ref, *refs):
    lt_ref, stats_ref, out_ref, hidden, buffer, staged, sems, out_sem = refs

    def assemble():
        n_v, n_pl, _, chunk = own_ref.shape
        core = lax.axis_index("co")
        staged[core] = own_ref[...].astype(F32)
        staged[1 - core] = other_ref[...].astype(F32)
        for v in range(n_v):
            groups = [staged[c, v, p] for p in range(n_pl) for c in range(2)]
            block = jnp.concatenate(groups, axis=0)
            hidden[:, v * chunk : (v + 1) * chunk] = block.astype(BF16)

    def compute(here):
        lt_ref[:, here] = lax.dot_general(
            hidden[...], buffer[here, :], (((1,), (1,)), ((), ())), preferred_element_type=F32
        )

    stream(w_ref, buffer, sems, LOGIT_TILE, 3, compute, assemble)
    keep = pltpu.make_async_copy(hidden, out_ref, out_sem)
    keep.start()
    values = lt_ref[...]
    top = jnp.max(values, axis=1, keepdims=True)
    total = jnp.sum(jnp.exp(values - top), axis=1, keepdims=True)
    stats_ref[...] = jnp.concatenate([top, total], axis=1)
    keep.wait()


def student_logits(own, other, weight):
    rows, width = weight.shape
    n_v, n_pl, group, _ = own.shape
    tokens = 2 * n_pl * group
    anywhere = pl.BlockSpec(memory_space=pl.ANY)
    return pl.pallas_call(
        logits_kernel,
        in_specs=[*in_vmem(2), anywhere],
        out_specs=[*in_vmem(2), anywhere],
        out_shape=[
            jax.ShapeDtypeStruct((tokens, rows), F32),
            jax.ShapeDtypeStruct((tokens, 2), F32),
            pltpu.HBM((tokens, width), BF16),
        ],
        scratch_shapes=[
            pltpu.VMEM((tokens, width), BF16),
            pltpu.VMEM((rows, width), BF16),
            pltpu.VMEM((2, *own.shape), F32),
            pltpu.SemaphoreType.DMA((rows // LOGIT_TILE + 1,)),
            pltpu.SemaphoreType.DMA,
        ],
        compiler_params=params(46 * MIB),
        cost_estimate=pl.CostEstimate(
            flops=8 * rows * width * tokens, bytes_accessed=2 * rows * width, transcendentals=0
        ),
    )(own, other, weight)


def split_kernel(t_ref, out_ref, buffer, sem):
    load = pltpu.make_async_copy(t_ref, buffer, sem)
    load.start()
    load.wait()
    total, (count, _, cols) = buffer.shape[1], out_ref.shape
    for s in range(2):
        for d in range(count // 2):
            start = (s * (count // 2) + d) * cols
            low = start // LANES * LANES
            high = min(-(-(start + cols) // LANES) * LANES, total)
            values = buffer[:, low:high].astype(F32)
            out_ref[d * 2 + s] = values[:, start - low : start - low + cols].astype(BF16)


def split_teacher(piece, n_dp):
    half, total = piece.shape
    return pl.pallas_call(
        split_kernel,
        in_specs=[pl.BlockSpec(memory_space=pl.ANY)],
        out_specs=pl.BlockSpec(memory_space=pltpu.VMEM),
        out_shape=pltpu.HBM((2 * n_dp, half, total // (2 * n_dp)), BF16),
        scratch_shapes=[pltpu.VMEM(piece.shape, BF16), pltpu.SemaphoreType.DMA],
        compiler_params=params(8 * MIB),
    )(pltpu.with_memory_space_constraint(piece, pltpu.HBM))


def message_kernel(t_ref, s_ref, stats_ref, share_ref, message_ref):
    values = jnp.concatenate([t_ref[j].astype(F32) for j in range(t_ref.shape[0])], axis=0)
    tokens = values.shape[0]
    top = jnp.max(values, axis=1, keepdims=True)
    weights = jnp.exp(values - top)
    total = jnp.sum(weights, axis=1, keepdims=True)
    share_ref[...] = weights * (1.0 / total)
    row = lax.broadcasted_iota(jnp.int32, (tokens, tokens), 0)
    col = lax.broadcasted_iota(jnp.int32, (tokens, tokens), 1)
    flip = lambda c: jnp.sum(jnp.where(row == col, c, 0.0), axis=0, keepdims=True)
    columns = [s_ref[:, 0:1], s_ref[:, 1:2], top, total]
    stats = jnp.concatenate([*map(flip, columns), jnp.zeros((4, tokens), F32)], axis=0)
    stats_ref[...] = stats
    lanes = message_ref.shape[2]
    if lanes > tokens:
        stats = jnp.concatenate([stats, jnp.zeros((8, lanes - tokens), F32)], axis=1)
    for k in range(message_ref.shape[0]):
        message_ref[k] = stats


def stats_message(teacher, s_stats, count):
    tokens, cols = s_stats.shape[0], teacher.shape[2]
    lanes = -(-tokens // LANES) * LANES
    return pl.pallas_call(
        message_kernel,
        in_specs=in_vmem(2),
        out_specs=in_vmem(3),
        out_shape=[
            jax.ShapeDtypeStruct((8, tokens), F32),
            jax.ShapeDtypeStruct((tokens, cols), F32),
            pltpu.HBM((count, 8, lanes), F32),
        ],
        compiler_params=params(12 * MIB),
    )(teacher, s_stats)


def products_kernel(t_ref, lt_ref, stats_ref, w_ref, u_ref, both_ref, *refs):
    buffer, packed, both, sems, both_sem = refs
    keep = pltpu.make_async_copy(both, both_ref, both_sem)
    tokens = t_ref.shape[0]

    def prepare():
        teach = t_ref[...]
        share = jnp.exp(lt_ref[...] - stats_ref[:, 0:1]) * (1.0 / stats_ref[:, 1:2])
        packed[:tokens, :] = (share - teach).astype(BF16)
        packed[tokens:, :] = teach.astype(BF16)
        both[...] = jnp.concatenate([share, teach], axis=0).T
        keep.start()
        u_ref[...] = jnp.zeros_like(u_ref)

    def compute(here):
        width = u_ref.shape[1]
        block = column_tile(width, 512)
        for k in range(0, width, block):
            cols = slice(k, k + block)
            u_ref[:, cols] += jnp.dot(
                packed[:, here], buffer[here, cols], preferred_element_type=F32
            )

    stream(w_ref, buffer, sems, PRODUCT_TILE, 2, compute, prepare)
    keep.wait()


def local_products(weight, teacher, lt, stats):
    rows, width = weight.shape
    tokens = lt.shape[0]
    anywhere = pl.BlockSpec(memory_space=pl.ANY)
    return pl.pallas_call(
        products_kernel,
        in_specs=[*in_vmem(3), anywhere],
        out_specs=[*in_vmem(1), anywhere],
        out_shape=[
            jax.ShapeDtypeStruct((2 * tokens, width), F32),
            pltpu.HBM((rows, 2 * tokens), F32),
        ],
        scratch_shapes=[
            pltpu.VMEM((rows, width), BF16),
            pltpu.VMEM((2 * tokens, rows), BF16),
            pltpu.VMEM((rows, 2 * tokens), F32),
            pltpu.SemaphoreType.DMA((rows // PRODUCT_TILE + 1,)),
            pltpu.SemaphoreType.DMA,
        ],
        compiler_params=params(46 * MIB),
        cost_estimate=pl.CostEstimate(
            flops=8 * rows * width * tokens, bytes_accessed=2 * rows * width, transcendentals=0
        ),
    )(teacher, lt, stats, weight)


def combine_kernel(all_ref, mine_ref, u_ref, hp_ref, mass_ref):
    tokens = mine_ref.shape[1]

    def mass(k):
        top_all = all_ref[:, k, :tokens]
        top = jnp.max(top_all, axis=0, keepdims=True)
        total = jnp.sum(jnp.exp(top_all - top) * all_ref[:, k + 1, :tokens], axis=0, keepdims=True)
        return jnp.exp(mine_ref[k : k + 1, :] - top) * mine_ref[k + 1 : k + 2, :] / total

    student, teacher = mass(0), mass(2)
    mass_ref[...] = GRAD_SCALE * jnp.concatenate([student, teacher], axis=1)
    row = lax.broadcasted_iota(jnp.int32, (tokens, tokens), 0)
    col = lax.broadcasted_iota(jnp.int32, (tokens, tokens), 1)
    flip = lambda r: jnp.sum(jnp.where(row == col, r, 0.0), axis=1, keepdims=True)
    scale_x = GRAD_SCALE * flip(student)
    scale_t = GRAD_SCALE * flip(student - teacher)
    width = hp_ref.shape[2]
    for v in range(hp_ref.shape[0]):
        cols = slice(v * width, (v + 1) * width)
        hp_ref[v] = (u_ref[:tokens, cols] * scale_x + u_ref[tokens:, cols] * scale_t).astype(BF16)


def combine(stats_all, stats, products, n_v):
    tokens = stats.shape[1]
    width = products.shape[1] // n_v
    return pl.pallas_call(
        combine_kernel,
        in_specs=in_vmem(3),
        out_specs=in_vmem(2),
        out_shape=[
            pltpu.HBM((n_v, tokens, width), BF16),
            jax.ShapeDtypeStruct((1, 2 * tokens), F32),
        ],
        compiler_params=params(12 * MIB),
    )(stats_all, stats, products)


def head_blocks(width):
    first = column_tile(width, 512)
    rest = column_tile(width - first, 1024)
    return [(0, first)] + [(k, rest) for k in range(first, width, rest)]


def head_kernel(tile, both_ref, mass_ref, hidden_ref, out_ref, both, hidden, result, sems, out_sems):
    rows = both_ref.shape[0]
    tokens, width = hidden_ref.shape
    steps = rows // tile
    load_hidden = pltpu.make_async_copy(hidden_ref, hidden, sems.at[steps])

    def load(step):
        here = tile_rows(step, tile, rows)
        return pltpu.make_async_copy(both_ref.at[here, :], both.at[here, :], sems.at[step])

    def store(step, block, start, size):
        here, cols = tile_rows(step, tile, rows), slice(start, start + size)
        return pltpu.make_async_copy(
            result.at[here, cols], out_ref.at[here, cols], out_sems.at[step, block]
        )

    load(0).start()
    load_hidden.start()
    for step in range(1, steps):
        load(step).start()
    load_hidden.wait()

    def body(step, carry):
        load(step).wait()
        here = tile_rows(step, tile, rows)
        scaled = both[here, :] * mass_ref[...]
        grad = (scaled[:, :tokens] - scaled[:, tokens:]).astype(BF16)
        for block, (start, size) in enumerate(head_blocks(width)):
            inner = column_tile(size, 256)
            for k in range(start, start + size, inner):
                result[here, k : k + inner] = jnp.dot(
                    grad, hidden[:, k : k + inner], preferred_element_type=F32
                ).astype(BF16)
            store(step, block, start, size).start()
        return carry

    lax.fori_loop(0, steps, body, 0)
    for step in range(steps):
        for block, (start, size) in enumerate(head_blocks(width)):
            store(step, block, start, size).wait()


def head_gradient(both, mass, hidden):
    rows = both.shape[0]
    tokens, width = hidden.shape
    tile = row_tile(rows, 1584)
    steps = rows // tile
    anywhere = pl.BlockSpec(memory_space=pl.ANY)
    in_hbm = lambda x: pltpu.with_memory_space_constraint(x, pltpu.HBM)
    return pl.pallas_call(
        functools.partial(head_kernel, tile),
        in_specs=[anywhere, *in_vmem(1), anywhere],
        out_specs=anywhere,
        out_shape=jax.ShapeDtypeStruct((rows, width), BF16),
        scratch_shapes=[
            pltpu.VMEM((rows, 2 * tokens), F32),
            pltpu.VMEM((tokens, width), BF16),
            pltpu.VMEM((rows, width), BF16),
            pltpu.SemaphoreType.DMA((steps + 1,)),
            pltpu.SemaphoreType.DMA((steps, len(head_blocks(width)))),
        ],
        compiler_params=params(46 * MIB),
        cost_estimate=pl.CostEstimate(
            flops=8 * rows * width * tokens, bytes_accessed=2 * rows * width, transcendentals=0
        ),
    )(in_hbm(both), mass, in_hbm(hidden))


def exchange(parts, axes):
    return lax.all_to_all(parts, axes, split_axis=0, concat_axis=0, tiled=True)


def shards(n_dp, n_v, hidden, head_weight, teacher_logits):
    everyone = ("vk", "vs", "pl", "co")
    n_pl = n_dp // 2
    count = n_dp * n_v
    group, width = hidden.shape
    weight = head_weight[0]

    own = exchange(copies(hidden, n_v * n_pl), ("vk", "vs", "pl"))
    sends = split_teacher(teacher_logits[0], n_dp)
    sends, own = lax.optimization_barrier((sends, own))
    other = lax.ppermute(own, "co", [(0, 1), (1, 0)])
    teacher = exchange(sends, ("pl", "co", "vs"))
    square = (n_v, n_pl, group, width)

    lt, s_stats, every_row = student_logits(own.reshape(square), other.reshape(square), weight)
    stats, shares, message = stats_message(teacher, s_stats, count)
    stats_all = exchange(message, everyone)
    products, both = local_products(weight, shares, lt, s_stats)
    partial_value, mass = combine(stats_all, stats, products, n_v)
    pieces = exchange(partial_value.reshape(count, group, width), everyone)
    head_grad = head_gradient(both, mass, every_row)
    hidden_grad = jnp.sum(pieces.astype(F32), axis=0).astype(BF16)
    return hidden_grad, head_grad[None]


def solution(mesh):
    n_dp, n_v = mesh.shape["dp"], mesh.shape["vocab"]
    split = Mesh(mesh.devices.reshape(n_dp // 2, 2, n_v // 2, 2), ("pl", "co", "vk", "vs"))
    dp, vocab = ("pl", "co"), ("vk", "vs")
    return jax.shard_map(
        functools.partial(shards, n_dp, n_v),
        mesh=split,
        in_specs=(P(dp, vocab), P(vocab, dp, None), P(vocab, dp, None)),
        out_specs=(P(dp, vocab), P(vocab, dp, None)),
        check_vma=False,
    )
```

```python
import functools

import jax
import jax.numpy as jnp
from jax import lax
from jax.experimental import pallas as pl
from jax.experimental.pallas import tpu as pltpu
from jax.sharding import Mesh
from jax.sharding import PartitionSpec as P

GRAD_SCALE = 32.0
F32 = jnp.float32
BF16 = jnp.bfloat16
MIB = 2**20
LANES = 128
LOGIT_TILE = 512
PRODUCT_TILE = 1024


def row_tile(rows, limit):
    best = rows
    for tile in range(16, limit + 1, 16):
        if rows % tile == 0:
            best = tile
    return best


def column_tile(width, limit):
    return max(c for c in range(LANES, limit + 1, LANES) if width % c == 0)


def tile_rows(step, tile, rows):
    if tile == rows:
        return slice(None)
    return pl.ds(pl.multiple_of(step * tile, tile), tile)


def params(limit):
    return pltpu.CompilerParams(vmem_limit_bytes=limit)


def whole(shape):
    return pl.BlockSpec(shape, lambda *_: (0,) * len(shape))


def in_vmem(count):
    return [pl.BlockSpec(memory_space=pltpu.VMEM)] * count


def stream(w_ref, buffer, sems, first, tile, ahead, compute, between):
    rows = w_ref.shape[0]
    if rows < first + tile:
        first = 0
    steps = (rows - first) // tile
    begin, last = slice(0, first), slice(first + steps * tile, rows)
    rest = rows - last.start

    def copy(here, sem):
        return pltpu.make_async_copy(w_ref.at[here, :], buffer.at[here, :], sem)

    def place(step):
        return pl.ds(pl.multiple_of(first + step * tile, LANES), tile)

    ahead = min(ahead, steps)
    if first:
        copy(begin, sems.at[steps + 1]).start()
    for step in range(ahead):
        copy(place(step), sems.at[step]).start()
    if rest and ahead == steps:
        copy(last, sems.at[steps]).start()
    between()
    if first:
        copy(begin, sems.at[steps + 1]).wait()
        compute(begin)

    def body(step, carry):
        @pl.when(step + ahead < steps)
        def _():
            copy(place(step + ahead), sems.at[step + ahead]).start()

        if rest and ahead < steps:

            @pl.when(step + ahead == steps)
            def _():
                copy(last, sems.at[steps]).start()

        copy(place(step), sems.at[step]).wait()
        compute(place(step))
        return carry

    if steps:
        lax.fori_loop(0, steps, body, 0)
    if rest:
        copy(last, sems.at[steps]).wait()
        compute(last)


def logits_kernel(own_ref, other_ref, w_ref, *refs):
    lt_out, stats_ref, out_ref, lt_ref, hidden, buffer, staged, sems, out_sems = refs

    def assemble():
        n_pl, n_v, _, chunk = own_ref.shape
        core, plane = lax.axis_index("co"), lax.axis_index("pl")
        shard = lax.axis_index("vk") * 2 + lax.axis_index("vs")
        staged[core] = own_ref[...].astype(F32)
        staged[1 - core] = other_ref[...].astype(F32)
        for v in range(n_v):
            groups = [staged[c, p ^ plane, v ^ shard] for p in range(n_pl) for c in range(2)]
            block = jnp.concatenate(groups, axis=0)
            hidden[:, v * chunk : (v + 1) * chunk] = block.astype(BF16)

    def compute(here):
        lt_ref[:, here] = lax.dot_general(
            hidden[...], buffer[here, :], (((1,), (1,)), ((), ())), preferred_element_type=F32
        )

    stream(w_ref, buffer, sems, 0, LOGIT_TILE, 3, compute, assemble)
    keep = [
        pltpu.make_async_copy(lt_ref, lt_out, out_sems.at[0]),
        pltpu.make_async_copy(hidden, out_ref, out_sems.at[1]),
    ]
    for copy in keep:
        copy.start()
    values = lt_ref[...]
    top = jnp.max(values, axis=1, keepdims=True)
    total = jnp.sum(jnp.exp(values - top), axis=1, keepdims=True)
    stats_ref[...] = jnp.concatenate([top, total], axis=1)
    for copy in keep:
        copy.wait()


def student_logits(own, other, weight):
    rows, width = weight.shape
    n_pl, n_v, group, _ = own.shape
    tokens = 2 * n_pl * group
    anywhere = pl.BlockSpec(memory_space=pl.ANY)
    return pl.pallas_call(
        logits_kernel,
        in_specs=[*in_vmem(2), anywhere],
        out_specs=[anywhere, *in_vmem(1), anywhere],
        out_shape=[
            pltpu.HBM((tokens, rows), F32),
            jax.ShapeDtypeStruct((tokens, 2), F32),
            pltpu.HBM((tokens, width), BF16),
        ],
        scratch_shapes=[
            pltpu.VMEM((tokens, rows), F32),
            pltpu.VMEM((tokens, width), BF16),
            pltpu.VMEM((rows, width), BF16),
            pltpu.VMEM((2, *own.shape), F32),
            pltpu.SemaphoreType.DMA((rows // LOGIT_TILE + 2,)),
            pltpu.SemaphoreType.DMA((2,)),
        ],
        compiler_params=params(46 * MIB),
        cost_estimate=pl.CostEstimate(
            flops=8 * rows * width * tokens, bytes_accessed=2 * rows * width, transcendentals=0
        ),
    )(own, other, weight)


def split_kernel(t_ref, out_ref, buffer, sem):
    load = pltpu.make_async_copy(t_ref, buffer, sem)
    load.start()
    load.wait()
    total, (count, _, cols) = buffer.shape[1], out_ref.shape
    for s in range(2):
        for d in range(count // 2):
            start = (s * (count // 2) + d) * cols
            low = start // LANES * LANES
            high = min(-(-(start + cols) // LANES) * LANES, total)
            values = buffer[:, low:high].astype(F32)
            out_ref[d * 2 + s] = values[:, start - low : start - low + cols].astype(BF16)


def split_teacher(piece, n_dp):
    half, total = piece.shape
    return pl.pallas_call(
        split_kernel,
        in_specs=[pl.BlockSpec(memory_space=pl.ANY)],
        out_specs=pl.BlockSpec(memory_space=pltpu.VMEM),
        out_shape=pltpu.HBM((2 * n_dp, half, total // (2 * n_dp)), BF16),
        scratch_shapes=[pltpu.VMEM(piece.shape, BF16), pltpu.SemaphoreType.DMA],
        compiler_params=params(8 * MIB),
    )(pltpu.with_memory_space_constraint(piece, pltpu.HBM))


def teacher_values(t_ref):
    return jnp.concatenate([t_ref[j].astype(F32) for j in range(t_ref.shape[0])], axis=0)


def message_kernel(t_ref, s_ref, stats_ref, columns_ref, message_ref):
    values = teacher_values(t_ref)
    tokens = values.shape[0]
    top = jnp.max(values, axis=1, keepdims=True)
    total = jnp.sum(jnp.exp(values - top), axis=1, keepdims=True)
    row = lax.broadcasted_iota(jnp.int32, (tokens, tokens), 0)
    col = lax.broadcasted_iota(jnp.int32, (tokens, tokens), 1)
    flip = lambda c: jnp.sum(jnp.where(row == col, c, 0.0), axis=0, keepdims=True)
    columns = [s_ref[:, 0:1], s_ref[:, 1:2], top, total]
    columns_ref[...] = jnp.concatenate(columns, axis=1)
    stats = jnp.concatenate([*map(flip, columns), jnp.zeros((4, tokens), F32)], axis=0)
    stats_ref[...] = stats
    lanes = message_ref.shape[2]
    if lanes > tokens:
        stats = jnp.concatenate([stats, jnp.zeros((8, lanes - tokens), F32)], axis=1)
    for k in range(message_ref.shape[0]):
        message_ref[k] = stats


def stats_message(teacher, s_stats, count):
    tokens = s_stats.shape[0]
    lanes = -(-tokens // LANES) * LANES
    return pl.pallas_call(
        message_kernel,
        in_specs=in_vmem(2),
        out_specs=in_vmem(3),
        out_shape=[
            jax.ShapeDtypeStruct((8, tokens), F32),
            jax.ShapeDtypeStruct((tokens, 4), F32),
            pltpu.HBM((count, 8, lanes), F32),
        ],
        compiler_params=params(12 * MIB),
    )(teacher, s_stats)


def products_kernel(t_ref, lt_in, stats_ref, w_ref, u_ref, both_ref, *refs):
    lt_ref, buffer, packed, both, sems, own_sems = refs
    load = pltpu.make_async_copy(lt_in, lt_ref, own_sems.at[0])
    keep = pltpu.make_async_copy(both, both_ref, own_sems.at[1])
    tokens = stats_ref.shape[0]
    load.start()

    def prepare():
        values = teacher_values(t_ref)
        teach = jnp.exp(values - stats_ref[:, 2:3]) * (1.0 / stats_ref[:, 3:4])
        load.wait()
        share = jnp.exp(lt_ref[...] - stats_ref[:, 0:1]) * (1.0 / stats_ref[:, 1:2])
        packed[:tokens, :] = (share - teach).astype(BF16)
        packed[tokens:, :] = teach.astype(BF16)
        both[...] = jnp.concatenate([share, teach], axis=0).T
        keep.start()
        u_ref[...] = jnp.zeros_like(u_ref)

    def compute(here):
        width = u_ref.shape[1]
        block = column_tile(width, 512)
        for k in range(0, width, block):
            cols = slice(k, k + block)
            u_ref[:, cols] += jnp.dot(
                packed[:, here], buffer[here, cols], preferred_element_type=F32
            )

    stream(w_ref, buffer, sems, 512, PRODUCT_TILE, 2, compute, prepare)
    keep.wait()


def local_products(weight, teacher, lt, stats):
    rows, width = weight.shape
    tokens = lt.shape[0]
    anywhere = pl.BlockSpec(memory_space=pl.ANY)
    return pl.pallas_call(
        products_kernel,
        in_specs=[*in_vmem(1), anywhere, *in_vmem(1), anywhere],
        out_specs=[*in_vmem(1), anywhere],
        out_shape=[
            jax.ShapeDtypeStruct((2 * tokens, width), F32),
            pltpu.HBM((rows, 2 * tokens), F32),
        ],
        scratch_shapes=[
            pltpu.VMEM((tokens, rows), F32),
            pltpu.VMEM((rows, width), BF16),
            pltpu.VMEM((2 * tokens, rows), BF16),
            pltpu.VMEM((rows, 2 * tokens), F32),
            pltpu.SemaphoreType.DMA((rows // PRODUCT_TILE + 2,)),
            pltpu.SemaphoreType.DMA((2,)),
        ],
        compiler_params=params(46 * MIB),
        cost_estimate=pl.CostEstimate(
            flops=8 * rows * width * tokens, bytes_accessed=2 * rows * width, transcendentals=0
        ),
    )(teacher, pltpu.with_memory_space_constraint(lt, pltpu.HBM), stats, weight)


def combine_kernel(all_ref, mine_ref, u_ref, hp_ref, mass_ref):
    tokens = mine_ref.shape[1]

    def mass(k):
        top_all = all_ref[:, k, :tokens]
        top = jnp.max(top_all, axis=0, keepdims=True)
        total = jnp.sum(jnp.exp(top_all - top) * all_ref[:, k + 1, :tokens], axis=0, keepdims=True)
        return jnp.exp(mine_ref[k : k + 1, :] - top) * mine_ref[k + 1 : k + 2, :] / total

    student, teacher = mass(0), mass(2)
    mass_ref[...] = GRAD_SCALE * jnp.concatenate([student, teacher], axis=1)
    row = lax.broadcasted_iota(jnp.int32, (tokens, tokens), 0)
    col = lax.broadcasted_iota(jnp.int32, (tokens, tokens), 1)
    flip = lambda r: jnp.sum(jnp.where(row == col, r, 0.0), axis=1, keepdims=True)
    scale_x = GRAD_SCALE * flip(student)
    scale_t = GRAD_SCALE * flip(student - teacher)
    width = hp_ref.shape[2]
    for v in range(hp_ref.shape[0]):
        cols = slice(v * width, (v + 1) * width)
        hp_ref[v] = (u_ref[:tokens, cols] * scale_x + u_ref[tokens:, cols] * scale_t).astype(BF16)


def combine(stats_all, stats, products, n_v):
    tokens = stats.shape[1]
    width = products.shape[1] // n_v
    return pl.pallas_call(
        combine_kernel,
        in_specs=in_vmem(3),
        out_specs=in_vmem(2),
        out_shape=[
            pltpu.HBM((n_v, tokens, width), BF16),
            jax.ShapeDtypeStruct((1, 2 * tokens), F32),
        ],
        compiler_params=params(12 * MIB),
    )(stats_all, stats, products)


def head_blocks(width):
    first = column_tile(width, 512)
    rest = column_tile(width - first, 1024)
    return [(0, first)] + [(k, rest) for k in range(first, width, rest)]


def head_kernel(tile, both_ref, mass_ref, hidden_ref, out_ref, both, hidden, result, sems, out_sems):
    rows = both_ref.shape[0]
    tokens, width = hidden_ref.shape
    steps = rows // tile
    load_hidden = pltpu.make_async_copy(hidden_ref, hidden, sems.at[steps])

    def load(step):
        here = tile_rows(step, tile, rows)
        return pltpu.make_async_copy(both_ref.at[here, :], both.at[here, :], sems.at[step])

    def store(step, block, start, size):
        here, cols = tile_rows(step, tile, rows), slice(start, start + size)
        return pltpu.make_async_copy(
            result.at[here, cols], out_ref.at[here, cols], out_sems.at[step, block]
        )

    load(0).start()
    load_hidden.start()
    for step in range(1, steps):
        load(step).start()
    load_hidden.wait()

    def body(step, carry):
        load(step).wait()
        here = tile_rows(step, tile, rows)
        scaled = both[here, :] * mass_ref[...]
        grad = (scaled[:, :tokens] - scaled[:, tokens:]).astype(BF16)
        for block, (start, size) in enumerate(head_blocks(width)):
            inner = column_tile(size, 256)
            for k in range(start, start + size, inner):
                result[here, k : k + inner] = jnp.dot(
                    grad, hidden[:, k : k + inner], preferred_element_type=F32
                ).astype(BF16)
            store(step, block, start, size).start()
        return carry

    lax.fori_loop(0, steps, body, 0)
    for step in range(steps):
        for block, (start, size) in enumerate(head_blocks(width)):
            store(step, block, start, size).wait()


def head_gradient(both, mass, hidden):
    rows = both.shape[0]
    tokens, width = hidden.shape
    tile = row_tile(rows, 1584)
    steps = rows // tile
    anywhere = pl.BlockSpec(memory_space=pl.ANY)
    in_hbm = lambda x: pltpu.with_memory_space_constraint(x, pltpu.HBM)
    return pl.pallas_call(
        functools.partial(head_kernel, tile),
        in_specs=[anywhere, *in_vmem(1), anywhere],
        out_specs=anywhere,
        out_shape=jax.ShapeDtypeStruct((rows, width), BF16),
        scratch_shapes=[
            pltpu.VMEM((rows, 2 * tokens), F32),
            pltpu.VMEM((tokens, width), BF16),
            pltpu.VMEM((rows, width), BF16),
            pltpu.SemaphoreType.DMA((steps + 1,)),
            pltpu.SemaphoreType.DMA((steps, len(head_blocks(width)))),
        ],
        compiler_params=params(46 * MIB),
        cost_estimate=pl.CostEstimate(
            flops=8 * rows * width * tokens, bytes_accessed=2 * rows * width, transcendentals=0
        ),
    )(in_hbm(both), mass, in_hbm(hidden))


def exchange(parts, axes):
    return lax.all_to_all(parts, axes, split_axis=0, concat_axis=0, tiled=True)


def partners(value, axes, size):
    got = [value]
    for s in range(1, size):
        got.append(lax.ppermute(value, axes, [(i, i ^ s) for i in range(size)]))
    return got


def shards(n_dp, n_v, hidden, head_weight, teacher_logits):
    everyone = ("vk", "vs", "pl", "co")
    n_pl = n_dp // 2
    count = n_dp * n_v
    group, width = hidden.shape
    weight = head_weight[0]

    columns = jnp.stack(partners(hidden, ("vk", "vs"), n_v))
    own = jnp.stack(partners(columns, "pl", n_pl))
    sends = split_teacher(teacher_logits[0], n_dp)
    sends, own = lax.optimization_barrier((sends, own))
    other = lax.ppermute(own, "co", [(0, 1), (1, 0)])
    teacher = exchange(sends, ("pl", "co", "vs"))

    lt, s_stats, every_row = student_logits(own, other, weight)
    stats, own_stats, message = stats_message(teacher, s_stats, count)
    stats_all = exchange(message, everyone)
    products, both = local_products(weight, teacher, lt, own_stats)
    partial_value, mass = combine(stats_all, stats, products, n_v)
    pieces = exchange(partial_value.reshape(count, group, width), everyone)
    head_grad = head_gradient(both, mass, every_row)
    hidden_grad = jnp.sum(pieces.astype(F32), axis=0).astype(BF16)
    return hidden_grad, head_grad[None]


def solution(mesh):
    n_dp, n_v = mesh.shape["dp"], mesh.shape["vocab"]
    split = Mesh(mesh.devices.reshape(n_dp // 2, 2, n_v // 2, 2), ("pl", "co", "vk", "vs"))
    dp, vocab = ("pl", "co"), ("vk", "vs")
    return jax.shard_map(
        functools.partial(shards, n_dp, n_v),
        mesh=split,
        in_specs=(P(dp, vocab), P(vocab, dp, None), P(vocab, dp, None)),
        out_specs=(P(dp, vocab), P(vocab, dp, None)),
        check_vma=False,
    )
```

```python
import functools

import jax
import jax.numpy as jnp
from jax import lax
from jax.experimental import pallas as pl
from jax.experimental.pallas import tpu as pltpu
from jax.sharding import Mesh
from jax.sharding import PartitionSpec as P

GRAD_SCALE = 32.0
F32 = jnp.float32
BF16 = jnp.bfloat16
MIB = 2**20
LANES = 128
LOWEST = -1e30
LOGIT_TILE = 512
PRODUCT_TILE = 1024


def row_tile(rows, limit):
    best = rows
    for tile in range(16, limit + 1, 16):
        if rows % tile == 0:
            best = tile
    return best


def column_tile(width, limit):
    return max(c for c in range(LANES, limit + 1, LANES) if width % c == 0)


def tile_rows(step, tile, rows):
    if tile == rows:
        return slice(None)
    return pl.ds(pl.multiple_of(step * tile, tile), tile)


def params(limit):
    return pltpu.CompilerParams(vmem_limit_bytes=limit)


def whole(shape):
    return pl.BlockSpec(shape, lambda *_: (0,) * len(shape))


def in_vmem(count):
    return [pl.BlockSpec(memory_space=pltpu.VMEM)] * count


def stream(w_ref, buffer, sems, first, tile, ahead, compute, between):
    rows = w_ref.shape[0]
    if rows < first + tile:
        first = 0
    steps = (rows - first) // tile
    begin, last = slice(0, first), slice(first + steps * tile, rows)
    rest = rows - last.start

    def copy(here, sem):
        return pltpu.make_async_copy(w_ref.at[here, :], buffer.at[here, :], sem)

    def place(step):
        return pl.ds(pl.multiple_of(first + step * tile, LANES), tile)

    ahead = min(ahead, steps)
    if first:
        copy(begin, sems.at[steps + 1]).start()
    for step in range(ahead):
        copy(place(step), sems.at[step]).start()
    if rest and ahead == steps:
        copy(last, sems.at[steps]).start()
    between()
    if first:
        copy(begin, sems.at[steps + 1]).wait()
        compute(begin, steps + 1)

    def body(step, carry):
        @pl.when(step + ahead < steps)
        def _():
            copy(place(step + ahead), sems.at[step + ahead]).start()

        if rest and ahead < steps:

            @pl.when(step + ahead == steps)
            def _():
                copy(last, sems.at[steps]).start()

        copy(place(step), sems.at[step]).wait()
        compute(place(step), step)
        return carry

    if steps:
        lax.fori_loop(0, steps, body, 0)
    if rest:
        copy(last, sems.at[steps]).wait()
        compute(last, steps)
    chunks = [(k, slice(first + k * tile, first + (k + 1) * tile)) for k in range(steps)]
    return chunks + [(steps, last)] * bool(rest) + [(steps + 1, begin)] * bool(first)


def turn(column):
    size = column.shape[0]
    row = lax.broadcasted_iota(jnp.int32, (size, size), 0)
    col = lax.broadcasted_iota(jnp.int32, (size, size), 1)
    return jnp.sum(jnp.where(row == col, column, 0.0), axis=0, keepdims=True)


def turn_back(line):
    size = line.shape[1]
    row = lax.broadcasted_iota(jnp.int32, (size, size), 0)
    col = lax.broadcasted_iota(jnp.int32, (size, size), 1)
    return jnp.sum(jnp.where(row == col, line, 0.0), axis=1, keepdims=True)


def logits_kernel(own_ref, other_ref, t_stats_ref, w_ref, *refs):
    stats_ref, lt_out, out_ref, message_ref, *scratch = refs
    lt_ref, hidden, buffer, staged, sems, lt_sems, out_sem = scratch
    keep = pltpu.make_async_copy(hidden, out_ref, out_sem)

    def assemble():
        n_v, n_pl, _, chunk = own_ref.shape
        core = lax.axis_index("co")
        staged[core] = own_ref[...].astype(F32)
        staged[1 - core] = other_ref[...].astype(F32)
        for v in range(n_v):
            groups = [staged[c, v, p] for p in range(n_pl) for c in range(2)]
            block = jnp.concatenate(groups, axis=0)
            hidden[:, v * chunk : (v + 1) * chunk] = block.astype(BF16)
        keep.start()

    def send(here, index):
        return pltpu.make_async_copy(lt_ref.at[:, here], lt_out.at[:, here], lt_sems.at[index])

    def compute(here, index):
        lt_ref[:, here] = lax.dot_general(
            hidden[...], buffer[here, :], (((1,), (1,)), ((), ())), preferred_element_type=F32
        )
        send(here, index).start()

    chunks = stream(w_ref, buffer, sems, 0, LOGIT_TILE, 3, compute, assemble)
    values = lt_ref[...]
    top = jnp.max(values, axis=1, keepdims=True)
    total = jnp.sum(jnp.exp(values - top), axis=1, keepdims=True)
    stats_ref[...] = jnp.concatenate([top, total], axis=1)
    lines = jnp.concatenate([turn(top), turn(total)], axis=0)
    lanes = t_stats_ref.shape[1]
    if lanes > lines.shape[1]:
        lines = jnp.concatenate([lines, jnp.zeros((2, lanes - lines.shape[1]), F32)], axis=1)
    message = jnp.concatenate([lines, t_stats_ref[...], jnp.zeros((4, lanes), F32)], axis=0)
    for k in range(message_ref.shape[0]):
        message_ref[k] = message
    keep.wait()
    for index, here in chunks:
        send(here, index).wait()


def student_logits(own, other, t_stats, weight, count):
    rows, width = weight.shape
    n_v, n_pl, group, _ = own.shape
    tokens = 2 * n_pl * group
    anywhere = pl.BlockSpec(memory_space=pl.ANY)
    return pl.pallas_call(
        logits_kernel,
        in_specs=[*in_vmem(3), anywhere],
        out_specs=[*in_vmem(1), anywhere, anywhere, *in_vmem(1)],
        out_shape=[
            jax.ShapeDtypeStruct((tokens, 2), F32),
            pltpu.HBM((tokens, rows), F32),
            pltpu.HBM((tokens, width), BF16),
            pltpu.HBM((count, 8, t_stats.shape[1]), F32),
        ],
        scratch_shapes=[
            pltpu.VMEM((tokens, rows), F32),
            pltpu.VMEM((tokens, width), BF16),
            pltpu.VMEM((rows, width), BF16),
            pltpu.VMEM((2, *own.shape), F32),
            pltpu.SemaphoreType.DMA((rows // LOGIT_TILE + 2,)),
            pltpu.SemaphoreType.DMA((rows // LOGIT_TILE + 2,)),
            pltpu.SemaphoreType.DMA,
        ],
        compiler_params=params(46 * MIB),
        cost_estimate=pl.CostEstimate(
            flops=8 * rows * width * tokens, bytes_accessed=2 * rows * width, transcendentals=0
        ),
    )(own, other, t_stats, weight)


def copies_kernel(h_ref, out_ref, sems):
    sends = [
        pltpu.make_async_copy(h_ref, out_ref.at[k], sems.at[k]) for k in range(out_ref.shape[0])
    ]
    for send in sends:
        send.start()
    for send in sends:
        send.wait()


def copies(hidden, count):
    anywhere = pl.BlockSpec(memory_space=pl.ANY)
    return pl.pallas_call(
        copies_kernel,
        in_specs=[anywhere],
        out_specs=anywhere,
        out_shape=pltpu.HBM((count, *hidden.shape), BF16),
        scratch_shapes=[pltpu.SemaphoreType.DMA((count,))],
        compiler_params=params(4 * MIB),
    )(pltpu.with_memory_space_constraint(hidden, pltpu.HBM))


def pass_kernel(value_ref, other_ref, out_ref):
    pass


def after(value, other):
    anywhere = pl.BlockSpec(memory_space=pl.ANY)
    return pl.pallas_call(
        pass_kernel,
        in_specs=[anywhere] * 2,
        out_specs=anywhere,
        out_shape=pltpu.HBM(value.shape, value.dtype),
        input_output_aliases={0: 0},
        compiler_params=params(MIB),
        cost_estimate=pl.CostEstimate(flops=1, bytes_accessed=1, transcendentals=0),
    )(pltpu.with_memory_space_constraint(value, pltpu.HBM), other)


def split_kernel(t_ref, out_ref, stats_ref, buffer, sem):
    load = pltpu.make_async_copy(t_ref, buffer, sem)
    load.start()
    load.wait()
    total, (count, _, cols) = buffer.shape[1], out_ref.shape
    for s in range(2):
        for d in range(count // 2):
            start = (s * (count // 2) + d) * cols
            low = start // LANES * LANES
            high = min(-(-(start + cols) // LANES) * LANES, total)
            values = buffer[:, low:high].astype(F32)
            out_ref[d * 2 + s] = values[:, start - low : start - low + cols].astype(BF16)
    values = buffer[...].astype(F32)
    half, lanes = values.shape[0], stats_ref.shape[1]
    top = jnp.max(values, axis=1, keepdims=True)
    total = jnp.sum(jnp.exp(values - top), axis=1, keepdims=True)
    group = lax.axis_index("pl") * 2 + lax.axis_index("co")
    first = (group * 2 + lax.axis_index("vs")) * half
    row = lax.broadcasted_iota(jnp.int32, (half, lanes), 0)
    lane = lax.broadcasted_iota(jnp.int32, (half, lanes), 1)
    chosen = lane == first + row
    tops = jnp.max(jnp.where(chosen, top, LOWEST), axis=0, keepdims=True)
    totals = jnp.sum(jnp.where(chosen, total, 0.0), axis=0, keepdims=True)
    stats_ref[...] = jnp.concatenate([tops, totals], axis=0)


def split_teacher(piece, n_dp):
    half, total = piece.shape
    return pl.pallas_call(
        split_kernel,
        in_specs=[pl.BlockSpec(memory_space=pl.ANY)],
        out_specs=in_vmem(2),
        out_shape=[
            pltpu.HBM((2 * n_dp, half, total // (2 * n_dp)), BF16),
            pltpu.HBM((2, -(-2 * half * n_dp // LANES) * LANES), F32),
        ],
        scratch_shapes=[pltpu.VMEM(piece.shape, BF16), pltpu.SemaphoreType.DMA],
        compiler_params=params(8 * MIB),
    )(pltpu.with_memory_space_constraint(piece, pltpu.HBM))


def teacher_values(t_ref):
    return jnp.concatenate([t_ref[j].astype(F32) for j in range(t_ref.shape[0])], axis=0)


def products_kernel(t_ref, lt_in, stats_ref, w_ref, u_ref, t_stats_ref, shares_ref, *refs):
    lt_ref, buffer, packed, shares, sems, own_sems = refs
    load = pltpu.make_async_copy(lt_in, lt_ref, own_sems.at[0])
    keep = pltpu.make_async_copy(shares, shares_ref, own_sems.at[1])
    tokens = stats_ref.shape[0]
    load.start()

    def prepare():
        values = teacher_values(t_ref)
        top = jnp.max(values, axis=1, keepdims=True)
        weights = jnp.exp(values - top)
        total = jnp.sum(weights, axis=1, keepdims=True)
        t_stats_ref[...] = jnp.concatenate([top, total], axis=1)
        teach = weights * (1.0 / total)
        load.wait()
        share = jnp.exp(lt_ref[...] - stats_ref[:, 0:1]) * (1.0 / stats_ref[:, 1:2])
        shares[:tokens, :] = share
        shares[tokens:, :] = teach
        packed[:tokens, :] = (share - teach).astype(BF16)
        packed[tokens:, :] = teach.astype(BF16)
        keep.start()
        u_ref[...] = jnp.zeros_like(u_ref)

    def compute(here, index):
        width = u_ref.shape[1]
        block = column_tile(width, 512)
        for k in range(0, width, block):
            cols = slice(k, k + block)
            u_ref[:, cols] += jnp.dot(
                packed[:, here], buffer[here, cols], preferred_element_type=F32
            )

    stream(w_ref, buffer, sems, 512, PRODUCT_TILE, 2, compute, prepare)
    keep.wait()


def local_products(weight, teacher, lt, stats):
    rows, width = weight.shape
    tokens = lt.shape[0]
    anywhere = pl.BlockSpec(memory_space=pl.ANY)
    return pl.pallas_call(
        products_kernel,
        in_specs=[*in_vmem(1), anywhere, *in_vmem(1), anywhere],
        out_specs=[*in_vmem(2), anywhere],
        out_shape=[
            jax.ShapeDtypeStruct((2 * tokens, width), F32),
            jax.ShapeDtypeStruct((tokens, 2), F32),
            pltpu.HBM((2 * tokens, rows), F32),
        ],
        scratch_shapes=[
            pltpu.VMEM((tokens, rows), F32),
            pltpu.VMEM((rows, width), BF16),
            pltpu.VMEM((2 * tokens, rows), BF16),
            pltpu.VMEM((2 * tokens, rows), F32),
            pltpu.SemaphoreType.DMA((rows // PRODUCT_TILE + 2,)),
            pltpu.SemaphoreType.DMA((2,)),
        ],
        compiler_params=params(46 * MIB),
        cost_estimate=pl.CostEstimate(
            flops=8 * rows * width * tokens, bytes_accessed=2 * rows * width, transcendentals=0
        ),
    )(teacher, pltpu.with_memory_space_constraint(lt, pltpu.HBM), stats, weight)


def combine_kernel(all_ref, s_ref, t_ref, u_ref, hp_ref, mass_ref):
    tokens = s_ref.shape[0]

    def mass(k, mine_ref):
        top_all = all_ref[:, k, :tokens]
        top = jnp.max(top_all, axis=0, keepdims=True)
        total = jnp.sum(jnp.exp(top_all - top) * all_ref[:, k + 1, :tokens], axis=0, keepdims=True)
        return jnp.exp(mine_ref[:, 0:1] - turn_back(top)) * mine_ref[:, 1:2] / turn_back(total)

    student, teacher = mass(0, s_ref), mass(2, t_ref)
    mass_ref[...] = GRAD_SCALE * jnp.concatenate([student, teacher], axis=1)
    scale_x = GRAD_SCALE * student
    scale_t = GRAD_SCALE * (student - teacher)
    width = hp_ref.shape[2]
    for v in range(hp_ref.shape[0]):
        cols = slice(v * width, (v + 1) * width)
        hp_ref[v] = (u_ref[:tokens, cols] * scale_x + u_ref[tokens:, cols] * scale_t).astype(BF16)


def combine(stats_all, s_stats, t_stats, products, n_v):
    tokens = s_stats.shape[0]
    width = products.shape[1] // n_v
    return pl.pallas_call(
        combine_kernel,
        in_specs=in_vmem(4),
        out_specs=in_vmem(2),
        out_shape=[
            pltpu.HBM((n_v, tokens, width), BF16),
            jax.ShapeDtypeStruct((tokens, 2), F32),
        ],
        compiler_params=params(12 * MIB),
    )(stats_all, s_stats, t_stats, products)


def head_blocks(width):
    first = column_tile(width, 512)
    rest = column_tile(width - first, 1024)
    return [(0, first)] + [(k, rest) for k in range(first, width, rest)]


def head_kernel(tile, shares_ref, mass_ref, hidden_ref, out_ref, *scratch):
    shares, hidden, result, sems, hidden_sem, out_sems = scratch
    rows = shares_ref.shape[1]
    tokens, width = hidden_ref.shape
    steps = rows // tile
    chunks = [(step, slice(step * tile, (step + 1) * tile)) for step in range(steps)]
    last = slice(steps * tile, rows)
    if steps * tile < rows:
        chunks.append((steps, last))
    load_hidden = pltpu.make_async_copy(hidden_ref, hidden, hidden_sem)

    def load(here, index):
        return pltpu.make_async_copy(shares_ref.at[:, here], shares.at[:, here], sems.at[index])

    def store(here, index, block, start, size):
        cols = slice(start, start + size)
        return pltpu.make_async_copy(
            result.at[here, cols], out_ref.at[here, cols], out_sems.at[index, block]
        )

    load(chunks[0][1], chunks[0][0]).start()
    load_hidden.start()
    for index, here in chunks[1:]:
        load(here, index).start()
    load_hidden.wait()

    def produce(here, index):
        load(here, index).wait()
        student = shares[:tokens, here] * mass_ref[:, 0:1]
        teacher = shares[tokens:, here] * mass_ref[:, 1:2]
        grad = (student - teacher).T.astype(BF16)
        for block, (start, size) in enumerate(head_blocks(width)):
            inner = column_tile(size, 256)
            for k in range(start, start + size, inner):
                result[here, k : k + inner] = jnp.dot(
                    grad, hidden[:, k : k + inner], preferred_element_type=F32
                ).astype(BF16)
            store(here, index, block, start, size).start()

    def body(step, carry):
        produce(pl.ds(pl.multiple_of(step * tile, tile), tile), step)
        return carry

    if steps:
        lax.fori_loop(0, steps, body, 0)
    if steps * tile < rows:
        produce(last, steps)
    for index, here in chunks:
        for block, (start, size) in enumerate(head_blocks(width)):
            store(here, index, block, start, size).wait()


def head_gradient(shares, mass, hidden):
    rows = shares.shape[1]
    tokens, width = hidden.shape
    tile = 1536
    pieces = rows // tile + 1
    anywhere = pl.BlockSpec(memory_space=pl.ANY)
    in_hbm = lambda x: pltpu.with_memory_space_constraint(x, pltpu.HBM)
    return pl.pallas_call(
        functools.partial(head_kernel, tile),
        in_specs=[anywhere, *in_vmem(1), anywhere],
        out_specs=anywhere,
        out_shape=jax.ShapeDtypeStruct((rows, width), BF16),
        scratch_shapes=[
            pltpu.VMEM((2 * tokens, rows), F32),
            pltpu.VMEM((tokens, width), BF16),
            pltpu.VMEM((rows, width), BF16),
            pltpu.SemaphoreType.DMA((pieces,)),
            pltpu.SemaphoreType.DMA,
            pltpu.SemaphoreType.DMA((pieces, len(head_blocks(width)))),
        ],
        compiler_params=params(46 * MIB),
        cost_estimate=pl.CostEstimate(
            flops=8 * rows * width * tokens, bytes_accessed=2 * rows * width, transcendentals=0
        ),
    )(in_hbm(shares), mass, in_hbm(hidden))


def exchange(parts, axes):
    return lax.all_to_all(parts, axes, split_axis=0, concat_axis=0, tiled=True)


def shards(n_dp, n_v, hidden, head_weight, teacher_logits):
    everyone = ("vk", "vs", "pl", "co")
    n_pl = n_dp // 2
    count = n_dp * n_v
    group, width = hidden.shape
    weight = head_weight[0]
    square = (n_v, n_pl, group, width)

    own = exchange(copies(hidden, n_v * n_pl), ("vk", "vs", "pl"))
    sends, t_rows = split_teacher(teacher_logits[0], n_dp)
    other = lax.ppermute(own, "co", [(0, 1), (1, 0)])
    teacher = exchange(after(sends, own), ("pl", "co", "vs"))

    s_stats, lt, every_row, message = student_logits(
        own.reshape(square), other.reshape(square), t_rows, weight, count
    )
    stats_all = exchange(message, everyone)
    products, t_stats, shares = local_products(weight, teacher, lt, s_stats)
    partial_value, mass = combine(stats_all, s_stats, t_stats, products, n_v)
    pieces = exchange(partial_value.reshape(count, group, width), everyone)
    head_grad = head_gradient(shares, mass, every_row)
    hidden_grad = jnp.sum(pieces.astype(F32), axis=0).astype(BF16)
    return hidden_grad, head_grad[None]


def solution(mesh):
    n_dp, n_v = mesh.shape["dp"], mesh.shape["vocab"]
    split = Mesh(mesh.devices.reshape(n_dp // 2, 2, n_v // 2, 2), ("pl", "co", "vk", "vs"))
    dp, vocab = ("pl", "co"), ("vk", "vs")
    return jax.shard_map(
        functools.partial(shards, n_dp, n_v),
        mesh=split,
        in_specs=(P(dp, vocab), P(vocab, dp, None), P(vocab, dp, None)),
        out_specs=(P(dp, vocab), P(vocab, dp, None)),
        check_vma=False,
    )
```

```python
import functools

import jax
import jax.numpy as jnp
from jax import lax
from jax.experimental import pallas as pl
from jax.experimental.pallas import tpu as pltpu
from jax.sharding import Mesh
from jax.sharding import PartitionSpec as P

GRAD_SCALE = 32.0
F32 = jnp.float32
BF16 = jnp.bfloat16
MIB = 2**20
LANES = 128
LOWEST = -1e30
SUB_TILE = 128
LOGIT_TILE = 512
PRODUCT_TILE = 1024


def row_tile(rows, limit):
    best = rows
    for tile in range(16, limit + 1, 16):
        if rows % tile == 0:
            best = tile
    return best


def column_tile(width, limit):
    return max(c for c in range(LANES, limit + 1, LANES) if width % c == 0)


def tile_rows(step, tile, rows):
    if tile == rows:
        return slice(None)
    return pl.ds(pl.multiple_of(step * tile, tile), tile)


def params(limit):
    return pltpu.CompilerParams(vmem_limit_bytes=limit)


def whole(shape):
    return pl.BlockSpec(shape, lambda *_: (0,) * len(shape))


def in_vmem(count):
    return [pl.BlockSpec(memory_space=pltpu.VMEM)] * count


def stream(w_ref, buffer, sems, first, tile, ahead, compute, between):
    rows = w_ref.shape[0]
    if rows < first + tile:
        first = 0
    steps = (rows - first) // tile
    rest = rows - first - steps * tile
    ahead = min(ahead, steps)

    def copies_of(start, size, index):
        found = []
        for k, at in enumerate(range(0, size, SUB_TILE)):
            here = pl.ds(start + at, min(SUB_TILE, size - at))
            found.append(
                pltpu.make_async_copy(w_ref.at[here, :], buffer.at[here, :], sems.at[index, k])
            )
        return found

    def fetch(start, size, index):
        for copy in copies_of(start, size, index):
            copy.start()

    def arrive(start, size, index):
        for copy in copies_of(start, size, index):
            copy.wait()

    def origin(step):
        return pl.multiple_of(first + step * tile, LANES)

    tail = (first + steps * tile, rest, steps)
    if first:
        fetch(0, first, steps + 1)
    for step in range(ahead):
        fetch(first + step * tile, tile, step)
    if rest and ahead == steps:
        fetch(*tail)
    between()
    if first:
        arrive(0, first, steps + 1)
        compute(slice(0, first), steps + 1)

    def body(step, carry):
        @pl.when(step + ahead < steps)
        def _():
            fetch(origin(step + ahead), tile, step + ahead)

        if rest and ahead < steps:

            @pl.when(step + ahead == steps)
            def _():
                fetch(*tail)

        arrive(origin(step), tile, step)
        compute(pl.ds(origin(step), tile), step)
        return carry

    if steps:
        lax.fori_loop(0, steps, body, 0)
    if rest:
        arrive(*tail)
        compute(slice(tail[0], rows), steps)
    chunks = [(k, slice(first + k * tile, first + (k + 1) * tile)) for k in range(steps)]
    chunks += [(steps, slice(tail[0], rows))] * bool(rest)
    return chunks + [(steps + 1, slice(0, first))] * bool(first)


def stream_sems(rows, tile):
    return pltpu.SemaphoreType.DMA((rows // tile + 2, -(-tile // SUB_TILE)))


def turn(column):
    size = column.shape[0]
    row = lax.broadcasted_iota(jnp.int32, (size, size), 0)
    col = lax.broadcasted_iota(jnp.int32, (size, size), 1)
    return jnp.sum(jnp.where(row == col, column, 0.0), axis=0, keepdims=True)


def turn_back(line):
    size = line.shape[1]
    row = lax.broadcasted_iota(jnp.int32, (size, size), 0)
    col = lax.broadcasted_iota(jnp.int32, (size, size), 1)
    return jnp.sum(jnp.where(row == col, line, 0.0), axis=1, keepdims=True)


def logits_kernel(own_ref, other_ref, t_stats_ref, w_ref, *refs):
    stats_ref, lt_out, out_ref, message_ref, *scratch = refs
    lt_ref, hidden, buffer, staged, sems, lt_sems, out_sem = scratch
    keep = pltpu.make_async_copy(hidden, out_ref, out_sem)

    def assemble():
        n_v, n_pl, _, chunk = own_ref.shape
        core = lax.axis_index("co")
        staged[core] = own_ref[...].astype(F32)
        staged[1 - core] = other_ref[...].astype(F32)
        for v in range(n_v):
            groups = [staged[c, v, p] for p in range(n_pl) for c in range(2)]
            block = jnp.concatenate(groups, axis=0)
            hidden[:, v * chunk : (v + 1) * chunk] = block.astype(BF16)
        keep.start()

    def send(here, index):
        return pltpu.make_async_copy(lt_ref.at[:, here], lt_out.at[:, here], lt_sems.at[index])

    def compute(here, index):
        lt_ref[:, here] = lax.dot_general(
            hidden[...], buffer[here, :], (((1,), (1,)), ((), ())), preferred_element_type=F32
        )
        send(here, index).start()

    chunks = stream(w_ref, buffer, sems, 0, LOGIT_TILE, 3, compute, assemble)
    values = lt_ref[...]
    top = jnp.max(values, axis=1, keepdims=True)
    total = jnp.sum(jnp.exp(values - top), axis=1, keepdims=True)
    stats_ref[...] = jnp.concatenate([top, total], axis=1)
    lines = jnp.concatenate([turn(top), turn(total)], axis=0)
    lanes = t_stats_ref.shape[1]
    if lanes > lines.shape[1]:
        lines = jnp.concatenate([lines, jnp.zeros((2, lanes - lines.shape[1]), F32)], axis=1)
    message = jnp.concatenate([lines, t_stats_ref[...], jnp.zeros((4, lanes), F32)], axis=0)
    for k in range(message_ref.shape[0]):
        message_ref[k] = message
    keep.wait()
    for index, here in chunks:
        send(here, index).wait()


def student_logits(own, other, t_stats, weight, count):
    rows, width = weight.shape
    n_v, n_pl, group, _ = own.shape
    tokens = 2 * n_pl * group
    anywhere = pl.BlockSpec(memory_space=pl.ANY)
    return pl.pallas_call(
        logits_kernel,
        in_specs=[*in_vmem(3), anywhere],
        out_specs=[*in_vmem(1), anywhere, anywhere, *in_vmem(1)],
        out_shape=[
            jax.ShapeDtypeStruct((tokens, 2), F32),
            pltpu.HBM((tokens, rows), F32),
            pltpu.HBM((tokens, width), BF16),
            pltpu.HBM((count, 8, t_stats.shape[1]), F32),
        ],
        scratch_shapes=[
            pltpu.VMEM((tokens, rows), F32),
            pltpu.VMEM((tokens, width), BF16),
            pltpu.VMEM((rows, width), BF16),
            pltpu.VMEM((2, *own.shape), F32),
            stream_sems(rows, LOGIT_TILE),
            pltpu.SemaphoreType.DMA((rows // LOGIT_TILE + 2,)),
            pltpu.SemaphoreType.DMA,
        ],
        compiler_params=params(46 * MIB),
        cost_estimate=pl.CostEstimate(
            flops=8 * rows * width * tokens, bytes_accessed=2 * rows * width, transcendentals=0
        ),
    )(own, other, t_stats, weight)


def copies_kernel(h_ref, out_ref, buffer, sem, sems):
    load = pltpu.make_async_copy(h_ref, buffer, sem)
    load.start()
    load.wait()
    sends = [
        pltpu.make_async_copy(buffer, out_ref.at[k], sems.at[k]) for k in range(out_ref.shape[0])
    ]
    for send in sends:
        send.start()
    for send in sends:
        send.wait()


def copies(hidden, count):
    anywhere = pl.BlockSpec(memory_space=pl.ANY)
    return pl.pallas_call(
        copies_kernel,
        in_specs=[anywhere],
        out_specs=anywhere,
        out_shape=pltpu.HBM((count, *hidden.shape), BF16),
        scratch_shapes=[
            pltpu.VMEM(hidden.shape, BF16),
            pltpu.SemaphoreType.DMA,
            pltpu.SemaphoreType.DMA((count,)),
        ],
        compiler_params=params(4 * MIB),
    )(pltpu.with_memory_space_constraint(hidden, pltpu.HBM))


def split_kernel(t_ref, out_ref, stats_ref, buffer, sem):
    load = pltpu.make_async_copy(t_ref, buffer, sem)
    load.start()
    load.wait()
    total, (count, _, cols) = buffer.shape[1], out_ref.shape
    for s in range(2):
        for d in range(count // 2):
            start = (s * (count // 2) + d) * cols
            low = start // LANES * LANES
            high = min(-(-(start + cols) // LANES) * LANES, total)
            values = buffer[:, low:high].astype(F32)
            out_ref[d * 2 + s] = values[:, start - low : start - low + cols].astype(BF16)
    values = buffer[...].astype(F32)
    half, lanes = values.shape[0], stats_ref.shape[1]
    top = jnp.max(values, axis=1, keepdims=True)
    total = jnp.sum(jnp.exp(values - top), axis=1, keepdims=True)
    group = lax.axis_index("pl") * 2 + lax.axis_index("co")
    first = (group * 2 + lax.axis_index("vs")) * half
    row = lax.broadcasted_iota(jnp.int32, (half, lanes), 0)
    lane = lax.broadcasted_iota(jnp.int32, (half, lanes), 1)
    chosen = lane == first + row
    tops = jnp.max(jnp.where(chosen, top, LOWEST), axis=0, keepdims=True)
    totals = jnp.sum(jnp.where(chosen, total, 0.0), axis=0, keepdims=True)
    stats_ref[...] = jnp.concatenate([tops, totals], axis=0)


def split_teacher(piece, n_dp):
    half, total = piece.shape
    return pl.pallas_call(
        split_kernel,
        in_specs=[pl.BlockSpec(memory_space=pl.ANY)],
        out_specs=in_vmem(2),
        out_shape=[
            pltpu.HBM((2 * n_dp, half, total // (2 * n_dp)), BF16),
            pltpu.HBM((2, -(-2 * half * n_dp // LANES) * LANES), F32),
        ],
        scratch_shapes=[pltpu.VMEM(piece.shape, BF16), pltpu.SemaphoreType.DMA],
        compiler_params=params(8 * MIB),
    )(pltpu.with_memory_space_constraint(piece, pltpu.HBM))


def teacher_values(t_ref):
    return jnp.concatenate([t_ref[j].astype(F32) for j in range(t_ref.shape[0])], axis=0)


def products_kernel(t_ref, lt_in, stats_ref, w_ref, u_ref, t_stats_ref, shares_ref, *refs):
    lt_ref, buffer, packed, shares, sems, own_sems = refs
    load = pltpu.make_async_copy(lt_in, lt_ref, own_sems.at[0])
    keep = pltpu.make_async_copy(shares, shares_ref, own_sems.at[1])
    tokens = stats_ref.shape[0]
    load.start()

    def prepare():
        values = teacher_values(t_ref)
        top = jnp.max(values, axis=1, keepdims=True)
        weights = jnp.exp(values - top)
        total = jnp.sum(weights, axis=1, keepdims=True)
        t_stats_ref[...] = jnp.concatenate([top, total], axis=1)
        teach = weights * (1.0 / total)
        load.wait()
        share = jnp.exp(lt_ref[...] - stats_ref[:, 0:1]) * (1.0 / stats_ref[:, 1:2])
        shares[:tokens, :] = share
        shares[tokens:, :] = teach
        packed[:tokens, :] = (share - teach).astype(BF16)
        packed[tokens:, :] = teach.astype(BF16)
        keep.start()
        u_ref[...] = jnp.zeros_like(u_ref)

    def compute(here, index):
        width = u_ref.shape[1]
        block = column_tile(width, 512)
        for k in range(0, width, block):
            cols = slice(k, k + block)
            u_ref[:, cols] += jnp.dot(
                packed[:, here], buffer[here, cols], preferred_element_type=F32
            )

    stream(w_ref, buffer, sems, 512, PRODUCT_TILE, 2, compute, prepare)
    keep.wait()


def local_products(weight, teacher, lt, stats):
    rows, width = weight.shape
    tokens = lt.shape[0]
    anywhere = pl.BlockSpec(memory_space=pl.ANY)
    return pl.pallas_call(
        products_kernel,
        in_specs=[*in_vmem(1), anywhere, *in_vmem(1), anywhere],
        out_specs=[*in_vmem(2), anywhere],
        out_shape=[
            jax.ShapeDtypeStruct((2 * tokens, width), F32),
            jax.ShapeDtypeStruct((tokens, 2), F32),
            pltpu.HBM((2 * tokens, rows), F32),
        ],
        scratch_shapes=[
            pltpu.VMEM((tokens, rows), F32),
            pltpu.VMEM((rows, width), BF16),
            pltpu.VMEM((2 * tokens, rows), BF16),
            pltpu.VMEM((2 * tokens, rows), F32),
            stream_sems(rows, PRODUCT_TILE),
            pltpu.SemaphoreType.DMA((2,)),
        ],
        compiler_params=params(46 * MIB),
        cost_estimate=pl.CostEstimate(
            flops=8 * rows * width * tokens, bytes_accessed=2 * rows * width, transcendentals=0
        ),
    )(teacher, pltpu.with_memory_space_constraint(lt, pltpu.HBM), stats, weight)


def combine_kernel(all_ref, s_ref, t_ref, u_ref, hp_ref, mass_ref):
    tokens = s_ref.shape[0]

    def mass(k, mine_ref):
        top_all = all_ref[:, k, :tokens]
        top = jnp.max(top_all, axis=0, keepdims=True)
        total = jnp.sum(jnp.exp(top_all - top) * all_ref[:, k + 1, :tokens], axis=0, keepdims=True)
        return jnp.exp(mine_ref[:, 0:1] - turn_back(top)) * mine_ref[:, 1:2] / turn_back(total)

    student, teacher = mass(0, s_ref), mass(2, t_ref)
    mass_ref[...] = GRAD_SCALE * jnp.concatenate([student, teacher], axis=1)
    scale_x = GRAD_SCALE * student
    scale_t = GRAD_SCALE * (student - teacher)
    width = hp_ref.shape[2]
    for v in range(hp_ref.shape[0]):
        cols = slice(v * width, (v + 1) * width)
        hp_ref[v] = (u_ref[:tokens, cols] * scale_x + u_ref[tokens:, cols] * scale_t).astype(BF16)


def combine(stats_all, s_stats, t_stats, products, n_v):
    tokens = s_stats.shape[0]
    width = products.shape[1] // n_v
    return pl.pallas_call(
        combine_kernel,
        in_specs=in_vmem(4),
        out_specs=in_vmem(2),
        out_shape=[
            pltpu.HBM((n_v, tokens, width), BF16),
            jax.ShapeDtypeStruct((tokens, 2), F32),
        ],
        compiler_params=params(12 * MIB),
    )(stats_all, s_stats, t_stats, products)


def head_blocks(width):
    first = column_tile(width, 512)
    rest = column_tile(width - first, 1024)
    return [(0, first)] + [(k, rest) for k in range(first, width, rest)]


def head_kernel(tile, shares_ref, mass_ref, hidden_ref, out_ref, *scratch):
    shares, hidden, result, sems, hidden_sem, out_sems = scratch
    rows = shares_ref.shape[1]
    tokens, width = hidden_ref.shape
    steps = rows // tile
    chunks = [(step, slice(step * tile, (step + 1) * tile)) for step in range(steps)]
    last = slice(steps * tile, rows)
    if steps * tile < rows:
        chunks.append((steps, last))
    load_hidden = pltpu.make_async_copy(hidden_ref, hidden, hidden_sem)

    def load(here, index):
        return pltpu.make_async_copy(shares_ref.at[:, here], shares.at[:, here], sems.at[index])

    def store(here, index, block, start, size):
        cols = slice(start, start + size)
        return pltpu.make_async_copy(
            result.at[here, cols], out_ref.at[here, cols], out_sems.at[index, block]
        )

    load(chunks[0][1], chunks[0][0]).start()
    load_hidden.start()
    for index, here in chunks[1:]:
        load(here, index).start()
    load_hidden.wait()

    def produce(here, index):
        load(here, index).wait()
        student = shares[:tokens, here] * mass_ref[:, 0:1]
        teacher = shares[tokens:, here] * mass_ref[:, 1:2]
        grad = (student - teacher).T.astype(BF16)
        for block, (start, size) in enumerate(head_blocks(width)):
            inner = column_tile(size, 256)
            for k in range(start, start + size, inner):
                result[here, k : k + inner] = jnp.dot(
                    grad, hidden[:, k : k + inner], preferred_element_type=F32
                ).astype(BF16)
            store(here, index, block, start, size).start()

    def body(step, carry):
        produce(pl.ds(pl.multiple_of(step * tile, tile), tile), step)
        return carry

    if steps:
        lax.fori_loop(0, steps, body, 0)
    if steps * tile < rows:
        produce(last, steps)
    for index, here in chunks:
        for block, (start, size) in enumerate(head_blocks(width)):
            store(here, index, block, start, size).wait()


def head_gradient(shares, mass, hidden):
    rows = shares.shape[1]
    tokens, width = hidden.shape
    tile = 1536
    pieces = rows // tile + 1
    anywhere = pl.BlockSpec(memory_space=pl.ANY)
    in_hbm = lambda x: pltpu.with_memory_space_constraint(x, pltpu.HBM)
    return pl.pallas_call(
        functools.partial(head_kernel, tile),
        in_specs=[anywhere, *in_vmem(1), anywhere],
        out_specs=anywhere,
        out_shape=jax.ShapeDtypeStruct((rows, width), BF16),
        scratch_shapes=[
            pltpu.VMEM((2 * tokens, rows), F32),
            pltpu.VMEM((tokens, width), BF16),
            pltpu.VMEM((rows, width), BF16),
            pltpu.SemaphoreType.DMA((pieces,)),
            pltpu.SemaphoreType.DMA,
            pltpu.SemaphoreType.DMA((pieces, len(head_blocks(width)))),
        ],
        compiler_params=params(46 * MIB),
        cost_estimate=pl.CostEstimate(
            flops=8 * rows * width * tokens, bytes_accessed=2 * rows * width, transcendentals=0
        ),
    )(in_hbm(shares), mass, in_hbm(hidden))


def exchange(parts, axes):
    return lax.all_to_all(parts, axes, split_axis=0, concat_axis=0, tiled=True)


def shards(n_dp, n_v, hidden, head_weight, teacher_logits):
    everyone = ("vk", "vs", "pl", "co")
    n_pl = n_dp // 2
    count = n_dp * n_v
    group, width = hidden.shape
    weight = head_weight[0]
    square = (n_v, n_pl, group, width)

    own = exchange(copies(hidden, n_v * n_pl), ("vk", "vs", "pl"))
    sends, t_rows = split_teacher(teacher_logits[0], n_dp)
    sends, own = lax.optimization_barrier((sends, own))
    other = lax.ppermute(own, "co", [(0, 1), (1, 0)])
    teacher = exchange(sends, ("pl", "co", "vs"))

    s_stats, lt, every_row, message = student_logits(
        own.reshape(square), other.reshape(square), t_rows, weight, count
    )
    stats_all = exchange(message, everyone)
    products, t_stats, shares = local_products(weight, teacher, lt, s_stats)
    partial_value, mass = combine(stats_all, s_stats, t_stats, products, n_v)
    pieces = exchange(partial_value.reshape(count, group, width), everyone)
    head_grad = head_gradient(shares, mass, every_row)
    hidden_grad = jnp.sum(pieces.astype(F32), axis=0).astype(BF16)
    return hidden_grad, head_grad[None]


def solution(mesh):
    n_dp, n_v = mesh.shape["dp"], mesh.shape["vocab"]
    split = Mesh(mesh.devices.reshape(n_dp // 2, 2, n_v // 2, 2), ("pl", "co", "vk", "vs"))
    dp, vocab = ("pl", "co"), ("vk", "vs")
    return jax.shard_map(
        functools.partial(shards, n_dp, n_v),
        mesh=split,
        in_specs=(P(dp, vocab), P(vocab, dp, None), P(vocab, dp, None)),
        out_specs=(P(dp, vocab), P(vocab, dp, None)),
        check_vma=False,
    )
```

```python
import functools

import jax
import jax.numpy as jnp
from jax import lax
from jax.experimental import pallas as pl
from jax.experimental.pallas import tpu as pltpu
from jax.sharding import Mesh
from jax.sharding import PartitionSpec as P

GRAD_SCALE = 32.0
F32 = jnp.float32
BF16 = jnp.bfloat16
MIB = 2**20
LANES = 128
LOWEST = -1e30
LOGIT_TILE = 512
PRODUCT_TILE = 1024


def row_tile(rows, limit):
    best = rows
    for tile in range(16, limit + 1, 16):
        if rows % tile == 0:
            best = tile
    return best


def column_tile(width, limit):
    return max(c for c in range(LANES, limit + 1, LANES) if width % c == 0)


def tile_rows(step, tile, rows):
    if tile == rows:
        return slice(None)
    return pl.ds(pl.multiple_of(step * tile, tile), tile)


def params(limit):
    return pltpu.CompilerParams(vmem_limit_bytes=limit)


def whole(shape):
    return pl.BlockSpec(shape, lambda *_: (0,) * len(shape))


def in_vmem(count):
    return [pl.BlockSpec(memory_space=pltpu.VMEM)] * count


def stream(w_ref, buffer, sems, first, tile, ahead, compute, between):
    rows = w_ref.shape[0]
    if rows < first + tile:
        first = 0
    steps = (rows - first) // tile
    begin, last = slice(0, first), slice(first + steps * tile, rows)
    rest = rows - last.start

    def copy(here, sem):
        return pltpu.make_async_copy(w_ref.at[here, :], buffer.at[here, :], sem)

    def place(step):
        return pl.ds(pl.multiple_of(first + step * tile, LANES), tile)

    ahead = min(ahead, steps)
    if first:
        copy(begin, sems.at[steps + 1]).start()
    for step in range(ahead):
        copy(place(step), sems.at[step]).start()
    if rest and ahead == steps:
        copy(last, sems.at[steps]).start()
    between()
    if first:
        copy(begin, sems.at[steps + 1]).wait()
        compute(begin, steps + 1)

    def body(step, carry):
        @pl.when(step + ahead < steps)
        def _():
            copy(place(step + ahead), sems.at[step + ahead]).start()

        if rest and ahead < steps:

            @pl.when(step + ahead == steps)
            def _():
                copy(last, sems.at[steps]).start()

        copy(place(step), sems.at[step]).wait()
        compute(place(step), step)
        return carry

    if steps:
        lax.fori_loop(0, steps, body, 0)
    if rest:
        copy(last, sems.at[steps]).wait()
        compute(last, steps)
    chunks = [(k, slice(first + k * tile, first + (k + 1) * tile)) for k in range(steps)]
    return chunks + [(steps, last)] * bool(rest) + [(steps + 1, begin)] * bool(first)


def turn(column):
    size = column.shape[0]
    row = lax.broadcasted_iota(jnp.int32, (size, size), 0)
    col = lax.broadcasted_iota(jnp.int32, (size, size), 1)
    return jnp.sum(jnp.where(row == col, column, 0.0), axis=0, keepdims=True)


def turn_back(line):
    size = line.shape[1]
    row = lax.broadcasted_iota(jnp.int32, (size, size), 0)
    col = lax.broadcasted_iota(jnp.int32, (size, size), 1)
    return jnp.sum(jnp.where(row == col, line, 0.0), axis=1, keepdims=True)


def logits_kernel(own_ref, other_ref, t_stats_ref, w_ref, *refs):
    stats_ref, lt_out, out_ref, message_ref, *scratch = refs
    lt_ref, hidden, buffer, staged, t_stats, sems, lt_sems, out_sems = scratch
    keep = pltpu.make_async_copy(hidden, out_ref, out_sems.at[0])
    load = pltpu.make_async_copy(t_stats_ref, t_stats, out_sems.at[1])
    load.start()

    def assemble():
        n_v, n_pl, _, chunk = own_ref.shape
        core = lax.axis_index("co")
        staged[core] = own_ref[...].astype(F32)
        staged[1 - core] = other_ref[...].astype(F32)
        for v in range(n_v):
            groups = [staged[c, v, p] for p in range(n_pl) for c in range(2)]
            block = jnp.concatenate(groups, axis=0)
            hidden[:, v * chunk : (v + 1) * chunk] = block.astype(BF16)
        keep.start()

    def send(here, index):
        return pltpu.make_async_copy(lt_ref.at[:, here], lt_out.at[:, here], lt_sems.at[index])

    def compute(here, index):
        lt_ref[:, here] = lax.dot_general(
            hidden[...], buffer[here, :], (((1,), (1,)), ((), ())), preferred_element_type=F32
        )
        send(here, index).start()

    chunks = stream(w_ref, buffer, sems, 0, LOGIT_TILE, 3, compute, assemble)
    values = lt_ref[...]
    top = jnp.max(values, axis=1, keepdims=True)
    total = jnp.sum(jnp.exp(values - top), axis=1, keepdims=True)
    stats_ref[...] = jnp.concatenate([top, total], axis=1)
    lines = jnp.concatenate([turn(top), turn(total)], axis=0)
    load.wait()
    lanes = t_stats.shape[1]
    if lanes > lines.shape[1]:
        lines = jnp.concatenate([lines, jnp.zeros((2, lanes - lines.shape[1]), F32)], axis=1)
    message = jnp.concatenate([lines, t_stats[...], jnp.zeros((4, lanes), F32)], axis=0)
    for k in range(message_ref.shape[0]):
        message_ref[k] = message
    keep.wait()
    for index, here in chunks:
        send(here, index).wait()


def student_logits(own, other, t_stats, weight, count):
    rows, width = weight.shape
    n_v, n_pl, group, _ = own.shape
    tokens = 2 * n_pl * group
    anywhere = pl.BlockSpec(memory_space=pl.ANY)
    return pl.pallas_call(
        logits_kernel,
        in_specs=[*in_vmem(2), anywhere, anywhere],
        out_specs=[*in_vmem(1), anywhere, anywhere, *in_vmem(1)],
        out_shape=[
            jax.ShapeDtypeStruct((tokens, 2), F32),
            pltpu.HBM((tokens, rows), F32),
            pltpu.HBM((tokens, width), BF16),
            pltpu.HBM((count, 8, t_stats.shape[1]), F32),
        ],
        scratch_shapes=[
            pltpu.VMEM((tokens, rows), F32),
            pltpu.VMEM((tokens, width), BF16),
            pltpu.VMEM((rows, width), BF16),
            pltpu.VMEM((2, *own.shape), F32),
            pltpu.VMEM(t_stats.shape, F32),
            pltpu.SemaphoreType.DMA((rows // LOGIT_TILE + 2,)),
            pltpu.SemaphoreType.DMA((rows // LOGIT_TILE + 2,)),
            pltpu.SemaphoreType.DMA((2,)),
        ],
        compiler_params=params(46 * MIB),
        cost_estimate=pl.CostEstimate(
            flops=8 * rows * width * tokens, bytes_accessed=2 * rows * width, transcendentals=0
        ),
    )(own, other, pltpu.with_memory_space_constraint(t_stats, pltpu.HBM), weight)


def copies_kernel(h_ref, out_ref, buffer, sem, sems):
    load = pltpu.make_async_copy(h_ref, buffer, sem)
    load.start()
    load.wait()
    sends = [
        pltpu.make_async_copy(buffer, out_ref.at[k], sems.at[k]) for k in range(out_ref.shape[0])
    ]
    for send in sends:
        send.start()
    for send in sends:
        send.wait()


def copies(hidden, count):
    anywhere = pl.BlockSpec(memory_space=pl.ANY)
    return pl.pallas_call(
        copies_kernel,
        in_specs=[anywhere],
        out_specs=anywhere,
        out_shape=pltpu.HBM((count, *hidden.shape), BF16),
        scratch_shapes=[
            pltpu.VMEM(hidden.shape, BF16),
            pltpu.SemaphoreType.DMA,
            pltpu.SemaphoreType.DMA((count,)),
        ],
        compiler_params=params(4 * MIB),
    )(pltpu.with_memory_space_constraint(hidden, pltpu.HBM))


def split_kernel(t_ref, out_ref, stats_ref, buffer, sem):
    load = pltpu.make_async_copy(t_ref, buffer, sem)
    load.start()
    load.wait()
    total, (count, _, cols) = buffer.shape[1], out_ref.shape
    for s in range(2):
        for d in range(count // 2):
            start = (s * (count // 2) + d) * cols
            low = start // LANES * LANES
            high = min(-(-(start + cols) // LANES) * LANES, total)
            values = buffer[:, low:high].astype(F32)
            out_ref[d * 2 + s] = values[:, start - low : start - low + cols].astype(BF16)
    values = buffer[...].astype(F32)
    half, lanes = values.shape[0], stats_ref.shape[1]
    top = jnp.max(values, axis=1, keepdims=True)
    total = jnp.sum(jnp.exp(values - top), axis=1, keepdims=True)
    group = lax.axis_index("pl") * 2 + lax.axis_index("co")
    first = (group * 2 + lax.axis_index("vs")) * half
    row = lax.broadcasted_iota(jnp.int32, (half, lanes), 0)
    lane = lax.broadcasted_iota(jnp.int32, (half, lanes), 1)
    chosen = lane == first + row
    tops = jnp.max(jnp.where(chosen, top, LOWEST), axis=0, keepdims=True)
    totals = jnp.sum(jnp.where(chosen, total, 0.0), axis=0, keepdims=True)
    stats_ref[...] = jnp.concatenate([tops, totals], axis=0)


def split_teacher(piece, n_dp):
    half, total = piece.shape
    return pl.pallas_call(
        split_kernel,
        in_specs=[pl.BlockSpec(memory_space=pl.ANY)],
        out_specs=in_vmem(2),
        out_shape=[
            pltpu.HBM((2 * n_dp, half, total // (2 * n_dp)), BF16),
            pltpu.HBM((2, -(-2 * half * n_dp // LANES) * LANES), F32),
        ],
        scratch_shapes=[pltpu.VMEM(piece.shape, BF16), pltpu.SemaphoreType.DMA],
        compiler_params=params(8 * MIB),
    )(pltpu.with_memory_space_constraint(piece, pltpu.HBM))


def teacher_values(t_ref):
    return jnp.concatenate([t_ref[j].astype(F32) for j in range(t_ref.shape[0])], axis=0)


def products_kernel(t_ref, lt_in, stats_ref, w_ref, u_ref, t_stats_ref, shares_ref, *refs):
    lt_ref, buffer, packed, shares, sems, own_sems = refs
    load = pltpu.make_async_copy(lt_in, lt_ref, own_sems.at[0])
    keep = pltpu.make_async_copy(shares, shares_ref, own_sems.at[1])
    tokens = stats_ref.shape[0]
    load.start()

    def prepare():
        values = teacher_values(t_ref)
        top = jnp.max(values, axis=1, keepdims=True)
        weights = jnp.exp(values - top)
        total = jnp.sum(weights, axis=1, keepdims=True)
        t_stats_ref[...] = jnp.concatenate([top, total], axis=1)
        teach = weights * (1.0 / total)
        load.wait()
        share = jnp.exp(lt_ref[...] - stats_ref[:, 0:1]) * (1.0 / stats_ref[:, 1:2])
        shares[:tokens, :] = share
        shares[tokens:, :] = teach
        packed[:tokens, :] = (share - teach).astype(BF16)
        packed[tokens:, :] = teach.astype(BF16)
        keep.start()
        u_ref[...] = jnp.zeros_like(u_ref)

    def compute(here, index):
        width = u_ref.shape[1]
        block = column_tile(width, 512)

        def add(step, carry):
            cols = pl.ds(pl.multiple_of(step * block, block), block)
            u_ref[:, cols] += jnp.dot(
                packed[:, here], buffer[here, cols], preferred_element_type=F32
            )
            return carry

        lax.fori_loop(0, width // block, add, 0)

    stream(w_ref, buffer, sems, 512, PRODUCT_TILE, 2, compute, prepare)
    keep.wait()


def local_products(weight, teacher, lt, stats):
    rows, width = weight.shape
    tokens = lt.shape[0]
    anywhere = pl.BlockSpec(memory_space=pl.ANY)
    return pl.pallas_call(
        products_kernel,
        in_specs=[*in_vmem(1), anywhere, *in_vmem(1), anywhere],
        out_specs=[*in_vmem(2), anywhere],
        out_shape=[
            jax.ShapeDtypeStruct((2 * tokens, width), F32),
            jax.ShapeDtypeStruct((tokens, 2), F32),
            pltpu.HBM((2 * tokens, rows), F32),
        ],
        scratch_shapes=[
            pltpu.VMEM((tokens, rows), F32),
            pltpu.VMEM((rows, width), BF16),
            pltpu.VMEM((2 * tokens, rows), BF16),
            pltpu.VMEM((2 * tokens, rows), F32),
            pltpu.SemaphoreType.DMA((rows // PRODUCT_TILE + 2,)),
            pltpu.SemaphoreType.DMA((2,)),
        ],
        compiler_params=params(46 * MIB),
        cost_estimate=pl.CostEstimate(
            flops=8 * rows * width * tokens, bytes_accessed=2 * rows * width, transcendentals=0
        ),
    )(teacher, pltpu.with_memory_space_constraint(lt, pltpu.HBM), stats, weight)


def combine_kernel(all_ref, s_ref, t_ref, u_ref, hp_ref, mass_ref):
    tokens = s_ref.shape[0]

    def mass(k, mine_ref):
        top_all = all_ref[:, k, :tokens]
        top = jnp.max(top_all, axis=0, keepdims=True)
        total = jnp.sum(jnp.exp(top_all - top) * all_ref[:, k + 1, :tokens], axis=0, keepdims=True)
        return jnp.exp(mine_ref[:, 0:1] - turn_back(top)) * mine_ref[:, 1:2] / turn_back(total)

    student, teacher = mass(0, s_ref), mass(2, t_ref)
    mass_ref[...] = GRAD_SCALE * jnp.concatenate([student, teacher], axis=1)
    scale_x = GRAD_SCALE * student
    scale_t = GRAD_SCALE * (student - teacher)
    width = hp_ref.shape[2]
    for v in range(hp_ref.shape[0]):
        cols = slice(v * width, (v + 1) * width)
        hp_ref[v] = (u_ref[:tokens, cols] * scale_x + u_ref[tokens:, cols] * scale_t).astype(BF16)


def combine(stats_all, s_stats, t_stats, products, n_v):
    tokens = s_stats.shape[0]
    width = products.shape[1] // n_v
    return pl.pallas_call(
        combine_kernel,
        in_specs=in_vmem(4),
        out_specs=in_vmem(2),
        out_shape=[
            pltpu.HBM((n_v, tokens, width), BF16),
            jax.ShapeDtypeStruct((tokens, 2), F32),
        ],
        compiler_params=params(12 * MIB),
    )(stats_all, s_stats, t_stats, products)


def head_kernel(tile, shares_ref, mass_ref, hidden_ref, out_ref, *scratch):
    shares, hidden, result, sems, hidden_sem, out_sems = scratch
    rows = shares_ref.shape[1]
    tokens, width = hidden_ref.shape
    steps = rows // tile
    chunks = [(step, slice(step * tile, (step + 1) * tile)) for step in range(steps)]
    last = slice(steps * tile, rows)
    if steps * tile < rows:
        chunks.append((steps, last))
    load_hidden = pltpu.make_async_copy(hidden_ref, hidden, hidden_sem)

    def load(here, index):
        return pltpu.make_async_copy(shares_ref.at[:, here], shares.at[:, here], sems.at[index])

    def store(here, index):
        return pltpu.make_async_copy(result.at[here, :], out_ref.at[here, :], out_sems.at[index])

    block = column_tile(width, 512)

    load(chunks[0][1], chunks[0][0]).start()
    load_hidden.start()
    for index, here in chunks[1:]:
        load(here, index).start()
    load_hidden.wait()

    def produce(here, index):
        load(here, index).wait()
        student = shares[:tokens, here] * mass_ref[:, 0:1]
        teacher = shares[tokens:, here] * mass_ref[:, 1:2]
        grad = (student - teacher).T.astype(BF16)

        def columns(step, carry):
            cols = pl.ds(pl.multiple_of(step * block, block), block)
            result[here, cols] = jnp.dot(
                grad, hidden[:, cols], preferred_element_type=F32
            ).astype(BF16)
            return carry

        lax.fori_loop(0, width // block, columns, 0)
        store(here, index).start()

    def body(step, carry):
        produce(pl.ds(pl.multiple_of(step * tile, tile), tile), step)
        return carry

    if steps:
        lax.fori_loop(0, steps, body, 0)
    if steps * tile < rows:
        produce(last, steps)
    for index, here in chunks:
        store(here, index).wait()


def head_gradient(shares, mass, hidden):
    rows = shares.shape[1]
    tokens, width = hidden.shape
    tile = 512
    pieces = rows // tile + 1
    anywhere = pl.BlockSpec(memory_space=pl.ANY)
    in_hbm = lambda x: pltpu.with_memory_space_constraint(x, pltpu.HBM)
    return pl.pallas_call(
        functools.partial(head_kernel, tile),
        in_specs=[anywhere, *in_vmem(1), anywhere],
        out_specs=anywhere,
        out_shape=jax.ShapeDtypeStruct((rows, width), BF16),
        scratch_shapes=[
            pltpu.VMEM((2 * tokens, rows), F32),
            pltpu.VMEM((tokens, width), BF16),
            pltpu.VMEM((rows, width), BF16),
            pltpu.SemaphoreType.DMA((pieces,)),
            pltpu.SemaphoreType.DMA,
            pltpu.SemaphoreType.DMA((pieces,)),
        ],
        compiler_params=params(46 * MIB),
        cost_estimate=pl.CostEstimate(
            flops=8 * rows * width * tokens, bytes_accessed=2 * rows * width, transcendentals=0
        ),
    )(in_hbm(shares), mass, in_hbm(hidden))


def exchange(parts, axes):
    return lax.all_to_all(parts, axes, split_axis=0, concat_axis=0, tiled=True)


def shards(n_dp, n_v, hidden, head_weight, teacher_logits):
    everyone = ("vk", "vs", "pl", "co")
    n_pl = n_dp // 2
    count = n_dp * n_v
    group, width = hidden.shape
    weight = head_weight[0]
    square = (n_v, n_pl, group, width)

    own = exchange(copies(hidden, n_v * n_pl), ("vk", "vs", "pl"))
    sends, t_rows = split_teacher(teacher_logits[0], n_dp)
    sends, own = lax.optimization_barrier((sends, own))
    other = lax.ppermute(own, "co", [(0, 1), (1, 0)])
    teacher = exchange(sends, ("pl", "co", "vs"))

    s_stats, lt, every_row, message = student_logits(
        own.reshape(square), other.reshape(square), t_rows, weight, count
    )
    stats_all = exchange(message, everyone)
    products, t_stats, shares = local_products(weight, teacher, lt, s_stats)
    partial_value, mass = combine(stats_all, s_stats, t_stats, products, n_v)
    pieces = exchange(partial_value.reshape(count, group, width), everyone)
    head_grad = head_gradient(shares, mass, every_row)
    hidden_grad = jnp.sum(pieces.astype(F32), axis=0).astype(BF16)
    return hidden_grad, head_grad[None]


def solution(mesh):
    n_dp, n_v = mesh.shape["dp"], mesh.shape["vocab"]
    split = Mesh(mesh.devices.reshape(n_dp // 2, 2, n_v // 2, 2), ("pl", "co", "vk", "vs"))
    dp, vocab = ("pl", "co"), ("vk", "vs")
    return jax.shard_map(
        functools.partial(shards, n_dp, n_v),
        mesh=split,
        in_specs=(P(dp, vocab), P(vocab, dp, None), P(vocab, dp, None)),
        out_specs=(P(dp, vocab), P(vocab, dp, None)),
        check_vma=False,
    )
```

```python
import functools

import jax
import jax.numpy as jnp
from jax import lax
from jax.experimental import pallas as pl
from jax.experimental.pallas import tpu as pltpu
from jax.sharding import Mesh
from jax.sharding import PartitionSpec as P

GRAD_SCALE = 32.0
F32 = jnp.float32
BF16 = jnp.bfloat16
MIB = 2**20
LANES = 128
LOWEST = -1e30
LOGIT_TILE = 512
PRODUCT_TILE = 1024


def row_tile(rows, limit):
    best = rows
    for tile in range(16, limit + 1, 16):
        if rows % tile == 0:
            best = tile
    return best


def column_tile(width, limit):
    return max(c for c in range(LANES, limit + 1, LANES) if width % c == 0)


def tile_rows(step, tile, rows):
    if tile == rows:
        return slice(None)
    return pl.ds(pl.multiple_of(step * tile, tile), tile)


def params(limit):
    return pltpu.CompilerParams(vmem_limit_bytes=limit)


def whole(shape):
    return pl.BlockSpec(shape, lambda *_: (0,) * len(shape))


def in_vmem(count):
    return [pl.BlockSpec(memory_space=pltpu.VMEM)] * count


def stream(w_ref, buffer, sems, first, tile, ahead, compute, between):
    rows = w_ref.shape[0]
    if rows < first + tile:
        first = 0
    steps = (rows - first) // tile
    begin, last = slice(0, first), slice(first + steps * tile, rows)
    rest = rows - last.start

    def copy(here, sem):
        return pltpu.make_async_copy(w_ref.at[here, :], buffer.at[here, :], sem)

    def place(step):
        return pl.ds(pl.multiple_of(first + step * tile, LANES), tile)

    ahead = min(ahead, steps)
    if first:
        copy(begin, sems.at[steps + 1]).start()
    for step in range(ahead):
        copy(place(step), sems.at[step]).start()
    if rest and ahead == steps:
        copy(last, sems.at[steps]).start()
    between()
    if first:
        copy(begin, sems.at[steps + 1]).wait()
        compute(begin, steps + 1)

    def body(step, carry):
        @pl.when(step + ahead < steps)
        def _():
            copy(place(step + ahead), sems.at[step + ahead]).start()

        if rest and ahead < steps:

            @pl.when(step + ahead == steps)
            def _():
                copy(last, sems.at[steps]).start()

        copy(place(step), sems.at[step]).wait()
        compute(place(step), step)
        return carry

    if steps:
        lax.fori_loop(0, steps, body, 0)
    if rest:
        copy(last, sems.at[steps]).wait()
        compute(last, steps)
    chunks = [(k, slice(first + k * tile, first + (k + 1) * tile)) for k in range(steps)]
    return chunks + [(steps, last)] * bool(rest) + [(steps + 1, begin)] * bool(first)


def turn(column):
    size = column.shape[0]
    row = lax.broadcasted_iota(jnp.int32, (size, size), 0)
    col = lax.broadcasted_iota(jnp.int32, (size, size), 1)
    return jnp.sum(jnp.where(row == col, column, 0.0), axis=0, keepdims=True)


def turn_back(line):
    size = line.shape[1]
    row = lax.broadcasted_iota(jnp.int32, (size, size), 0)
    col = lax.broadcasted_iota(jnp.int32, (size, size), 1)
    return jnp.sum(jnp.where(row == col, line, 0.0), axis=1, keepdims=True)


def logits_kernel(own_ref, other_ref, t_stats_ref, w_ref, *refs):
    stats_ref, lt_out, out_ref, message_ref, *scratch = refs
    lt_ref, hidden, buffer, staged, t_stats, sems, lt_sems, out_sems = scratch
    keep = pltpu.make_async_copy(hidden, out_ref, out_sems.at[0])
    load = pltpu.make_async_copy(t_stats_ref, t_stats, out_sems.at[1])
    load.start()

    def assemble():
        n_v, n_pl, _, chunk = own_ref.shape
        core = lax.axis_index("co")
        staged[core] = own_ref[...].astype(F32)
        staged[1 - core] = other_ref[...].astype(F32)
        for v in range(n_v):
            groups = [staged[c, v, p] for p in range(n_pl) for c in range(2)]
            block = jnp.concatenate(groups, axis=0)
            hidden[:, v * chunk : (v + 1) * chunk] = block.astype(BF16)
        keep.start()

    def send(here, index):
        return pltpu.make_async_copy(lt_ref.at[:, here], lt_out.at[:, here], lt_sems.at[index])

    def compute(here, index):
        lt_ref[:, here] = lax.dot_general(
            hidden[...], buffer[here, :], (((1,), (1,)), ((), ())), preferred_element_type=F32
        )
        send(here, index).start()

    chunks = stream(w_ref, buffer, sems, 256, LOGIT_TILE, 3, compute, assemble)
    values = lt_ref[...]
    top = jnp.max(values, axis=1, keepdims=True)
    total = jnp.sum(jnp.exp(values - top), axis=1, keepdims=True)
    stats_ref[...] = jnp.concatenate([top, total], axis=1)
    lines = jnp.concatenate([turn(top), turn(total)], axis=0)
    load.wait()
    lanes = t_stats.shape[1]
    if lanes > lines.shape[1]:
        lines = jnp.concatenate([lines, jnp.zeros((2, lanes - lines.shape[1]), F32)], axis=1)
    message = jnp.concatenate([lines, t_stats[...], jnp.zeros((4, lanes), F32)], axis=0)
    for k in range(message_ref.shape[0]):
        message_ref[k] = message
    keep.wait()
    for index, here in chunks:
        send(here, index).wait()


def student_logits(own, other, t_stats, weight, count):
    rows, width = weight.shape
    n_v, n_pl, group, _ = own.shape
    tokens = 2 * n_pl * group
    anywhere = pl.BlockSpec(memory_space=pl.ANY)
    return pl.pallas_call(
        logits_kernel,
        in_specs=[*in_vmem(2), anywhere, anywhere],
        out_specs=[*in_vmem(1), anywhere, anywhere, *in_vmem(1)],
        out_shape=[
            jax.ShapeDtypeStruct((tokens, 2), F32),
            pltpu.HBM((tokens, rows), F32),
            pltpu.HBM((tokens, width), BF16),
            pltpu.HBM((count, 8, t_stats.shape[1]), F32),
        ],
        scratch_shapes=[
            pltpu.VMEM((tokens, rows), F32),
            pltpu.VMEM((tokens, width), BF16),
            pltpu.VMEM((rows, width), BF16),
            pltpu.VMEM((2, *own.shape), F32),
            pltpu.VMEM(t_stats.shape, F32),
            pltpu.SemaphoreType.DMA((rows // LOGIT_TILE + 2,)),
            pltpu.SemaphoreType.DMA((rows // LOGIT_TILE + 2,)),
            pltpu.SemaphoreType.DMA((2,)),
        ],
        compiler_params=params(46 * MIB),
        cost_estimate=pl.CostEstimate(
            flops=8 * rows * width * tokens, bytes_accessed=2 * rows * width, transcendentals=0
        ),
    )(own, other, pltpu.with_memory_space_constraint(t_stats, pltpu.HBM), weight)


def copies_kernel(h_ref, out_ref, buffer, sem, sems):
    load = pltpu.make_async_copy(h_ref, buffer, sem)
    load.start()
    load.wait()
    sends = [
        pltpu.make_async_copy(buffer, out_ref.at[k], sems.at[k]) for k in range(out_ref.shape[0])
    ]
    for send in sends:
        send.start()
    for send in sends:
        send.wait()


def copies(hidden, count):
    anywhere = pl.BlockSpec(memory_space=pl.ANY)
    return pl.pallas_call(
        copies_kernel,
        in_specs=[anywhere],
        out_specs=anywhere,
        out_shape=pltpu.HBM((count, *hidden.shape), BF16),
        scratch_shapes=[
            pltpu.VMEM(hidden.shape, BF16),
            pltpu.SemaphoreType.DMA,
            pltpu.SemaphoreType.DMA((count,)),
        ],
        compiler_params=params(4 * MIB),
    )(pltpu.with_memory_space_constraint(hidden, pltpu.HBM))


def split_kernel(t_ref, out_ref, stats_ref, buffer, sem):
    load = pltpu.make_async_copy(t_ref, buffer, sem)
    load.start()
    load.wait()
    total, (count, _, cols) = buffer.shape[1], out_ref.shape
    for s in range(2):
        for d in range(count // 2):
            start = (s * (count // 2) + d) * cols
            low = start // LANES * LANES
            high = min(-(-(start + cols) // LANES) * LANES, total)
            values = buffer[:, low:high].astype(F32)
            out_ref[d * 2 + s] = values[:, start - low : start - low + cols].astype(BF16)
    values = buffer[...].astype(F32)
    half, lanes = values.shape[0], stats_ref.shape[1]
    top = jnp.max(values, axis=1, keepdims=True)
    total = jnp.sum(jnp.exp(values - top), axis=1, keepdims=True)
    group = lax.axis_index("pl") * 2 + lax.axis_index("co")
    first = (group * 2 + lax.axis_index("vs")) * half
    row = lax.broadcasted_iota(jnp.int32, (half, lanes), 0)
    lane = lax.broadcasted_iota(jnp.int32, (half, lanes), 1)
    chosen = lane == first + row
    tops = jnp.max(jnp.where(chosen, top, LOWEST), axis=0, keepdims=True)
    totals = jnp.sum(jnp.where(chosen, total, 0.0), axis=0, keepdims=True)
    stats_ref[...] = jnp.concatenate([tops, totals], axis=0)


def split_teacher(piece, n_dp):
    half, total = piece.shape
    return pl.pallas_call(
        split_kernel,
        in_specs=[pl.BlockSpec(memory_space=pl.ANY)],
        out_specs=in_vmem(2),
        out_shape=[
            pltpu.HBM((2 * n_dp, half, total // (2 * n_dp)), BF16),
            pltpu.HBM((2, -(-2 * half * n_dp // LANES) * LANES), F32),
        ],
        scratch_shapes=[pltpu.VMEM(piece.shape, BF16), pltpu.SemaphoreType.DMA],
        compiler_params=params(8 * MIB),
    )(pltpu.with_memory_space_constraint(piece, pltpu.HBM))


def teacher_values(t_ref):
    return jnp.concatenate([t_ref[j].astype(F32) for j in range(t_ref.shape[0])], axis=0)


def products_kernel(t_ref, lt_in, stats_ref, w_ref, u_ref, t_stats_ref, both_ref, *refs):
    lt_ref, buffer, packed, both, sems, own_sems = refs
    load = pltpu.make_async_copy(lt_in, lt_ref, own_sems.at[0])
    keep = pltpu.make_async_copy(both, both_ref, own_sems.at[1])
    tokens = stats_ref.shape[0]
    load.start()

    def prepare():
        values = teacher_values(t_ref)
        top = jnp.max(values, axis=1, keepdims=True)
        weights = jnp.exp(values - top)
        total = jnp.sum(weights, axis=1, keepdims=True)
        t_stats_ref[...] = jnp.concatenate([top, total], axis=1)
        teach = weights * (1.0 / total)
        load.wait()
        share = jnp.exp(lt_ref[...] - stats_ref[:, 0:1]) * (1.0 / stats_ref[:, 1:2])
        both[...] = jnp.concatenate([share, teach], axis=0).T
        packed[:tokens, :] = (share - teach).astype(BF16)
        packed[tokens:, :] = teach.astype(BF16)
        keep.start()
        u_ref[...] = jnp.zeros_like(u_ref)

    def compute(here, index):
        width = u_ref.shape[1]
        block = column_tile(width, 512)
        for k in range(0, width, block):
            cols = slice(k, k + block)
            u_ref[:, cols] += jnp.dot(
                packed[:, here], buffer[here, cols], preferred_element_type=F32
            )

    stream(w_ref, buffer, sems, 512, PRODUCT_TILE, 2, compute, prepare)
    keep.wait()


def local_products(weight, teacher, lt, stats):
    rows, width = weight.shape
    tokens = lt.shape[0]
    anywhere = pl.BlockSpec(memory_space=pl.ANY)
    return pl.pallas_call(
        products_kernel,
        in_specs=[*in_vmem(1), anywhere, *in_vmem(1), anywhere],
        out_specs=[*in_vmem(2), anywhere],
        out_shape=[
            jax.ShapeDtypeStruct((2 * tokens, width), F32),
            jax.ShapeDtypeStruct((tokens, 2), F32),
            pltpu.HBM((rows, 2 * tokens), F32),
        ],
        scratch_shapes=[
            pltpu.VMEM((tokens, rows), F32),
            pltpu.VMEM((rows, width), BF16),
            pltpu.VMEM((2 * tokens, rows), BF16),
            pltpu.VMEM((rows, 2 * tokens), F32),
            pltpu.SemaphoreType.DMA((rows // PRODUCT_TILE + 2,)),
            pltpu.SemaphoreType.DMA((2,)),
        ],
        compiler_params=params(46 * MIB),
        cost_estimate=pl.CostEstimate(
            flops=8 * rows * width * tokens, bytes_accessed=2 * rows * width, transcendentals=0
        ),
    )(teacher, pltpu.with_memory_space_constraint(lt, pltpu.HBM), stats, weight)


def combine_kernel(all_ref, s_ref, t_ref, u_ref, hp_ref, mass_ref):
    tokens = s_ref.shape[0]

    def mass(k, mine_ref):
        top_all = all_ref[:, k, :tokens]
        top = jnp.max(top_all, axis=0, keepdims=True)
        total = jnp.sum(jnp.exp(top_all - top) * all_ref[:, k + 1, :tokens], axis=0, keepdims=True)
        return jnp.exp(mine_ref[:, 0:1] - turn_back(top)) * mine_ref[:, 1:2] / turn_back(total)

    student, teacher = mass(0, s_ref), mass(2, t_ref)
    mass_ref[...] = GRAD_SCALE * jnp.concatenate([turn(student), turn(teacher)], axis=1)
    scale_x = GRAD_SCALE * student
    scale_t = GRAD_SCALE * (student - teacher)
    width = hp_ref.shape[2]
    for v in range(hp_ref.shape[0]):
        cols = slice(v * width, (v + 1) * width)
        hp_ref[v] = (u_ref[:tokens, cols] * scale_x + u_ref[tokens:, cols] * scale_t).astype(BF16)


def combine(stats_all, s_stats, t_stats, products, n_v):
    tokens = s_stats.shape[0]
    width = products.shape[1] // n_v
    return pl.pallas_call(
        combine_kernel,
        in_specs=in_vmem(4),
        out_specs=in_vmem(2),
        out_shape=[
            pltpu.HBM((n_v, tokens, width), BF16),
            jax.ShapeDtypeStruct((1, 2 * tokens), F32),
        ],
        compiler_params=params(12 * MIB),
    )(stats_all, s_stats, t_stats, products)


def head_blocks(width):
    first = column_tile(width, 512)
    rest = column_tile(width - first, 1024)
    return [(0, first)] + [(k, rest) for k in range(first, width, rest)]


def head_kernel(tile, both_ref, mass_ref, hidden_ref, out_ref, both, hidden, result, sems, out_sems):
    rows = both_ref.shape[0]
    tokens, width = hidden_ref.shape
    steps = rows // tile
    load_hidden = pltpu.make_async_copy(hidden_ref, hidden, sems.at[steps])

    def load(step):
        here = tile_rows(step, tile, rows)
        return pltpu.make_async_copy(both_ref.at[here, :], both.at[here, :], sems.at[step])

    def store(step, block, start, size):
        here, cols = tile_rows(step, tile, rows), slice(start, start + size)
        return pltpu.make_async_copy(
            result.at[here, cols], out_ref.at[here, cols], out_sems.at[step, block]
        )

    load(0).start()
    load_hidden.start()
    for step in range(1, steps):
        load(step).start()
    load_hidden.wait()

    def body(step, carry):
        load(step).wait()
        here = tile_rows(step, tile, rows)
        scaled = both[here, :] * mass_ref[...]
        grad = (scaled[:, :tokens] - scaled[:, tokens:]).astype(BF16)
        for block, (start, size) in enumerate(head_blocks(width)):
            inner = column_tile(size, 256)
            for k in range(start, start + size, inner):
                result[here, k : k + inner] = jnp.dot(
                    grad, hidden[:, k : k + inner], preferred_element_type=F32
                ).astype(BF16)
            store(step, block, start, size).start()
        return carry

    lax.fori_loop(0, steps, body, 0)
    for step in range(steps):
        for block, (start, size) in enumerate(head_blocks(width)):
            store(step, block, start, size).wait()


def head_gradient(both, mass, hidden):
    rows = both.shape[0]
    tokens, width = hidden.shape
    tile = row_tile(rows, 1584)
    steps = rows // tile
    anywhere = pl.BlockSpec(memory_space=pl.ANY)
    in_hbm = lambda x: pltpu.with_memory_space_constraint(x, pltpu.HBM)
    return pl.pallas_call(
        functools.partial(head_kernel, tile),
        in_specs=[anywhere, *in_vmem(1), anywhere],
        out_specs=anywhere,
        out_shape=jax.ShapeDtypeStruct((rows, width), BF16),
        scratch_shapes=[
            pltpu.VMEM((rows, 2 * tokens), F32),
            pltpu.VMEM((tokens, width), BF16),
            pltpu.VMEM((rows, width), BF16),
            pltpu.SemaphoreType.DMA((steps + 1,)),
            pltpu.SemaphoreType.DMA((steps, len(head_blocks(width)))),
        ],
        compiler_params=params(46 * MIB),
        cost_estimate=pl.CostEstimate(
            flops=8 * rows * width * tokens, bytes_accessed=2 * rows * width, transcendentals=0
        ),
    )(in_hbm(both), mass, in_hbm(hidden))


def exchange(parts, axes):
    return lax.all_to_all(parts, axes, split_axis=0, concat_axis=0, tiled=True)


def shards(n_dp, n_v, hidden, head_weight, teacher_logits):
    everyone = ("vk", "vs", "pl", "co")
    n_pl = n_dp // 2
    count = n_dp * n_v
    group, width = hidden.shape
    weight = head_weight[0]
    square = (n_v, n_pl, group, width)

    own = exchange(copies(hidden, n_v * n_pl), ("vk", "vs", "pl"))
    sends, t_rows = split_teacher(teacher_logits[0], n_dp)
    sends, own = lax.optimization_barrier((sends, own))
    other = lax.ppermute(own, "co", [(0, 1), (1, 0)])
    teacher = exchange(sends, ("pl", "co", "vs"))

    s_stats, lt, every_row, message = student_logits(
        own.reshape(square), other.reshape(square), t_rows, weight, count
    )
    stats_all = exchange(message, everyone)
    products, t_stats, shares = local_products(weight, teacher, lt, s_stats)
    partial_value, mass = combine(stats_all, s_stats, t_stats, products, n_v)
    pieces = exchange(partial_value.reshape(count, group, width), everyone)
    head_grad = head_gradient(shares, mass, every_row)
    hidden_grad = jnp.sum(pieces.astype(F32), axis=0).astype(BF16)
    return hidden_grad, head_grad[None]


def solution(mesh):
    n_dp, n_v = mesh.shape["dp"], mesh.shape["vocab"]
    split = Mesh(mesh.devices.reshape(n_dp // 2, 2, n_v // 2, 2), ("pl", "co", "vk", "vs"))
    dp, vocab = ("pl", "co"), ("vk", "vs")
    return jax.shard_map(
        functools.partial(shards, n_dp, n_v),
        mesh=split,
        in_specs=(P(dp, vocab), P(vocab, dp, None), P(vocab, dp, None)),
        out_specs=(P(dp, vocab), P(vocab, dp, None)),
        check_vma=False,
    )
```

```python
import functools

import jax
import jax.numpy as jnp
from jax import lax
from jax.experimental import pallas as pl
from jax.experimental.pallas import tpu as pltpu
from jax.sharding import Mesh
from jax.sharding import PartitionSpec as P

GRAD_SCALE = 32.0
F32 = jnp.float32
BF16 = jnp.bfloat16
MIB = 2**20
LANES = 128
LOWEST = -1e30
LOGIT_TILE = 512
PRODUCT_TILE = 1024


def row_tile(rows, limit):
    best = rows
    for tile in range(16, limit + 1, 16):
        if rows % tile == 0:
            best = tile
    return best


def column_tile(width, limit):
    return max(c for c in range(LANES, limit + 1, LANES) if width % c == 0)


def tile_rows(step, tile, rows):
    if tile == rows:
        return slice(None)
    return pl.ds(pl.multiple_of(step * tile, tile), tile)


def params(limit):
    return pltpu.CompilerParams(vmem_limit_bytes=limit)


def whole(shape):
    return pl.BlockSpec(shape, lambda *_: (0,) * len(shape))


def in_vmem(count):
    return [pl.BlockSpec(memory_space=pltpu.VMEM)] * count


def stream(w_ref, buffer, sems, first, tile, ahead, compute, between, beside=None):
    rows = w_ref.shape[0]
    if rows < first + tile:
        first = 0
    steps = (rows - first) // tile
    begin, last = slice(0, first), slice(first + steps * tile, rows)
    rest = rows - last.start

    def copy(here, sem):
        return pltpu.make_async_copy(w_ref.at[here, :], buffer.at[here, :], sem)

    def place(step):
        return pl.ds(pl.multiple_of(first + step * tile, LANES), tile)

    ahead = min(ahead, steps)
    if first:
        copy(begin, sems.at[steps + 1]).start()
    for step in range(ahead):
        copy(place(step), sems.at[step]).start()
    if rest and ahead == steps:
        copy(last, sems.at[steps]).start()
    between()
    if first:
        copy(begin, sems.at[steps + 1]).wait()
        compute(begin, steps + 1)
        if beside is not None:
            beside()

    def body(step, carry):
        @pl.when(step + ahead < steps)
        def _():
            copy(place(step + ahead), sems.at[step + ahead]).start()

        if rest and ahead < steps:

            @pl.when(step + ahead == steps)
            def _():
                copy(last, sems.at[steps]).start()

        copy(place(step), sems.at[step]).wait()
        compute(place(step), step)
        return carry

    if steps:
        lax.fori_loop(0, steps, body, 0)
    if rest:
        copy(last, sems.at[steps]).wait()
        compute(last, steps)
    chunks = [(k, slice(first + k * tile, first + (k + 1) * tile)) for k in range(steps)]
    return chunks + [(steps, last)] * bool(rest) + [(steps + 1, begin)] * bool(first)


def turn(column):
    size = column.shape[0]
    row = lax.broadcasted_iota(jnp.int32, (size, size), 0)
    col = lax.broadcasted_iota(jnp.int32, (size, size), 1)
    return jnp.sum(jnp.where(row == col, column, 0.0), axis=0, keepdims=True)


def turn_back(line):
    size = line.shape[1]
    row = lax.broadcasted_iota(jnp.int32, (size, size), 0)
    col = lax.broadcasted_iota(jnp.int32, (size, size), 1)
    return jnp.sum(jnp.where(row == col, line, 0.0), axis=1, keepdims=True)


def logits_kernel(own_ref, other_ref, t_stats_ref, w_ref, *refs):
    stats_ref, lt_out, out_ref, message_ref, *scratch = refs
    lt_ref, hidden, buffer, staged, t_stats, sems, lt_sems, out_sems = scratch
    keep = pltpu.make_async_copy(hidden, out_ref, out_sems.at[0])
    load = pltpu.make_async_copy(t_stats_ref, t_stats, out_sems.at[1])
    load.start()

    def assemble():
        n_v, n_pl, _, chunk = own_ref.shape
        core = lax.axis_index("co")
        staged[core] = own_ref[...].astype(F32)
        staged[1 - core] = other_ref[...].astype(F32)
        for v in range(n_v):
            groups = [staged[c, v, p] for p in range(n_pl) for c in range(2)]
            block = jnp.concatenate(groups, axis=0)
            hidden[:, v * chunk : (v + 1) * chunk] = block.astype(BF16)
        keep.start()

    def send(here, index):
        return pltpu.make_async_copy(lt_ref.at[:, here], lt_out.at[:, here], lt_sems.at[index])

    def compute(here, index):
        lt_ref[:, here] = lax.dot_general(
            hidden[...], buffer[here, :], (((1,), (1,)), ((), ())), preferred_element_type=F32
        )
        send(here, index).start()

    chunks = stream(w_ref, buffer, sems, 256, LOGIT_TILE, 3, compute, assemble)
    values = lt_ref[...]
    top = jnp.max(values, axis=1, keepdims=True)
    total = jnp.sum(jnp.exp(values - top), axis=1, keepdims=True)
    stats_ref[...] = jnp.concatenate([top, total], axis=1)
    lines = jnp.concatenate([turn(top), turn(total)], axis=0)
    load.wait()
    lanes = t_stats.shape[1]
    if lanes > lines.shape[1]:
        lines = jnp.concatenate([lines, jnp.zeros((2, lanes - lines.shape[1]), F32)], axis=1)
    message = jnp.concatenate([lines, t_stats[...], jnp.zeros((4, lanes), F32)], axis=0)
    for k in range(message_ref.shape[0]):
        message_ref[k] = message
    keep.wait()
    for index, here in chunks:
        send(here, index).wait()


def student_logits(own, other, t_stats, weight, count):
    rows, width = weight.shape
    n_v, n_pl, group, _ = own.shape
    tokens = 2 * n_pl * group
    anywhere = pl.BlockSpec(memory_space=pl.ANY)
    return pl.pallas_call(
        logits_kernel,
        in_specs=[*in_vmem(2), anywhere, anywhere],
        out_specs=[*in_vmem(1), anywhere, anywhere, *in_vmem(1)],
        out_shape=[
            jax.ShapeDtypeStruct((tokens, 2), F32),
            pltpu.HBM((tokens, rows), F32),
            pltpu.HBM((tokens, width), BF16),
            pltpu.HBM((count, 8, t_stats.shape[1]), F32),
        ],
        scratch_shapes=[
            pltpu.VMEM((tokens, rows), F32),
            pltpu.VMEM((tokens, width), BF16),
            pltpu.VMEM((rows, width), BF16),
            pltpu.VMEM((2, *own.shape), F32),
            pltpu.VMEM(t_stats.shape, F32),
            pltpu.SemaphoreType.DMA((rows // LOGIT_TILE + 2,)),
            pltpu.SemaphoreType.DMA((rows // LOGIT_TILE + 2,)),
            pltpu.SemaphoreType.DMA((2,)),
        ],
        compiler_params=params(46 * MIB),
        cost_estimate=pl.CostEstimate(
            flops=8 * rows * width * tokens, bytes_accessed=2 * rows * width, transcendentals=0
        ),
    )(own, other, pltpu.with_memory_space_constraint(t_stats, pltpu.HBM), weight)


def copies_kernel(h_ref, out_ref, buffer, sem, sems):
    load = pltpu.make_async_copy(h_ref, buffer, sem)
    load.start()
    load.wait()
    sends = [
        pltpu.make_async_copy(buffer, out_ref.at[k], sems.at[k]) for k in range(out_ref.shape[0])
    ]
    for send in sends:
        send.start()
    for send in sends:
        send.wait()


def copies(hidden, count):
    anywhere = pl.BlockSpec(memory_space=pl.ANY)
    return pl.pallas_call(
        copies_kernel,
        in_specs=[anywhere],
        out_specs=anywhere,
        out_shape=pltpu.HBM((count, *hidden.shape), BF16),
        scratch_shapes=[
            pltpu.VMEM(hidden.shape, BF16),
            pltpu.SemaphoreType.DMA,
            pltpu.SemaphoreType.DMA((count,)),
        ],
        compiler_params=params(4 * MIB),
    )(pltpu.with_memory_space_constraint(hidden, pltpu.HBM))


def split_kernel(t_ref, out_ref, stats_ref, buffer, sem):
    load = pltpu.make_async_copy(t_ref, buffer, sem)
    load.start()
    load.wait()
    total, (count, _, cols) = buffer.shape[1], out_ref.shape
    for s in range(2):
        for d in range(count // 2):
            start = (s * (count // 2) + d) * cols
            low = start // LANES * LANES
            high = min(-(-(start + cols) // LANES) * LANES, total)
            values = buffer[:, low:high].astype(F32)
            out_ref[d * 2 + s] = values[:, start - low : start - low + cols].astype(BF16)
    values = buffer[...].astype(F32)
    half, lanes = values.shape[0], stats_ref.shape[1]
    top = jnp.max(values, axis=1, keepdims=True)
    total = jnp.sum(jnp.exp(values - top), axis=1, keepdims=True)
    group = lax.axis_index("pl") * 2 + lax.axis_index("co")
    first = (group * 2 + lax.axis_index("vs")) * half
    row = lax.broadcasted_iota(jnp.int32, (half, lanes), 0)
    lane = lax.broadcasted_iota(jnp.int32, (half, lanes), 1)
    chosen = lane == first + row
    tops = jnp.max(jnp.where(chosen, top, LOWEST), axis=0, keepdims=True)
    totals = jnp.sum(jnp.where(chosen, total, 0.0), axis=0, keepdims=True)
    stats_ref[...] = jnp.concatenate([tops, totals], axis=0)


def split_teacher(piece, n_dp):
    half, total = piece.shape
    return pl.pallas_call(
        split_kernel,
        in_specs=[pl.BlockSpec(memory_space=pl.ANY)],
        out_specs=in_vmem(2),
        out_shape=[
            pltpu.HBM((2 * n_dp, half, total // (2 * n_dp)), BF16),
            pltpu.HBM((2, -(-2 * half * n_dp // LANES) * LANES), F32),
        ],
        scratch_shapes=[pltpu.VMEM(piece.shape, BF16), pltpu.SemaphoreType.DMA],
        compiler_params=params(8 * MIB),
    )(pltpu.with_memory_space_constraint(piece, pltpu.HBM))


def teacher_values(t_ref):
    return jnp.concatenate([t_ref[j].astype(F32) for j in range(t_ref.shape[0])], axis=0)


def products_kernel(t_ref, lt_in, stats_ref, w_ref, u_ref, t_stats_ref, both_ref, *refs):
    lt_ref, buffer, packed, both, sems, own_sems = refs
    load = pltpu.make_async_copy(lt_in, lt_ref, own_sems.at[0])
    keep = pltpu.make_async_copy(both, both_ref, own_sems.at[1])
    tokens = stats_ref.shape[0]
    load.start()

    rows = w_ref.shape[0]
    early = 512 if rows >= 512 + PRODUCT_TILE else rows

    def shares_of(here):
        values = jnp.concatenate(
            [t_ref[j][:, here].astype(F32) for j in range(t_ref.shape[0])], axis=0
        )
        teach = jnp.exp(values - t_stats_ref[:, 0:1]) * (1.0 / t_stats_ref[:, 1:2])
        share = jnp.exp(lt_ref[:, here] - stats_ref[:, 0:1]) * (1.0 / stats_ref[:, 1:2])
        packed[:tokens, here] = (share - teach).astype(BF16)
        packed[tokens:, here] = teach.astype(BF16)
        both[here, :] = jnp.concatenate([share, teach], axis=0).T

    def prepare():
        values = teacher_values(t_ref)
        top = jnp.max(values, axis=1, keepdims=True)
        total = jnp.sum(jnp.exp(values - top), axis=1, keepdims=True)
        t_stats_ref[...] = jnp.concatenate([top, total], axis=1)
        load.wait()
        shares_of(slice(0, early))
        if early == rows:
            u_ref[...] = jnp.zeros_like(u_ref)
            keep.start()

    def prepare_rest():
        shares_of(slice(early, rows))
        keep.start()

    def compute(here, index):
        width = u_ref.shape[1]
        block = column_tile(width, 512)
        for k in range(0, width, block):
            cols = slice(k, k + block)
            value = jnp.dot(packed[:, here], buffer[here, cols], preferred_element_type=F32)
            if early < rows and isinstance(here, slice) and here.start == 0:
                u_ref[:, cols] = value
            else:
                u_ref[:, cols] += value

    stream(w_ref, buffer, sems, 512, PRODUCT_TILE, 2, compute, prepare, prepare_rest)
    keep.wait()


def local_products(weight, teacher, lt, stats):
    rows, width = weight.shape
    tokens = lt.shape[0]
    anywhere = pl.BlockSpec(memory_space=pl.ANY)
    return pl.pallas_call(
        products_kernel,
        in_specs=[*in_vmem(1), anywhere, *in_vmem(1), anywhere],
        out_specs=[*in_vmem(2), anywhere],
        out_shape=[
            jax.ShapeDtypeStruct((2 * tokens, width), F32),
            jax.ShapeDtypeStruct((tokens, 2), F32),
            pltpu.HBM((rows, 2 * tokens), F32),
        ],
        scratch_shapes=[
            pltpu.VMEM((tokens, rows), F32),
            pltpu.VMEM((rows, width), BF16),
            pltpu.VMEM((2 * tokens, rows), BF16),
            pltpu.VMEM((rows, 2 * tokens), F32),
            pltpu.SemaphoreType.DMA((rows // PRODUCT_TILE + 2,)),
            pltpu.SemaphoreType.DMA((2,)),
        ],
        compiler_params=params(46 * MIB),
        cost_estimate=pl.CostEstimate(
            flops=8 * rows * width * tokens, bytes_accessed=2 * rows * width, transcendentals=0
        ),
    )(teacher, pltpu.with_memory_space_constraint(lt, pltpu.HBM), stats, weight)


def combine_kernel(all_ref, s_ref, t_ref, u_ref, hp_ref, mass_ref):
    tokens = s_ref.shape[0]

    def mass(k, mine_ref):
        top_all = all_ref[:, k, :tokens]
        top = jnp.max(top_all, axis=0, keepdims=True)
        total = jnp.sum(jnp.exp(top_all - top) * all_ref[:, k + 1, :tokens], axis=0, keepdims=True)
        return jnp.exp(mine_ref[:, 0:1] - turn_back(top)) * mine_ref[:, 1:2] / turn_back(total)

    student, teacher = mass(0, s_ref), mass(2, t_ref)
    mass_ref[...] = GRAD_SCALE * jnp.concatenate([turn(student), turn(teacher)], axis=1)
    scale_x = GRAD_SCALE * student
    scale_t = GRAD_SCALE * (student - teacher)
    width = hp_ref.shape[2]
    for v in range(hp_ref.shape[0]):
        cols = slice(v * width, (v + 1) * width)
        hp_ref[v] = (u_ref[:tokens, cols] * scale_x + u_ref[tokens:, cols] * scale_t).astype(BF16)


def combine(stats_all, s_stats, t_stats, products, n_v):
    tokens = s_stats.shape[0]
    width = products.shape[1] // n_v
    return pl.pallas_call(
        combine_kernel,
        in_specs=in_vmem(4),
        out_specs=in_vmem(2),
        out_shape=[
            pltpu.HBM((n_v, tokens, width), BF16),
            jax.ShapeDtypeStruct((1, 2 * tokens), F32),
        ],
        compiler_params=params(12 * MIB),
    )(stats_all, s_stats, t_stats, products)


def head_blocks(width):
    first = column_tile(width, 512)
    rest = column_tile(width - first, 1024)
    return [(0, first)] + [(k, rest) for k in range(first, width, rest)]


def head_kernel(tile, both_ref, mass_ref, hidden_ref, out_ref, both, hidden, result, sems, out_sems):
    rows = both_ref.shape[0]
    tokens, width = hidden_ref.shape
    steps = rows // tile
    load_hidden = pltpu.make_async_copy(hidden_ref, hidden, sems.at[steps])

    def load(step):
        here = tile_rows(step, tile, rows)
        return pltpu.make_async_copy(both_ref.at[here, :], both.at[here, :], sems.at[step])

    def store(step, block, start, size):
        here, cols = tile_rows(step, tile, rows), slice(start, start + size)
        return pltpu.make_async_copy(
            result.at[here, cols], out_ref.at[here, cols], out_sems.at[step, block]
        )

    load(0).start()
    load_hidden.start()
    for step in range(1, steps):
        load(step).start()
    load_hidden.wait()

    def body(step, carry):
        load(step).wait()
        here = tile_rows(step, tile, rows)
        scaled = both[here, :] * mass_ref[...]
        grad = (scaled[:, :tokens] - scaled[:, tokens:]).astype(BF16)
        for block, (start, size) in enumerate(head_blocks(width)):
            inner = column_tile(size, 256)
            for k in range(start, start + size, inner):
                result[here, k : k + inner] = jnp.dot(
                    grad, hidden[:, k : k + inner], preferred_element_type=F32
                ).astype(BF16)
            store(step, block, start, size).start()
        return carry

    lax.fori_loop(0, steps, body, 0)
    for step in range(steps):
        for block, (start, size) in enumerate(head_blocks(width)):
            store(step, block, start, size).wait()


def head_gradient(both, mass, hidden):
    rows = both.shape[0]
    tokens, width = hidden.shape
    tile = row_tile(rows, 1584)
    steps = rows // tile
    anywhere = pl.BlockSpec(memory_space=pl.ANY)
    in_hbm = lambda x: pltpu.with_memory_space_constraint(x, pltpu.HBM)
    return pl.pallas_call(
        functools.partial(head_kernel, tile),
        in_specs=[anywhere, *in_vmem(1), anywhere],
        out_specs=anywhere,
        out_shape=jax.ShapeDtypeStruct((rows, width), BF16),
        scratch_shapes=[
            pltpu.VMEM((rows, 2 * tokens), F32),
            pltpu.VMEM((tokens, width), BF16),
            pltpu.VMEM((rows, width), BF16),
            pltpu.SemaphoreType.DMA((steps + 1,)),
            pltpu.SemaphoreType.DMA((steps, len(head_blocks(width)))),
        ],
        compiler_params=params(46 * MIB),
        cost_estimate=pl.CostEstimate(
            flops=8 * rows * width * tokens, bytes_accessed=2 * rows * width, transcendentals=0
        ),
    )(in_hbm(both), mass, in_hbm(hidden))


def exchange(parts, axes):
    return lax.all_to_all(parts, axes, split_axis=0, concat_axis=0, tiled=True)


def shards(n_dp, n_v, hidden, head_weight, teacher_logits):
    everyone = ("vk", "vs", "pl", "co")
    n_pl = n_dp // 2
    count = n_dp * n_v
    group, width = hidden.shape
    weight = head_weight[0]
    square = (n_v, n_pl, group, width)

    own = exchange(copies(hidden, n_v * n_pl), ("vk", "vs", "pl"))
    sends, t_rows = split_teacher(teacher_logits[0], n_dp)
    sends, own = lax.optimization_barrier((sends, own))
    other = lax.ppermute(own, "co", [(0, 1), (1, 0)])
    teacher = exchange(sends, ("pl", "co", "vs"))

    s_stats, lt, every_row, message = student_logits(
        own.reshape(square), other.reshape(square), t_rows, weight, count
    )
    stats_all = exchange(message, everyone)
    products, t_stats, shares = local_products(weight, teacher, lt, s_stats)
    partial_value, mass = combine(stats_all, s_stats, t_stats, products, n_v)
    pieces = exchange(partial_value.reshape(count, group, width), everyone)
    head_grad = head_gradient(shares, mass, every_row)
    hidden_grad = jnp.sum(pieces.astype(F32), axis=0).astype(BF16)
    return hidden_grad, head_grad[None]


def solution(mesh):
    n_dp, n_v = mesh.shape["dp"], mesh.shape["vocab"]
    split = Mesh(mesh.devices.reshape(n_dp // 2, 2, n_v // 2, 2), ("pl", "co", "vk", "vs"))
    dp, vocab = ("pl", "co"), ("vk", "vs")
    return jax.shard_map(
        functools.partial(shards, n_dp, n_v),
        mesh=split,
        in_specs=(P(dp, vocab), P(vocab, dp, None), P(vocab, dp, None)),
        out_specs=(P(dp, vocab), P(vocab, dp, None)),
        check_vma=False,
    )
```

```python
import functools

import jax
import jax.numpy as jnp
from jax import lax
from jax.experimental import pallas as pl
from jax.experimental.pallas import tpu as pltpu
from jax.sharding import Mesh
from jax.sharding import PartitionSpec as P

GRAD_SCALE = 32.0
F32 = jnp.float32
BF16 = jnp.bfloat16
MIB = 2**20
LANES = 128
LOWEST = -1e30
LOGIT_TILE = 512
PRODUCT_TILE = 1024


def row_tile(rows, limit):
    best = rows
    for tile in range(16, limit + 1, 16):
        if rows % tile == 0:
            best = tile
    return best


def column_tile(width, limit):
    return max(c for c in range(LANES, limit + 1, LANES) if width % c == 0)


def tile_rows(step, tile, rows):
    if tile == rows:
        return slice(None)
    return pl.ds(pl.multiple_of(step * tile, tile), tile)


def params(limit):
    return pltpu.CompilerParams(vmem_limit_bytes=limit)


def whole(shape):
    return pl.BlockSpec(shape, lambda *_: (0,) * len(shape))


def in_vmem(count):
    return [pl.BlockSpec(memory_space=pltpu.VMEM)] * count


def stream(w_ref, buffer, sems, first, tile, ahead, compute, between, beside=None):
    rows = w_ref.shape[0]
    if rows < first + tile:
        first = 0
    steps = (rows - first) // tile
    begin, last = slice(0, first), slice(first + steps * tile, rows)
    rest = rows - last.start

    def copy(here, sem):
        return pltpu.make_async_copy(w_ref.at[here, :], buffer.at[here, :], sem)

    def place(step):
        return pl.ds(pl.multiple_of(first + step * tile, LANES), tile)

    ahead = min(ahead, steps)
    if first:
        copy(begin, sems.at[steps + 1]).start()
    for step in range(ahead):
        copy(place(step), sems.at[step]).start()
    if rest and ahead == steps:
        copy(last, sems.at[steps]).start()
    between()
    if first:
        copy(begin, sems.at[steps + 1]).wait()
        compute(begin, steps + 1)
        if beside is not None:
            beside()

    def body(step, carry):
        @pl.when(step + ahead < steps)
        def _():
            copy(place(step + ahead), sems.at[step + ahead]).start()

        if rest and ahead < steps:

            @pl.when(step + ahead == steps)
            def _():
                copy(last, sems.at[steps]).start()

        copy(place(step), sems.at[step]).wait()
        compute(place(step), step)
        return carry

    if steps:
        lax.fori_loop(0, steps, body, 0)
    if rest:
        copy(last, sems.at[steps]).wait()
        compute(last, steps)
    chunks = [(k, slice(first + k * tile, first + (k + 1) * tile)) for k in range(steps)]
    return chunks + [(steps, last)] * bool(rest) + [(steps + 1, begin)] * bool(first)


def turn(column):
    size = column.shape[0]
    row = lax.broadcasted_iota(jnp.int32, (size, size), 0)
    col = lax.broadcasted_iota(jnp.int32, (size, size), 1)
    return jnp.sum(jnp.where(row == col, column, 0.0), axis=0, keepdims=True)


def turn_back(line):
    size = line.shape[1]
    row = lax.broadcasted_iota(jnp.int32, (size, size), 0)
    col = lax.broadcasted_iota(jnp.int32, (size, size), 1)
    return jnp.sum(jnp.where(row == col, line, 0.0), axis=1, keepdims=True)


def logits_kernel(own_ref, other_ref, t_stats_ref, w_ref, *refs):
    stats_ref, lt_out, out_ref, message_out, *scratch = refs
    lt_ref, hidden, buffer, staged, t_stats, message_ref, sems, lt_sems, out_sems = scratch
    keep = pltpu.make_async_copy(hidden, out_ref, out_sems.at[0])
    load = pltpu.make_async_copy(t_stats_ref, t_stats, out_sems.at[1])
    load.start()

    def assemble():
        n_v, n_pl, _, chunk = own_ref.shape
        core = lax.axis_index("co")
        staged[core] = own_ref[...].astype(F32)
        staged[1 - core] = other_ref[...].astype(F32)
        for v in range(n_v):
            groups = [staged[c, v, p] for p in range(n_pl) for c in range(2)]
            block = jnp.concatenate(groups, axis=0)
            hidden[:, v * chunk : (v + 1) * chunk] = block.astype(BF16)
        keep.start()

    def send(here, index):
        return pltpu.make_async_copy(lt_ref.at[:, here], lt_out.at[:, here], lt_sems.at[index])

    def compute(here, index):
        lt_ref[:, here] = lax.dot_general(
            hidden[...], buffer[here, :], (((1,), (1,)), ((), ())), preferred_element_type=F32
        )
        send(here, index).start()

    chunks = stream(w_ref, buffer, sems, 256, LOGIT_TILE, 3, compute, assemble)
    values = lt_ref[...]
    top = jnp.max(values, axis=1, keepdims=True)
    total = jnp.sum(jnp.exp(values - top), axis=1, keepdims=True)
    stats_ref[...] = jnp.concatenate([top, total], axis=1)
    lines = jnp.concatenate([turn(top), turn(total)], axis=0)
    load.wait()
    lanes = t_stats.shape[1]
    if lanes > lines.shape[1]:
        lines = jnp.concatenate([lines, jnp.zeros((2, lanes - lines.shape[1]), F32)], axis=1)
    message = jnp.concatenate([lines, t_stats[...], jnp.zeros((4, lanes), F32)], axis=0)
    for k in range(message_ref.shape[0]):
        message_ref[k] = message
    send_message = pltpu.make_async_copy(message_ref, message_out, out_sems.at[2])
    send_message.start()
    keep.wait()
    for index, here in chunks:
        send(here, index).wait()
    send_message.wait()


def student_logits(own, other, t_stats, weight, count):
    rows, width = weight.shape
    n_v, n_pl, group, _ = own.shape
    tokens = 2 * n_pl * group
    anywhere = pl.BlockSpec(memory_space=pl.ANY)
    return pl.pallas_call(
        logits_kernel,
        in_specs=[*in_vmem(2), anywhere, anywhere],
        out_specs=[*in_vmem(1), anywhere, anywhere, anywhere],
        out_shape=[
            jax.ShapeDtypeStruct((tokens, 2), F32),
            pltpu.HBM((tokens, rows), F32),
            pltpu.HBM((tokens, width), BF16),
            pltpu.HBM((count, 8, t_stats.shape[1]), F32),
        ],
        scratch_shapes=[
            pltpu.VMEM((tokens, rows), F32),
            pltpu.VMEM((tokens, width), BF16),
            pltpu.VMEM((rows, width), BF16),
            pltpu.VMEM((2, *own.shape), F32),
            pltpu.VMEM(t_stats.shape, F32),
            pltpu.VMEM((count, 8, t_stats.shape[1]), F32),
            pltpu.SemaphoreType.DMA((rows // LOGIT_TILE + 2,)),
            pltpu.SemaphoreType.DMA((rows // LOGIT_TILE + 2,)),
            pltpu.SemaphoreType.DMA((3,)),
        ],
        compiler_params=params(46 * MIB),
        cost_estimate=pl.CostEstimate(
            flops=8 * rows * width * tokens, bytes_accessed=2 * rows * width, transcendentals=0
        ),
    )(own, other, pltpu.with_memory_space_constraint(t_stats, pltpu.HBM), weight)


def copies_kernel(h_ref, out_ref, buffer, sem, sems):
    load = pltpu.make_async_copy(h_ref, buffer, sem)
    load.start()
    load.wait()
    sends = [
        pltpu.make_async_copy(buffer, out_ref.at[k], sems.at[k]) for k in range(out_ref.shape[0])
    ]
    for send in sends:
        send.start()
    for send in sends:
        send.wait()


def copies(hidden, count):
    anywhere = pl.BlockSpec(memory_space=pl.ANY)
    return pl.pallas_call(
        copies_kernel,
        in_specs=[anywhere],
        out_specs=anywhere,
        out_shape=pltpu.HBM((count, *hidden.shape), BF16),
        scratch_shapes=[
            pltpu.VMEM(hidden.shape, BF16),
            pltpu.SemaphoreType.DMA,
            pltpu.SemaphoreType.DMA((count,)),
        ],
        compiler_params=params(4 * MIB),
    )(pltpu.with_memory_space_constraint(hidden, pltpu.HBM))


def split_kernel(t_ref, out_ref, stats_ref, buffer, sem):
    load = pltpu.make_async_copy(t_ref, buffer, sem)
    load.start()
    load.wait()
    total, (count, _, cols) = buffer.shape[1], out_ref.shape
    for s in range(2):
        for d in range(count // 2):
            start = (s * (count // 2) + d) * cols
            low = start // LANES * LANES
            high = min(-(-(start + cols) // LANES) * LANES, total)
            values = buffer[:, low:high].astype(F32)
            out_ref[d * 2 + s] = values[:, start - low : start - low + cols].astype(BF16)
    values = buffer[...].astype(F32)
    half, lanes = values.shape[0], stats_ref.shape[1]
    top = jnp.max(values, axis=1, keepdims=True)
    total = jnp.sum(jnp.exp(values - top), axis=1, keepdims=True)
    group = lax.axis_index("pl") * 2 + lax.axis_index("co")
    first = (group * 2 + lax.axis_index("vs")) * half
    row = lax.broadcasted_iota(jnp.int32, (half, lanes), 0)
    lane = lax.broadcasted_iota(jnp.int32, (half, lanes), 1)
    chosen = lane == first + row
    tops = jnp.max(jnp.where(chosen, top, LOWEST), axis=0, keepdims=True)
    totals = jnp.sum(jnp.where(chosen, total, 0.0), axis=0, keepdims=True)
    stats_ref[...] = jnp.concatenate([tops, totals], axis=0)


def split_teacher(piece, n_dp):
    half, total = piece.shape
    return pl.pallas_call(
        split_kernel,
        in_specs=[pl.BlockSpec(memory_space=pl.ANY)],
        out_specs=in_vmem(2),
        out_shape=[
            pltpu.HBM((2 * n_dp, half, total // (2 * n_dp)), BF16),
            pltpu.HBM((2, -(-2 * half * n_dp // LANES) * LANES), F32),
        ],
        scratch_shapes=[pltpu.VMEM(piece.shape, BF16), pltpu.SemaphoreType.DMA],
        compiler_params=params(8 * MIB),
    )(pltpu.with_memory_space_constraint(piece, pltpu.HBM))


def teacher_values(t_ref):
    return jnp.concatenate([t_ref[j].astype(F32) for j in range(t_ref.shape[0])], axis=0)


def products_kernel(t_ref, lt_in, stats_ref, w_ref, u_ref, t_stats_ref, both_ref, *refs):
    lt_ref, buffer, packed, both, sems, own_sems = refs
    load = pltpu.make_async_copy(lt_in, lt_ref, own_sems.at[0])
    keep = pltpu.make_async_copy(both, both_ref, own_sems.at[1])
    tokens = stats_ref.shape[0]
    load.start()

    rows = w_ref.shape[0]
    early = 512 if rows >= 512 + PRODUCT_TILE else rows

    def shares_of(here):
        values = jnp.concatenate(
            [t_ref[j][:, here].astype(F32) for j in range(t_ref.shape[0])], axis=0
        )
        teach = jnp.exp(values - t_stats_ref[:, 0:1]) * (1.0 / t_stats_ref[:, 1:2])
        share = jnp.exp(lt_ref[:, here] - stats_ref[:, 0:1]) * (1.0 / stats_ref[:, 1:2])
        packed[:tokens, here] = (share - teach).astype(BF16)
        packed[tokens:, here] = teach.astype(BF16)
        both[here, :] = jnp.concatenate([share, teach], axis=0).T

    def prepare():
        values = teacher_values(t_ref)
        top = jnp.max(values, axis=1, keepdims=True)
        total = jnp.sum(jnp.exp(values - top), axis=1, keepdims=True)
        t_stats_ref[...] = jnp.concatenate([top, total], axis=1)
        load.wait()
        shares_of(slice(0, early))
        if early == rows:
            u_ref[...] = jnp.zeros_like(u_ref)
            keep.start()

    def prepare_rest():
        shares_of(slice(early, rows))
        keep.start()

    def compute(here, index):
        width = u_ref.shape[1]
        block = column_tile(width, 512)
        for k in range(0, width, block):
            cols = slice(k, k + block)
            value = jnp.dot(packed[:, here], buffer[here, cols], preferred_element_type=F32)
            if early < rows and isinstance(here, slice) and here.start == 0:
                u_ref[:, cols] = value
            else:
                u_ref[:, cols] += value

    stream(w_ref, buffer, sems, 512, PRODUCT_TILE, 2, compute, prepare, prepare_rest)
    keep.wait()


def local_products(weight, teacher, lt, stats):
    rows, width = weight.shape
    tokens = lt.shape[0]
    anywhere = pl.BlockSpec(memory_space=pl.ANY)
    return pl.pallas_call(
        products_kernel,
        in_specs=[*in_vmem(1), anywhere, *in_vmem(1), anywhere],
        out_specs=[*in_vmem(2), anywhere],
        out_shape=[
            jax.ShapeDtypeStruct((2 * tokens, width), F32),
            jax.ShapeDtypeStruct((tokens, 2), F32),
            pltpu.HBM((rows, 2 * tokens), F32),
        ],
        scratch_shapes=[
            pltpu.VMEM((tokens, rows), F32),
            pltpu.VMEM((rows, width), BF16),
            pltpu.VMEM((2 * tokens, rows), BF16),
            pltpu.VMEM((rows, 2 * tokens), F32),
            pltpu.SemaphoreType.DMA((rows // PRODUCT_TILE + 2,)),
            pltpu.SemaphoreType.DMA((2,)),
        ],
        compiler_params=params(46 * MIB),
        cost_estimate=pl.CostEstimate(
            flops=8 * rows * width * tokens, bytes_accessed=2 * rows * width, transcendentals=0
        ),
    )(teacher, pltpu.with_memory_space_constraint(lt, pltpu.HBM), stats, weight)


def combine_kernel(all_ref, s_ref, t_ref, u_ref, hp_out, mass_ref, hp_ref, sems):
    tokens = s_ref.shape[0]

    def mass(k, mine_ref):
        top_all = all_ref[:, k, :tokens]
        top = jnp.max(top_all, axis=0, keepdims=True)
        total = jnp.sum(jnp.exp(top_all - top) * all_ref[:, k + 1, :tokens], axis=0, keepdims=True)
        return jnp.exp(mine_ref[:, 0:1] - turn_back(top)) * mine_ref[:, 1:2] / turn_back(total)

    student, teacher = mass(0, s_ref), mass(2, t_ref)
    mass_ref[...] = GRAD_SCALE * jnp.concatenate([turn(student), turn(teacher)], axis=1)
    scale_x = GRAD_SCALE * student
    scale_t = GRAD_SCALE * (student - teacher)
    width = hp_ref.shape[2]
    sends = []
    for v in range(hp_ref.shape[0]):
        cols = slice(v * width, (v + 1) * width)
        hp_ref[v] = (u_ref[:tokens, cols] * scale_x + u_ref[tokens:, cols] * scale_t).astype(BF16)
        sends.append(pltpu.make_async_copy(hp_ref.at[v], hp_out.at[v], sems.at[v]))
        sends[-1].start()
    for send in sends:
        send.wait()


def combine(stats_all, s_stats, t_stats, products, n_v):
    tokens = s_stats.shape[0]
    width = products.shape[1] // n_v
    return pl.pallas_call(
        combine_kernel,
        in_specs=in_vmem(4),
        out_specs=[pl.BlockSpec(memory_space=pl.ANY), *in_vmem(1)],
        out_shape=[
            pltpu.HBM((n_v, tokens, width), BF16),
            jax.ShapeDtypeStruct((1, 2 * tokens), F32),
        ],
        scratch_shapes=[
            pltpu.VMEM((n_v, tokens, width), BF16),
            pltpu.SemaphoreType.DMA((n_v,)),
        ],
        compiler_params=params(12 * MIB),
    )(stats_all, s_stats, t_stats, products)


def head_blocks(width):
    first = column_tile(width, 512)
    rest = column_tile(width - first, 1024)
    return [(0, first)] + [(k, rest) for k in range(first, width, rest)]


def head_kernel(tile, both_ref, mass_ref, hidden_ref, out_ref, both, hidden, result, sems, out_sems):
    rows = both_ref.shape[0]
    tokens, width = hidden_ref.shape
    steps = rows // tile
    load_hidden = pltpu.make_async_copy(hidden_ref, hidden, sems.at[steps])

    def load(step):
        here = tile_rows(step, tile, rows)
        return pltpu.make_async_copy(both_ref.at[here, :], both.at[here, :], sems.at[step])

    def store(step, block, start, size):
        here, cols = tile_rows(step, tile, rows), slice(start, start + size)
        return pltpu.make_async_copy(
            result.at[here, cols], out_ref.at[here, cols], out_sems.at[step, block]
        )

    load(0).start()
    load_hidden.start()
    for step in range(1, steps):
        load(step).start()
    load_hidden.wait()

    def body(step, carry):
        load(step).wait()
        here = tile_rows(step, tile, rows)
        scaled = both[here, :] * mass_ref[...]
        grad = (scaled[:, :tokens] - scaled[:, tokens:]).astype(BF16)
        for block, (start, size) in enumerate(head_blocks(width)):
            inner = column_tile(size, 256)
            for k in range(start, start + size, inner):
                result[here, k : k + inner] = jnp.dot(
                    grad, hidden[:, k : k + inner], preferred_element_type=F32
                ).astype(BF16)
            store(step, block, start, size).start()
        return carry

    lax.fori_loop(0, steps, body, 0)
    for step in range(steps):
        for block, (start, size) in enumerate(head_blocks(width)):
            store(step, block, start, size).wait()


def head_gradient(both, mass, hidden):
    rows = both.shape[0]
    tokens, width = hidden.shape
    tile = row_tile(rows, 1584)
    steps = rows // tile
    anywhere = pl.BlockSpec(memory_space=pl.ANY)
    in_hbm = lambda x: pltpu.with_memory_space_constraint(x, pltpu.HBM)
    return pl.pallas_call(
        functools.partial(head_kernel, tile),
        in_specs=[anywhere, *in_vmem(1), anywhere],
        out_specs=anywhere,
        out_shape=jax.ShapeDtypeStruct((rows, width), BF16),
        scratch_shapes=[
            pltpu.VMEM((rows, 2 * tokens), F32),
            pltpu.VMEM((tokens, width), BF16),
            pltpu.VMEM((rows, width), BF16),
            pltpu.SemaphoreType.DMA((steps + 1,)),
            pltpu.SemaphoreType.DMA((steps, len(head_blocks(width)))),
        ],
        compiler_params=params(46 * MIB),
        cost_estimate=pl.CostEstimate(
            flops=8 * rows * width * tokens, bytes_accessed=2 * rows * width, transcendentals=0
        ),
    )(in_hbm(both), mass, in_hbm(hidden))


def exchange(parts, axes):
    return lax.all_to_all(parts, axes, split_axis=0, concat_axis=0, tiled=True)


def shards(n_dp, n_v, hidden, head_weight, teacher_logits):
    everyone = ("vk", "vs", "pl", "co")
    n_pl = n_dp // 2
    count = n_dp * n_v
    group, width = hidden.shape
    weight = head_weight[0]
    square = (n_v, n_pl, group, width)

    own = exchange(copies(hidden, n_v * n_pl), ("vk", "vs", "pl"))
    sends, t_rows = split_teacher(teacher_logits[0], n_dp)
    sends, own = lax.optimization_barrier((sends, own))
    other = lax.ppermute(own, "co", [(0, 1), (1, 0)])
    teacher = exchange(sends, ("pl", "co", "vs"))

    s_stats, lt, every_row, message = student_logits(
        own.reshape(square), other.reshape(square), t_rows, weight, count
    )
    stats_all = exchange(message, everyone)
    products, t_stats, shares = local_products(weight, teacher, lt, s_stats)
    partial_value, mass = combine(stats_all, s_stats, t_stats, products, n_v)
    pieces = exchange(partial_value.reshape(count, group, width), everyone)
    head_grad = head_gradient(shares, mass, every_row)
    hidden_grad = jnp.sum(pieces.astype(F32), axis=0).astype(BF16)
    return hidden_grad, head_grad[None]


def solution(mesh):
    n_dp, n_v = mesh.shape["dp"], mesh.shape["vocab"]
    split = Mesh(mesh.devices.reshape(n_dp // 2, 2, n_v // 2, 2), ("pl", "co", "vk", "vs"))
    dp, vocab = ("pl", "co"), ("vk", "vs")
    return jax.shard_map(
        functools.partial(shards, n_dp, n_v),
        mesh=split,
        in_specs=(P(dp, vocab), P(vocab, dp, None), P(vocab, dp, None)),
        out_specs=(P(dp, vocab), P(vocab, dp, None)),
        check_vma=False,
    )
```
